32 devices in a mesh: wide: 8 (over z, y), narrow: 4 (over x, core).
Axes of the slice: x: 2, y: 2, z: 4, core: 2. Of those that a mesh axis runs over, the one named last changes fastest.
Arguments:
- tokens: bfloat16 [4096, 2048], P('wide', 'narrow'), may hold values from -6 to 6
- cotangent: bfloat16 [4096, 2048], P('wide', 'narrow'), may hold values from -6 to 6
- ln_gain: bfloat16 [2048], P(('narrow', 'wide')), may hold values from 0.5 to 1.5
- ln_shift: bfloat16 [2048], P(('narrow', 'wide')), may hold values from -1.75 to 1.75
- w_query: bfloat16 [2048, 2048], P('wide', 'narrow'), may hold values from -0.125 to 0.125
- b_query: bfloat16 [2048], P(('narrow', 'wide')), may hold values from -1.75 to 1.75
- w_key: bfloat16 [2048, 2048], P('wide', 'narrow'), may hold values from -0.125 to 0.125
- b_key: bfloat16 [2048], P(('narrow', 'wide')), may hold values from -1.75 to 1.75
- w_value: bfloat16 [2048, 2048], P('wide', 'narrow'), may hold values from -0.125 to 0.125
- b_value: bfloat16 [2048], P(('narrow', 'wide')), may hold values from -1.75 to 1.75
- w_dense: bfloat16 [2048, 2048], P('narrow', 'wide'), may hold values from -4 to 4
- b_dense: bfloat16 [2048], P(('narrow', 'wide')), may hold values from -1.75 to 1.75
- w_fc1: bfloat16 [2048, 8192], P('wide', 'narrow'), may hold values from -0.125 to 0.125
- b_fc1: bfloat16 [8192], P(('narrow', 'wide')), may hold values from -1.75 to 1.75
- w_fc2: bfloat16 [8192, 2048], P('narrow', 'wide'), may hold values from -0.0625 to 0.0625
- b_fc2: bfloat16 [2048], P(('narrow', 'wide')), may hold values from -1.75 to 1.75
Outputs:
- output: bfloat16 [4096, 2048], P('wide', 'narrow')
- input_grad: float32 [4096, 2048], P('wide', 'narrow')
- grad_ln_gain: float32 [2048], P(('narrow', 'wide'))
- grad_ln_shift: float32 [2048], P(('narrow', 'wide'))
- grad_w_query: float32 [2048, 2048], P('wide', 'narrow')
- grad_b_query: float32 [2048], P(('narrow', 'wide'))
- grad_w_key: float32 [2048, 2048], P('wide', 'narrow')
- grad_b_key: float32 [2048], P(('narrow', 'wide'))
- grad_w_value: float32 [2048, 2048], P('wide', 'narrow')
- grad_b_value: float32 [2048], P(('narrow', 'wide'))
- grad_w_dense: float32 [2048, 2048], P('narrow', 'wide')
- grad_b_dense: float32 [2048], P(('narrow', 'wide'))
- grad_w_fc1: float32 [2048, 8192], P('wide', 'narrow')
- grad_b_fc1: float32 [8192], P(('narrow', 'wide'))
- grad_w_fc2: float32 [8192, 2048], P('narrow', 'wide')
- grad_b_fc2: float32 [2048], P(('narrow', 'wide'))
The draws below stay inside these ranges and needn't reach their ends.
All inputs are finite; a program needn't handle non-finite values.
Results may differ from the reference program's by a relative error of at most 0.015.
Values may be sent and summed in bfloat16 or wider, within the bound.
No kernel may reach another device: no remote copies, remote signals or barrier semaphores. Data moves between devices by JAX's collectives and lax.ppermute only.
A program may use at most 192 MiB of HBM per device.

```python
import math
import jax
import jax.numpy as jnp
from jax import lax

D = 2048
HEADS = 32
HEAD_DIM = 64
ROT = 32
FF = 8192
SEQ_LEN = 2048
TOKENS = 4096


def levels(rng, dims, shards, least, top_value):
    def one(position, parts):
        heights = jax.random.uniform(jax.random.fold_in(jax.random.fold_in(rng, 6), position), (parts,), jnp.float32, least / len(shards), top_value / len(shards))
        return jnp.repeat(jnp.exp(heights), dims[position] // parts).reshape((-1,) + (1,) * (len(dims) - position - 1))

    gain = one(*shards[0])
    for cut in shards[1:]:
        gain = gain * one(*cut)
    return gain


def normal_values(own_key, dims, width, reach, split=(), kind=jnp.bfloat16):
    factor_of = levels(own_key, dims, split, -0.22, 0.18) if split else 1.0
    drawn = jax.random.normal(own_key, dims, jnp.float32) * width * factor_of
    return jnp.minimum(jnp.maximum(drawn, -reach), reach).astype(kind)


def setup_inputs(seed: int = 0) -> dict:
    seeds = jax.random.split(jax.random.key(seed), 17)
    tokens = normal_values(seeds[0], (TOKENS, D), 1.0, 6.0, ((0, 8), (1, 4)))
    cotangent = normal_values(seeds[1], (TOKENS, D), 1.0, 6.0, ((0, 8), (1, 4)))
    ln_gain = jnp.clip(1.0 + 0.1 * jax.random.normal(seeds[2], (D,), jnp.float32), 0.5, 1.5).astype(jnp.bfloat16)
    ln_shift = normal_values(seeds[3], (D,), 0.3, 1.75, ((0, 32),))
    w_query = normal_values(seeds[4], (D, D), D ** -0.5, 0.125, ((0, 8), (1, 4)))
    b_query = normal_values(seeds[5], (D,), 0.3, 1.75, ((0, 32),))
    w_key = normal_values(seeds[6], (D, D), D ** -0.5, 0.125, ((0, 8), (1, 4)))
    b_key = normal_values(seeds[7], (D,), 0.3, 1.75, ((0, 32),))
    w_value = normal_values(seeds[8], (D, D), D ** -0.5, 0.125, ((0, 8), (1, 4)))
    b_value = normal_values(seeds[9], (D,), 0.3, 1.75, ((0, 32),))
    w_dense = normal_values(seeds[10], (D, D), 2 ** -0.5, 4.0, ((0, 4), (1, 8)))
    b_dense = normal_values(seeds[11], (D,), 0.3, 1.75, ((0, 32),))
    w_fc1 = normal_values(seeds[12], (D, FF), D ** -0.5, 0.125, ((0, 8), (1, 4)))
    b_fc1 = normal_values(seeds[13], (FF,), 0.3, 1.75, ((0, 32),))
    w_fc2 = normal_values(seeds[14], (FF, D), FF ** -0.5, 0.0625, ((0, 4), (1, 8)))
    b_fc2 = normal_values(seeds[15], (D,), 0.3, 1.75, ((0, 32),))
    return dict(tokens=tokens, cotangent=cotangent, ln_gain=ln_gain, ln_shift=ln_shift, w_query=w_query, b_query=b_query, w_key=w_key, b_key=b_key, w_value=w_value, b_value=b_value, w_dense=w_dense, b_dense=b_dense, w_fc1=w_fc1, b_fc1=b_fc1, w_fc2=w_fc2, b_fc2=b_fc2)


@jax.custom_vjp
def low(v):
    return lax.optimization_barrier(v.astype(jnp.bfloat16)).astype(jnp.float32)

@jax.custom_vjp
def low_back(v):
    return v

def low_keep(v):
    return (low(v), None)

def low_pass(kept, grad):
    return (grad,)

def back_keep(v):
    return (v, None)

def back_low(kept, grad):
    return (low(grad),)
low.defvjp(low_keep, low_pass)
low_back.defvjp(back_keep, back_low)
epsilon = 1e-05

def product(left_side, right_side):
    return jnp.dot(left_side, right_side, precision=lax.Precision.HIGHEST)

def rotary_tables(places):
    halves = jnp.arange(ROT // 2).astype(jnp.float32)
    inverse = jnp.exp(halves * (-2.0 * math.log(10000.0) / ROT))
    phases = places[:, None] * inverse[None, :]
    phases = jnp.concatenate([phases, phases], axis=-1)
    return (jnp.cos(phases)[:, None, :], jnp.sin(phases)[:, None, :])

def rotate(values, cosine, sine_table):
    leading = values[..., :ROT]
    middle = ROT // 2
    turned = jnp.concatenate([-leading[..., middle:], leading[..., :middle]], axis=-1)
    return jnp.concatenate([leading * cosine + turned * sine_table, values[..., ROT:]], axis=-1)

def head_attention(head_parts):
    query_head, key_head, value_head = head_parts
    scores = low_back(product(query_head, key_head.T))
    places = jnp.arange(SEQ_LEN)
    allowed = places[:, None] >= places[None, :]
    scores = jnp.where(allowed, scores, -1e+30)
    row_max = lax.optimization_barrier(jnp.max(scores, axis=1, keepdims=True))
    weights = jnp.exp(scores - row_max)
    probabilities = low(weights / lax.optimization_barrier(jnp.sum(weights, axis=1, keepdims=True)))
    return product(probabilities, value_head)

def forward(inputs, ln_gain, ln_shift, w_query, b_query, w_key, b_key, w_value, b_value, w_dense, b_dense, w_fc1, b_fc1, w_fc2, b_fc2):
    row_mean = lax.optimization_barrier(jnp.mean(inputs, axis=-1, keepdims=True))
    spread = lax.optimization_barrier(jnp.mean(inputs * inputs, axis=-1, keepdims=True)) - row_mean * row_mean
    standard = (inputs - row_mean) * lax.rsqrt(spread + epsilon)
    normed = low(standard * ln_gain + ln_shift)
    cosine, sine_table = rotary_tables(jnp.arange(SEQ_LEN).astype(jnp.float32))
    head_shape = (SEQ_LEN, HEADS, HEAD_DIM)
    factor = 1.0 / math.sqrt(HEAD_DIM)
    queries = low_back(product(normed, w_query) + b_query).reshape(head_shape)
    queries = low(rotate(queries, cosine, sine_table) * factor)
    keys_all = low_back(product(normed, w_key) + b_key).reshape(head_shape)
    keys_all = low(rotate(keys_all, cosine, sine_table))
    values_all = low(low_back(product(normed, w_value) + b_value)).reshape(head_shape)
    heads_out = lax.map(jax.checkpoint(head_attention), (queries.transpose(1, 0, 2), keys_all.transpose(1, 0, 2), values_all.transpose(1, 0, 2)))
    attended = low(low_back(heads_out.transpose(1, 0, 2).reshape(SEQ_LEN, D)))
    up_input = low_back(product(normed, w_fc1) + b_fc1)
    up_output = low(jax.nn.gelu(up_input, approximate=True))
    return inputs + product(attended, w_dense) + b_dense + product(up_output, w_fc2) + b_fc2

def reference(tokens, cotangent, ln_gain, ln_shift, w_query, b_query, w_key, b_key, w_value, b_value, w_dense, b_dense, w_fc1, b_fc1, w_fc2, b_fc2):
    floats = tuple((item.astype(jnp.float32) for item in (ln_gain, ln_shift, w_query, b_query, w_key, b_key, w_value, b_value, w_dense, b_dense, w_fc1, b_fc1, w_fc2, b_fc2)))
    seq_inputs = tokens.astype(jnp.float32).reshape(-1, SEQ_LEN, D)
    seq_grads = cotangent.astype(jnp.float32).reshape(-1, SEQ_LEN, D)

    def per_sequence(totals, sequence_pair):
        inputs, grad_rows = sequence_pair
        result, pull = jax.vjp(forward, inputs, *floats)
        gradients = pull(grad_rows)
        totals = tuple((first + second for first, second in zip(totals, gradients[1:])))
        return (totals, (result.astype(jnp.bfloat16), gradients[0]))
    initial = tuple((jnp.zeros_like(item) for item in floats))
    totals, (outputs, input_grads) = lax.scan(per_sequence, initial, (seq_inputs, seq_grads))
    return (outputs.reshape(TOKENS, D), input_grads.reshape(TOKENS, D), totals[0], totals[1], totals[2], totals[3], totals[4], totals[5], totals[6], totals[7], totals[8], totals[9], totals[10], totals[11], totals[12], totals[13])
```

```python
from functools import partial
import math

import jax
import jax.numpy as jnp
import numpy as np
from jax import lax
from jax.experimental import pallas as pl
from jax.experimental.pallas import tpu as pltpu
from jax.sharding import Mesh, PartitionSpec as P

D = 2048
HEAD_DIM = 64
ROT = 32
SEQ_LEN = 2048
EPSILON = 1e-05
BLOCK = 256

WIDE = ("s", "g", "h")
LINE = ("s", "g")
CUBE = ("g", "h", "m", "c")


def matmul(left_side, right_side):
    return jnp.dot(left_side, right_side, preferred_element_type=jnp.float32)


def contract_rows(left_side, right_side):
    return lax.dot_general(
        left_side, right_side, (((0,), (0,)), ((), ())), preferred_element_type=jnp.float32
    )


def contract_cols(left_side, right_side):
    return lax.dot_general(
        left_side, right_side, (((1,), (1,)), ((), ())), preferred_element_type=jnp.float32
    )


def pick(blocks, index, axis=0):
    return lax.dynamic_index_in_dim(blocks, index, axis, keepdims=False)


def shifted(value, axis, step):
    count = lax.axis_size(axis)
    return lax.ppermute(value, axis, [(source, (source + step) % count) for source in range(count)])


def rotary_tables(rows):
    lane = np.arange(2 * HEAD_DIM) % HEAD_DIM
    pair = (lane % (ROT // 2)).astype(np.float32)
    inverse = np.exp(pair * np.float32(-2.0 * math.log(10000.0) / ROT)).astype(np.float32)
    phase = np.arange(rows, dtype=np.float32)[:, None] * inverse[None, :]
    turned = (lane < ROT)[None, :]
    sign = np.where(lane < ROT // 2, -1.0, 1.0)[None, :]
    cosine = np.where(turned, np.cos(phase), 1.0).astype(np.float32)
    sine = np.where(turned, np.sin(phase) * sign, 0.0).astype(np.float32)
    return (cosine, sine)


def norm_kernel(rows, tokens_ref, gain_ref, shift_ref, normed_ref, stats_ref):
    parts = [tokens_ref[0, j].astype(jnp.float32) for j in range(tokens_ref.shape[1])]
    total = sum(jnp.sum(part, axis=1, keepdims=True) for part in parts)
    squares = sum(jnp.sum(part * part, axis=1, keepdims=True) for part in parts)
    mean = total / D
    inverse_std = lax.rsqrt(squares / D - mean * mean + EPSILON)
    width = parts[0].shape[1]
    for j, part in enumerate(parts):
        cols = slice(j * width, (j + 1) * width)
        standard = (part - mean) * inverse_std
        normed_ref[:, cols] = (standard * gain_ref[:, cols] + shift_ref[:, cols]).astype(
            jnp.bfloat16
        )
    stats_ref[...] = jnp.concatenate(
        [jnp.broadcast_to(mean, (rows, 64)), jnp.broadcast_to(inverse_std, (rows, 64))], axis=1
    )


def layer_norm(blocks, gain, shift, row_count):
    row_blocks, col_blocks, _, width = blocks.shape
    rows = 256
    per = row_count // rows
    total_rows = row_blocks * row_count
    return pl.pallas_call(
        partial(norm_kernel, rows),
        grid=(row_blocks * per,),
        in_specs=[
            pl.BlockSpec((1, col_blocks, rows, width), lambda i: (i // per, 0, i % per, 0)),
            pl.BlockSpec((1, D), lambda i: (0, 0)),
            pl.BlockSpec((1, D), lambda i: (0, 0)),
        ],
        out_specs=[
            pl.BlockSpec((rows, D), lambda i: (i, 0)),
            pl.BlockSpec((rows, 128), lambda i: (i, 0)),
        ],
        out_shape=[
            jax.ShapeDtypeStruct((total_rows, D), jnp.bfloat16),
            jax.ShapeDtypeStruct((total_rows, 128), jnp.float32),
        ],
        compiler_params=pltpu.CompilerParams(vmem_limit_bytes=48 * 2**20),
        name="layer_norm",
    )(blocks, gain, shift)


def turn(values, cosine, sine):
    lane = lax.broadcasted_iota(jnp.int32, values.shape, 1) % HEAD_DIM
    width = values.shape[1]
    half = ROT // 2
    partner = jnp.where(
        lane < half, pltpu.roll(values, width - half, 1), pltpu.roll(values, half, 1)
    )
    return values * cosine + partner * sine


def attention_kernel(
    blocks,
    pre_ref,
    grad_ref,
    cosine_ref,
    sine_ref,
    attended_ref,
    pre_grad_ref,
    q_ref,
    k_ref,
    v_ref,
    score_ref,
    slope_ref,
    k_total,
    v_total,
):
    i = pl.program_id(0)
    width = 2 * HEAD_DIM
    factor = 1.0 / math.sqrt(HEAD_DIM)

    @pl.when(i == 0)
    def _():
        def prepare(b, carry):
            rows = pl.ds(pl.multiple_of(b * BLOCK, BLOCK), BLOCK)
            cosine, sine = cosine_ref[rows, :], sine_ref[rows, :]
            pre = pre_ref[rows, :]
            q_ref[rows, :] = (turn(pre[:, :width], cosine, sine) * factor).astype(jnp.bfloat16)
            k_ref[rows, :] = turn(pre[:, width : 2 * width], cosine, sine).astype(jnp.bfloat16)
            v_ref[rows, :] = pre[:, 2 * width :].astype(jnp.bfloat16)
            return carry

        lax.fori_loop(0, blocks, prepare, 0)
        k_total[...] = jnp.zeros_like(k_total)
        v_total[...] = jnp.zeros_like(v_total)

    own = pl.ds(pl.multiple_of(i * BLOCK, BLOCK), BLOCK)
    causal = lax.broadcasted_iota(jnp.int32, (BLOCK, BLOCK), 0) >= lax.broadcasted_iota(
        jnp.int32, (BLOCK, BLOCK), 1
    )
    attended_parts, q_grad_parts = [], []
    for head in range(2):
        cols = slice(head * HEAD_DIM, (head + 1) * HEAD_DIM)
        queries = q_ref[own, cols]
        out_grad = grad_ref[own, cols]

        def lanes(block):
            return [block[:, n : n + 128] for n in range(0, BLOCK, 128)]

        def score(j, best, diagonal):
            rows = pl.ds(pl.multiple_of(j * BLOCK, BLOCK), BLOCK)
            block = contract_cols(queries, k_ref[rows, cols])
            if diagonal:
                block = jnp.where(causal, block, -1e30)
            score_ref[j] = block
            for part in lanes(block):
                best = jnp.maximum(best, part)
            return best

        best = lax.fori_loop(
            0, i, lambda j, b: score(j, b, False), jnp.full((BLOCK, 128), -1e30, jnp.float32)
        )
        row_max = jnp.max(score(i, best, True), axis=1, keepdims=True)

        def weigh(j, carry):
            total, dots = carry
            rows = pl.ds(pl.multiple_of(j * BLOCK, BLOCK), BLOCK)
            weights = jnp.exp(score_ref[j] - row_max)
            slope = contract_cols(out_grad, v_ref[rows, cols])
            score_ref[j] = weights
            slope_ref[j] = slope
            for part in lanes(weights):
                total = total + part
            for part in lanes(weights * slope):
                dots = dots + part
            return total, dots

        zero = jnp.zeros((BLOCK, 128), jnp.float32)
        total, dots = lax.fori_loop(0, i + 1, weigh, (zero, zero))
        scale = 1.0 / jnp.sum(total, axis=1, keepdims=True)
        row_dot = jnp.sum(dots, axis=1, keepdims=True) * scale

        def push(j, carry):
            out, q_grad = carry
            rows = pl.ds(pl.multiple_of(j * BLOCK, BLOCK), BLOCK)
            probs = score_ref[j] * scale
            low = probs.astype(jnp.bfloat16)
            score_grad = (probs * (slope_ref[j] - row_dot)).astype(jnp.bfloat16)
            out = out + matmul(low, v_ref[rows, cols])
            q_grad = q_grad + matmul(score_grad, k_ref[rows, cols])
            k_total[rows, cols] += contract_rows(score_grad, queries)
            v_total[rows, cols] += contract_rows(low, out_grad)
            return out, q_grad

        narrow_zero = jnp.zeros((BLOCK, HEAD_DIM), jnp.float32)
        out, q_grad = lax.fori_loop(0, i + 1, push, (narrow_zero, narrow_zero))
        attended_parts.append(out)
        q_grad_parts.append(q_grad)
    attended_ref[own, :] = jnp.concatenate(attended_parts, axis=1).astype(jnp.bfloat16)
    q_grad = jnp.concatenate(q_grad_parts, axis=1) * factor
    pre_grad_ref[own, :width] = turn(q_grad, cosine_ref[own, :], -sine_ref[own, :]).astype(
        jnp.bfloat16
    )

    @pl.when(i == blocks - 1)
    def _():
        def finish(b, carry):
            rows = pl.ds(pl.multiple_of(b * BLOCK, BLOCK), BLOCK)
            pre_grad_ref[rows, width : 2 * width] = turn(
                k_total[rows, :], cosine_ref[rows, :], -sine_ref[rows, :]
            ).astype(jnp.bfloat16)
            pre_grad_ref[rows, 2 * width :] = v_total[rows, :].astype(jnp.bfloat16)
            return carry

        lax.fori_loop(0, blocks, finish, 0)


def attention(pre, out_grad):
    rows, width = pre.shape[0], 2 * HEAD_DIM
    blocks = rows // BLOCK
    cosine, sine = rotary_tables(rows)
    whole = lambda shape: pl.BlockSpec(shape, lambda i: (0, 0))
    pairs = rows * (rows + BLOCK)
    return pl.pallas_call(
        partial(attention_kernel, blocks),
        grid=(blocks,),
        in_specs=[
            whole((rows, 3 * width)),
            whole((rows, width)),
            whole((rows, width)),
            whole((rows, width)),
        ],
        out_specs=[whole((rows, width)), whole((rows, 3 * width))],
        out_shape=[
            jax.ShapeDtypeStruct((rows, width), jnp.bfloat16),
            jax.ShapeDtypeStruct((rows, 3 * width), jnp.bfloat16),
        ],
        scratch_shapes=[
            pltpu.VMEM((rows, width), jnp.bfloat16),
            pltpu.VMEM((rows, width), jnp.bfloat16),
            pltpu.VMEM((rows, width), jnp.bfloat16),
            pltpu.VMEM((blocks, BLOCK, BLOCK), jnp.float32),
            pltpu.VMEM((blocks, BLOCK, BLOCK), jnp.float32),
            pltpu.VMEM((rows, width), jnp.float32),
            pltpu.VMEM((rows, width), jnp.float32),
        ],
        compiler_params=pltpu.CompilerParams(vmem_limit_bytes=48 * 2**20),
        cost_estimate=pl.CostEstimate(
            flops=6 * pairs * 256 * 2, bytes_accessed=rows * width * 16, transcendentals=pairs
        ),
        name="attention",
    )(pre, out_grad, jnp.asarray(cosine), jnp.asarray(sine))


def gather_columns(shard):
    rows = shard.shape[0]
    own_g, own_h = lax.axis_index("g"), lax.axis_index("h")
    split = shard.reshape(rows, 2, 2, -1)
    mine = pick(split, own_h, 2)
    other = shifted(pick(split, 1 - own_h, 2), "h", 1)
    pair = jnp.stack(
        [jnp.where(own_h == 0, mine, other), jnp.where(own_h == 0, other, mine)], axis=0
    )
    same, cross = pick(pair, own_g, 2), pick(pair, 1 - own_g, 2)
    same = same.reshape(2 * rows, -1)
    cross = cross.reshape(2 * rows, -1)
    count = lax.axis_size(LINE)
    place = lax.axis_index(LINE)
    full = jnp.zeros((count, 2 * rows, same.shape[1]), shard.dtype)
    full = lax.dynamic_update_index_in_dim(full, same, place, 0)
    for step in range(1, count):
        arrived = shifted(cross if step % 2 else same, LINE, step)
        full = lax.dynamic_update_index_in_dim(full, arrived, (place - step) % count, 0)
    return full.reshape(count * 2 * rows, -1)


def scatter_columns(grad):
    count = lax.axis_size(LINE)
    place = lax.axis_index(LINE)
    own_g, own_h = lax.axis_index("g"), lax.axis_index("h")
    cols = grad.shape[1]
    blocks = grad.reshape(count, 2, -1, cols)
    rows = blocks.shape[2]
    same = pick(blocks, place).astype(jnp.float32)
    cross = None
    for step in range(1, count):
        arrived = shifted(pick(blocks, (place + step) % count), LINE, step).astype(jnp.float32)
        if step % 2:
            cross = arrived if cross is None else cross + arrived
        else:
            same = same + arrived
    both = jnp.stack(
        [jnp.where(own_g == 0, same, cross), jnp.where(own_g == 0, cross, same)], axis=0
    )
    mine = pick(both, own_h, 1)
    other = shifted(pick(both, 1 - own_h, 1).astype(jnp.bfloat16), "h", 1).astype(jnp.float32)
    lower, upper = jnp.where(own_h == 0, mine, other), jnp.where(own_h == 0, other, mine)
    return jnp.concatenate([lower[0], upper[0], lower[1], upper[1]], axis=1)


def body(
    tokens,
    cotangent,
    ln_gain,
    ln_shift,
    w_query,
    b_query,
    w_key,
    b_key,
    w_value,
    b_value,
    w_dense,
    b_dense,
    w_fc1,
    b_fc1,
    w_fc2,
    b_fc2,
):
    row_count, feature_count = tokens.shape
    sequences = lax.axis_size("s")
    own_s, own_g, own_h = lax.axis_index("s"), lax.axis_index("g"), lax.axis_index("h")
    own_n = lax.axis_index(("m", "c"))
    wide = lax.axis_size(WIDE)
    weight_rows = w_fc1.shape[0]
    heads_width = w_query.shape[1] // 4
    hidden = w_fc1.shape[1] // 4

    vectors = (ln_gain, ln_shift, b_query, b_key, b_value, b_dense, b_fc2, b_fc1)
    lengths = [vector.shape[0] for vector in vectors]
    packed = jnp.concatenate(vectors)
    lanes = -(-packed.shape[0] // feature_count) * feature_count
    packed = jnp.pad(packed, (0, lanes - packed.shape[0]))
    by_sequence = jnp.zeros((sequences, lanes), packed.dtype)
    by_sequence = lax.dynamic_update_index_in_dim(by_sequence, packed, own_s, 0)
    for step in range(1, sequences):
        by_sequence = lax.dynamic_update_index_in_dim(
            by_sequence, shifted(packed, "s", step), (own_s - step) % sequences, 0
        )
    extra = by_sequence.reshape(-1, feature_count)
    extra_rows = -(-extra.shape[0] // 16) * 16
    extra = jnp.pad(extra, ((0, extra_rows - extra.shape[0]), (0, 0)))
    token_blocks = lax.all_gather(
        jnp.concatenate([tokens, extra], axis=0), CUBE, axis=0, tiled=False
    )
    cotangent_blocks = lax.all_gather(cotangent, CUBE, axis=0, tiled=False)

    up_weight = gather_columns(w_fc1)
    attention_shard = jnp.concatenate(
        [
            part.reshape(weight_rows, 4, heads_width)
            for part in (w_query, w_key, w_value, w_dense.T)
        ],
        axis=2,
    )
    attention_weight = gather_columns(attention_shard.reshape(weight_rows, -1))
    down_weight = gather_columns(w_fc2.T)
    qkv_weight = attention_weight[:, : 3 * heads_width]
    back_weight = jnp.concatenate([attention_weight[:, 3 * heads_width :], down_weight], axis=1)

    table = token_blocks[:, row_count : row_count + sequences * lanes // feature_count, :]
    table = table.reshape(2, 2, 4, sequences, lanes).transpose(2, 3, 0, 1, 4)
    table = table.reshape(4, wide, lanes).astype(jnp.float32)
    pieces, start = [], 0
    for length in lengths:
        pieces.append(table[:, :, start : start + length])
        start += length
    gain = pieces[0].reshape(1, -1)
    shift = pieces[1].reshape(1, -1)
    here = pick(jnp.concatenate(pieces[2:], axis=2), own_n)
    start = 0
    local = []
    for length in lengths[2:]:
        local.append(here[:, start : start + length].reshape(-1))
        start += length
    quarter = 2 * own_g + own_h
    qkv_bias = jnp.concatenate([pick(part.reshape(4, -1), quarter) for part in local[:3]])
    out_bias = local[3] + local[4]
    up_bias = pick(local[5].reshape(4, -1), quarter)

    normed, stats = layer_norm(
        token_blocks.reshape(4, 4, row_count + extra_rows, feature_count), gain, shift, row_count
    )
    cotangent_full = (
        cotangent_blocks.reshape(4, 4, row_count, feature_count)
        .transpose(0, 2, 1, 3)
        .reshape(4 * row_count, 4 * feature_count)
    )

    up_input = matmul(normed, up_weight) + up_bias
    up_output, gelu_pull = jax.vjp(partial(jax.nn.gelu, approximate=True), up_input)
    up_short = up_output.astype(jnp.bfloat16)

    qkv_pre = matmul(normed, qkv_weight) + qkv_bias
    back = matmul(cotangent_full, back_weight)
    attended_grad = back[:, :heads_width].astype(jnp.bfloat16)
    up_grad = gelu_pull(back[:, heads_width:])[0].astype(jnp.bfloat16)
    attended, qkv_grad = attention(qkv_pre, attended_grad)

    grad_down = contract_rows(cotangent_full, up_short).astype(jnp.bfloat16)
    grad_dense = contract_rows(cotangent_full, attended).astype(jnp.bfloat16)
    grad_up = contract_rows(normed, up_grad).astype(jnp.bfloat16)
    grad_qkv = contract_rows(normed, qkv_grad).astype(jnp.bfloat16)

    branch = contract_cols(jnp.concatenate([attended, up_short], axis=1), back_weight)
    normed_grad = contract_cols(
        jnp.concatenate([qkv_grad, up_grad], axis=1),
        jnp.concatenate([qkv_weight, up_weight], axis=1),
    )

    def summed_blocks(partial_sum):
        blocks = partial_sum.astype(jnp.bfloat16).reshape(4, row_count, 4, feature_count)
        blocks = blocks.transpose(0, 2, 1, 3).reshape(16, row_count, feature_count)
        return lax.psum_scatter(blocks, CUBE, scatter_dimension=0, tiled=False).astype(
            jnp.float32
        )

    local_x = tokens.astype(jnp.float32)
    output = (local_x + summed_blocks(branch) + out_bias).astype(jnp.bfloat16)

    grad_down_sum = scatter_columns(grad_down).T
    grad_up_sum = scatter_columns(grad_up)
    grad_attention = scatter_columns(jnp.concatenate([grad_qkv, grad_dense], axis=1))
    grad_attention = grad_attention.reshape(weight_rows, 4, 4, heads_width)
    grad_query, grad_key, grad_value, grad_dense_sum = (
        grad_attention[:, :, n].reshape(weight_rows, -1) for n in range(4)
    )

    standard_grad = summed_blocks(normed_grad)
    own_stats = pick(stats.reshape(4, row_count, 128), quarter)
    row_mean, inverse_std = own_stats[:, :1], own_stats[:, 64:65]
    standard = (local_x - row_mean) * inverse_std
    own_gain = pick(pieces[0].reshape(4, -1), own_n)
    scaled_grad = standard_grad * own_gain
    back_sums = lax.psum(
        (jnp.sum(scaled_grad, axis=1), jnp.sum(scaled_grad * standard, axis=1)), ("m", "c")
    )
    input_grad = (
        scaled_grad - back_sums[0][:, None] / D - standard * (back_sums[1][:, None] / D)
    ) * inverse_std + cotangent.astype(jnp.float32)

    def spread(vector):
        placed = jnp.zeros((4, vector.shape[0]), jnp.float32)
        placed = lax.dynamic_update_index_in_dim(placed, vector, quarter, 0)
        return placed.reshape(wide, -1)

    def column_sums(values):
        return jnp.sum(values.astype(jnp.float32), axis=0)

    qkv_sums = column_sums(qkv_grad)
    terms = [
        jnp.sum(standard_grad * standard, axis=0).reshape(wide, -1),
        jnp.sum(standard_grad, axis=0).reshape(wide, -1),
        spread(qkv_sums[:heads_width]),
        spread(qkv_sums[heads_width : 2 * heads_width]),
        spread(qkv_sums[2 * heads_width :]),
        column_sums(cotangent).reshape(wide, -1),
        spread(column_sums(up_grad)),
    ]
    vector_sums = lax.psum_scatter(
        jnp.concatenate(terms, axis=1), WIDE, scatter_dimension=0, tiled=False
    )
    vector_grads, start = [], 0
    for term in terms:
        vector_grads.append(vector_sums[start : start + term.shape[1]])
        start += term.shape[1]
    return (
        output,
        input_grad,
        vector_grads[0],
        vector_grads[1],
        grad_query,
        vector_grads[2],
        grad_key,
        vector_grads[3],
        grad_value,
        vector_grads[4],
        grad_dense_sum.T,
        vector_grads[5],
        grad_up_sum,
        vector_grads[6],
        grad_down_sum,
        vector_grads[5],
    )


def solution(mesh):
    wide = mesh.shape["wide"]
    inner = Mesh(mesh.devices.reshape(wide // 4, 2, 2, 2, 2), ("s", "g", "h", "m", "c"))
    narrow = ("m", "c")
    acts = P(WIDE, narrow)
    vector = P(narrow + WIDE)
    by_rows = P(WIDE, narrow)
    by_cols = P(narrow, WIDE)
    in_specs = (
        (acts, acts, vector, vector)
        + (by_rows, vector) * 3
        + (by_cols, vector, by_rows, vector, by_cols, vector)
    )
    out_specs = (
        (acts, acts, vector, vector)
        + (by_rows, vector) * 3
        + (by_cols, vector, by_rows, vector, by_cols, vector)
    )
    return jax.shard_map(body, mesh=inner, in_specs=in_specs, out_specs=out_specs, check_vma=False)
```

```python
from functools import partial
import math

import jax
import jax.numpy as jnp
import numpy as np
from jax import lax
from jax.experimental import pallas as pl
from jax.experimental.pallas import tpu as pltpu
from jax.sharding import Mesh, PartitionSpec as P

D = 2048
HEAD_DIM = 64
ROT = 32
EPSILON = 1e-05
VMEM_LIMIT = 56 * 2**20

WIDE = ("s", "g", "h")
LINE = ("s", "g")
NARROW = ("m", "c")
CUBE = ("g", "h", "m", "c")


def matmul(left_side, right_side):
    return jnp.dot(left_side, right_side, preferred_element_type=jnp.float32)


def contract_rows(left_side, right_side):
    return lax.dot_general(
        left_side, right_side, (((0,), (0,)), ((), ())), preferred_element_type=jnp.float32
    )


def contract_cols(left_side, right_side):
    return lax.dot_general(
        left_side, right_side, (((1,), (1,)), ((), ())), preferred_element_type=jnp.float32
    )


def pick(blocks, index, axis=0):
    return lax.dynamic_index_in_dim(blocks, index, axis, keepdims=False)


def shifted(value, axis, step):
    count = lax.axis_size(axis)
    return lax.ppermute(value, axis, [(source, (source + step) % count) for source in range(count)])


def in_order(mine, other, index):
    return (jnp.where(index == 0, mine, other), jnp.where(index == 0, other, mine))


def call(kernel, name, grid, in_specs, out_specs, out_shape, scratch=(), flops=0, nbytes=0):
    return pl.pallas_call(
        kernel,
        grid=grid,
        in_specs=in_specs,
        out_specs=out_specs,
        out_shape=out_shape,
        scratch_shapes=list(scratch),
        compiler_params=pltpu.CompilerParams(vmem_limit_bytes=VMEM_LIMIT),
        cost_estimate=pl.CostEstimate(flops=flops, bytes_accessed=nbytes, transcendentals=0),
        name=name,
    )


def whole(*shape):
    return pl.BlockSpec(shape, lambda i: (0,) * len(shape))


def band(rows, cols):
    return pl.BlockSpec((rows, cols), lambda i: (i, 0))


def block_band(rows, row_count, col_blocks, width):
    per = row_count // rows
    return pl.BlockSpec((1, col_blocks, rows, width), lambda i: (i // per, 0, i % per, 0))


ANY = pl.BlockSpec(memory_space=pl.ANY)
SCALARS = pl.BlockSpec(memory_space=pltpu.SMEM)


def struct(shape, dtype):
    return jax.ShapeDtypeStruct(shape, dtype)


def fill(pieces, starts_ref, target, cols, semaphores):
    copies = []
    for n, piece in enumerate(pieces):
        rows = piece.shape[0]
        start = pl.multiple_of(starts_ref[n], rows)
        copy = pltpu.make_async_copy(
            piece.at[:, cols], target.at[pl.ds(start, rows), :], semaphores.at[n]
        )
        copy.start()
        copies.append(copy)
    for copy in copies:
        copy.wait()


def rotary_tables(rows):
    lane = np.arange(2 * HEAD_DIM) % HEAD_DIM
    pair = (lane % (ROT // 2)).astype(np.float32)
    inverse = np.exp(pair * np.float32(-2.0 * math.log(10000.0) / ROT)).astype(np.float32)
    phase = np.arange(rows, dtype=np.float32)[:, None] * inverse[None, :]
    turned = (lane < ROT)[None, :]
    sign = np.where(lane < ROT // 2, -1.0, 1.0)[None, :]
    cosine = np.where(turned, np.cos(phase), 1.0).astype(np.float32)
    sine = np.where(turned, np.sin(phase) * sign, 0.0).astype(np.float32)
    return (cosine, sine)


def turn(values, cosine, sine):
    lane = lax.broadcasted_iota(jnp.int32, values.shape, 1) % HEAD_DIM
    width = values.shape[1]
    half = ROT // 2
    partner = jnp.where(
        lane < half, pltpu.roll(values, width - half, 1), pltpu.roll(values, half, 1)
    )
    return values * cosine + partner * sine


def norm_up_kernel(
    count, starts_ref, tokens_ref, gain_ref, shift_ref, bias_ref, *refs
):
    pieces = refs[:count]
    normed_ref, stats_ref, low_ref, slope_ref, weight, semaphores = refs[count:]

    @pl.when(pl.program_id(0) == 0)
    def _():
        fill(pieces, starts_ref, weight, slice(None), semaphores)

    parts = [tokens_ref[0, j].astype(jnp.float32) for j in range(tokens_ref.shape[1])]
    rows, width = parts[0].shape
    total = sum(jnp.sum(part, axis=1, keepdims=True) for part in parts)
    squares = sum(jnp.sum(part * part, axis=1, keepdims=True) for part in parts)
    mean = total / D
    inverse_std = lax.rsqrt(squares / D - mean * mean + EPSILON)
    up_input = bias_ref[...]
    for j, part in enumerate(parts):
        cols = slice(j * width, (j + 1) * width)
        standard = (part - mean) * inverse_std
        normed = (standard * gain_ref[:, cols] + shift_ref[:, cols]).astype(jnp.bfloat16)
        normed_ref[:, cols] = normed
        up_input = up_input + matmul(normed, weight[cols, :])
    stats_ref[...] = jnp.concatenate(
        [jnp.broadcast_to(mean, (rows, 64)), jnp.broadcast_to(inverse_std, (rows, 64))], axis=1
    )
    root = math.sqrt(2.0 / math.pi)
    square = up_input * up_input
    bend = jnp.tanh(root * (up_input + 0.044715 * square * up_input))
    half = 0.5 * (1.0 + bend)
    low_ref[...] = (up_input * half).astype(jnp.bfloat16)
    slope_ref[...] = half + 0.5 * up_input * (1.0 - bend * bend) * (
        root * (1.0 + 3 * 0.044715 * square)
    )


def norm_up(blocks, gain, shift, bias, weight, rows=256):
    row_blocks, col_blocks, row_count, width = blocks.shape
    pieces, starts = weight
    total, hidden = row_blocks * row_count, bias.shape[1]
    return call(
        partial(norm_up_kernel, len(pieces)),
        "norm_up",
        (total // rows,),
        [SCALARS, block_band(rows, row_count, col_blocks, width)]
        + [whole(1, D), whole(1, D), whole(1, hidden)]
        + [ANY] * len(pieces),
        [band(rows, D), band(rows, 128), band(rows, hidden), band(rows, hidden)],
        [
            struct((total, D), jnp.bfloat16),
            struct((total, 128), jnp.float32),
            struct((total, hidden), jnp.bfloat16),
            struct((total, hidden), jnp.float32),
        ],
        [pltpu.VMEM((D, hidden), jnp.bfloat16), pltpu.SemaphoreType.DMA((len(pieces),))],
        flops=6 * total * D * hidden,
        nbytes=6 * total * D,
    )(starts, blocks, gain, shift, bias, *pieces)


def heads_kernel(count, starts_ref, normed_ref, bias_ref, cosine_ref, sine_ref, *refs):
    pieces = refs[:count]
    heads_ref, weight, semaphores = refs[count:]

    @pl.when(pl.program_id(0) == 0)
    def _():
        fill(pieces, starts_ref, weight, slice(0, weight.shape[1]), semaphores)

    pre = matmul(normed_ref[...], weight[...]) + bias_ref[...]
    lanes = 2 * HEAD_DIM
    cosine, sine = cosine_ref[...], sine_ref[...]
    factor = 1.0 / math.sqrt(HEAD_DIM)
    heads_ref[:, :lanes] = (turn(pre[:, :lanes], cosine, sine) * factor).astype(jnp.bfloat16)
    heads_ref[:, lanes : 2 * lanes] = turn(pre[:, lanes : 2 * lanes], cosine, sine).astype(
        jnp.bfloat16
    )
    heads_ref[:, 2 * lanes :] = pre[:, 2 * lanes :].astype(jnp.bfloat16)


def project_heads(normed, bias, weight, rows=512):
    pieces, starts = weight
    total, width = normed.shape[0], bias.shape[1]
    cosine, sine = rotary_tables(total)
    lanes = 2 * HEAD_DIM
    return call(
        partial(heads_kernel, len(pieces)),
        "project_heads",
        (total // rows,),
        [SCALARS, band(rows, D), whole(1, width), band(rows, lanes), band(rows, lanes)]
        + [ANY] * len(pieces),
        band(rows, width),
        struct((total, width), jnp.bfloat16),
        [pltpu.VMEM((D, width), jnp.bfloat16), pltpu.SemaphoreType.DMA((len(pieces),))],
        flops=4 * total * D * width,
        nbytes=4 * total * D,
    )(starts, normed, bias, jnp.asarray(cosine), jnp.asarray(sine), *pieces)


def out_grad_kernel(count, col_start, starts_ref, cot_ref, *refs):
    pieces = refs[:count]
    out_ref, weight, semaphores = refs[count:]

    @pl.when(pl.program_id(0) == 0)
    def _():
        width = weight.shape[1]
        fill(pieces, starts_ref, weight, slice(col_start, col_start + width), semaphores)

    width = cot_ref.shape[3]
    out = 0.0
    for j in range(cot_ref.shape[1]):
        out = out + matmul(cot_ref[0, j], weight[j * width : (j + 1) * width, :])
    out_ref[...] = out.astype(jnp.bfloat16)


def attended_gradient(cot, weight, width, col_start, rows=512):
    row_blocks, col_blocks, row_count, block_width = cot.shape
    pieces, starts = weight
    total = row_blocks * row_count
    return call(
        partial(out_grad_kernel, len(pieces), col_start),
        "attended_gradient",
        (total // rows,),
        [SCALARS, block_band(rows, row_count, col_blocks, block_width)] + [ANY] * len(pieces),
        band(rows, width),
        struct((total, width), jnp.bfloat16),
        [pltpu.VMEM((D, width), jnp.bfloat16), pltpu.SemaphoreType.DMA((len(pieces),))],
        flops=8 * total * D * width,
        nbytes=4 * total * D,
    )(starts, cot, *pieces)


def up_grad_kernel(count, starts_ref, cot_ref, slope_ref, *refs):
    pieces = refs[:count]
    up_ref, sums_ref, weight, semaphores = refs[count:]

    @pl.when(pl.program_id(0) == 0)
    def _():
        fill(pieces, starts_ref, weight, slice(None), semaphores)
        sums_ref[...] = jnp.zeros_like(sums_ref)

    width = cot_ref.shape[3]
    up = 0.0
    for j in range(cot_ref.shape[1]):
        up = up + matmul(cot_ref[0, j], weight[j * width : (j + 1) * width, :])
    up = (up * slope_ref[...]).astype(jnp.bfloat16)
    up_ref[...] = up
    sums_ref[...] += jnp.sum(up.astype(jnp.float32), axis=0, keepdims=True)


def up_gradient(cot, slope, weight, rows=512):
    row_blocks, col_blocks, row_count, block_width = cot.shape
    pieces, starts = weight
    total, hidden = slope.shape
    return call(
        partial(up_grad_kernel, len(pieces)),
        "up_gradient",
        (total // rows,),
        [SCALARS, block_band(rows, row_count, col_blocks, block_width), band(rows, hidden)]
        + [ANY] * len(pieces),
        [band(rows, hidden), whole(1, hidden)],
        [struct((total, hidden), jnp.bfloat16), struct((1, hidden), jnp.float32)],
        [pltpu.VMEM((D, hidden), jnp.bfloat16), pltpu.SemaphoreType.DMA((len(pieces),))],
        flops=4 * total * D * hidden,
        nbytes=4 * total * D,
    )(starts, cot, slope, *pieces)


def rows_of(index, size):
    return pl.ds(pl.multiple_of(index * size, size), size)


def attention_kernel(
    blocks,
    block,
    qkv_ref,
    grad_ref,
    cosine_ref,
    sine_ref,
    attended_ref,
    pre_grad_ref,
    sums_ref,
    qt_ref,
    kt_ref,
    vt_ref,
    gt_ref,
    score_ref,
    slope_ref,
    k_total,
    v_total,
):
    i = pl.program_id(0)
    width = 2 * HEAD_DIM
    factor = 1.0 / math.sqrt(HEAD_DIM)
    heads = [slice(n * HEAD_DIM, (n + 1) * HEAD_DIM) for n in range(2)]
    chunk = 256
    chunks = qkv_ref.shape[0] // chunk

    @pl.when(i == 0)
    def _():
        def prepare(b, carry):
            rows = rows_of(b, chunk)
            for n, ref in enumerate((qt_ref, kt_ref, vt_ref)):
                ref[:, rows] = qkv_ref[rows, n * width : (n + 1) * width].T
            gt_ref[:, rows] = grad_ref[rows, :].T
            return carry

        lax.fori_loop(0, chunks, prepare, 0)
        k_total[...] = jnp.zeros_like(k_total)
        v_total[...] = jnp.zeros_like(v_total)
        sums_ref[...] = jnp.zeros_like(sums_ref)

    own = rows_of(i, block)
    causal = lax.broadcasted_iota(jnp.int32, (block, block), 0) <= lax.broadcasted_iota(
        jnp.int32, (block, block), 1
    )

    def fold(values, combine):
        return combine(values.reshape(block // 8, 8, block), axis=0)

    def score(j, best, diagonal):
        rows = rows_of(j, block)
        new = []
        for n, head in enumerate(heads):
            start = width + n * HEAD_DIM
            part = matmul(qkv_ref[rows, start : start + HEAD_DIM], qt_ref[head, own])
            if diagonal:
                part = jnp.where(causal, part, -1e30)
            score_ref[n, j] = part
            new.append(jnp.maximum(best[n], fold(part, jnp.max)))
        return tuple(new)

    low = jnp.full((8, block), -1e30, jnp.float32)
    best = lax.fori_loop(0, i, lambda j, b: score(j, b, False), (low, low))
    best = score(i, best, True)
    top = [jnp.max(value, axis=0, keepdims=True) for value in best]

    def weigh(j, carry):
        rows = rows_of(j, block)
        new = []
        for n, head in enumerate(heads):
            total, dots = carry[n]
            begin = 2 * width + n * HEAD_DIM
            weights = jnp.exp(score_ref[n, j] - top[n])
            slope = matmul(qkv_ref[rows, begin : begin + HEAD_DIM], gt_ref[head, own])
            score_ref[n, j] = weights
            slope_ref[n, j] = slope
            new.append((total + fold(weights, jnp.sum), dots + fold(weights * slope, jnp.sum)))
        return tuple(new)

    zero = jnp.zeros((8, block), jnp.float32)
    weighed = lax.fori_loop(0, i + 1, weigh, ((zero, zero), (zero, zero)))
    scales = [1.0 / jnp.sum(total, axis=0, keepdims=True) for total, _ in weighed]
    dots = [
        jnp.sum(dot, axis=0, keepdims=True) * scale for (_, dot), scale in zip(weighed, scales)
    ]

    def push(j, carry):
        rows = rows_of(j, block)
        new = []
        for n, head in enumerate(heads):
            out, q_grad = carry[n]
            probs = score_ref[n, j] * scales[n]
            low = probs.astype(jnp.bfloat16)
            score_grad = (probs * (slope_ref[n, j] - dots[n])).astype(jnp.bfloat16)
            k_total[rows, head] += matmul(score_grad, qkv_ref[own, head])
            v_total[rows, head] += matmul(low, grad_ref[own, head])
            out = out + matmul(vt_ref[head, rows], low)
            new.append((out, q_grad + matmul(kt_ref[head, rows], score_grad)))
        return tuple(new)

    zero = jnp.zeros((HEAD_DIM, block), jnp.float32)
    pushed = lax.fori_loop(0, i + 1, push, ((zero, zero), (zero, zero)))
    attended_ref[own, :] = jnp.concatenate([out for out, _ in pushed], axis=0).T.astype(
        jnp.bfloat16
    )
    q_grad = jnp.concatenate([grad for _, grad in pushed], axis=0).T * factor
    q_pre = turn(q_grad, cosine_ref[own, :], -sine_ref[own, :]).astype(jnp.bfloat16)
    pre_grad_ref[own, :width] = q_pre
    sums_ref[:, :width] += jnp.sum(q_pre.astype(jnp.float32), axis=0, keepdims=True)

    @pl.when(i == blocks - 1)
    def _():
        def finish(b, carry):
            rows = rows_of(b, chunk)
            k_pre = turn(k_total[rows, :], cosine_ref[rows, :], -sine_ref[rows, :])
            k_pre = k_pre.astype(jnp.bfloat16)
            v_pre = v_total[rows, :].astype(jnp.bfloat16)
            pre_grad_ref[rows, width : 2 * width] = k_pre
            pre_grad_ref[rows, 2 * width :] = v_pre
            both = jnp.concatenate([k_pre, v_pre], axis=1).astype(jnp.float32)
            return carry + jnp.sum(both, axis=0, keepdims=True)

        sums_ref[:, width:] = lax.fori_loop(
            0, chunks, finish, jnp.zeros((1, 2 * width), jnp.float32)
        )


def attention(qkv, out_grad, block=512):
    rows, width = qkv.shape[0], 2 * HEAD_DIM
    blocks = rows // block
    cosine, sine = rotary_tables(rows)
    return call(
        partial(attention_kernel, blocks, block),
        "attention",
        (blocks,),
        [whole(rows, 3 * width), whole(rows, width), whole(rows, width), whole(rows, width)],
        [whole(rows, width), whole(rows, 3 * width), whole(1, 3 * width)],
        [
            struct((rows, width), jnp.bfloat16),
            struct((rows, 3 * width), jnp.bfloat16),
            struct((1, 3 * width), jnp.float32),
        ],
        [pltpu.VMEM((width, rows), jnp.bfloat16)] * 4
        + [
            pltpu.VMEM((2, blocks, block, block), jnp.float32),
            pltpu.VMEM((2, blocks, block, block), jnp.float32),
            pltpu.VMEM((rows, width), jnp.float32),
            pltpu.VMEM((rows, width), jnp.float32),
        ],
        flops=28 * 10**9,
        nbytes=rows * width * 16,
    )(qkv, out_grad, jnp.asarray(cosine), jnp.asarray(sine))


def weight_grad_kernel(sources, place_ref, *refs):
    pairs = [refs[2 * n : 2 * n + 2] for n in range(sources)]
    outs = refs[2 * sources :]
    parts = []
    for left_ref, right_ref in pairs:
        if len(right_ref.shape) == 4:
            size = right_ref.shape[2]
            part = 0.0
            for b in range(right_ref.shape[0]):
                rows = slice(b * size, (b + 1) * size)
                part = part + contract_rows(left_ref[rows, :], right_ref[b, 0])
        else:
            part = contract_rows(left_ref[...], right_ref[...])
        parts.append(part.astype(jnp.bfloat16))
    for n, out_ref in enumerate(outs):

        @pl.when(pl.program_id(0) == n)
        def _(out_ref=out_ref):
            start = 0
            for part in parts:
                out_ref[start : start + part.shape[0], :] = part
                start += part.shape[0]


def weight_grad(pairs, place, count):
    cols = D // count
    rows = pairs[0][0].shape[0]
    height = sum(left.shape[1] for left, _ in pairs)

    def at(n, place_ref):
        return lax.rem(place_ref[0] + n, count)

    in_specs, operands = [], []
    for left, right in pairs:
        in_specs.append(pl.BlockSpec(left.shape, lambda n, p: (0, 0)))
        if right.ndim == 4:
            row_blocks, _, row_count, width = right.shape
            per = width // cols
            in_specs.append(
                pl.BlockSpec(
                    (row_blocks, 1, row_count, cols),
                    lambda n, p, per=per: (0, at(n, p) // per, 0, at(n, p) % per),
                )
            )
        else:
            in_specs.append(pl.BlockSpec((rows, cols), lambda n, p: (0, at(n, p))))
        operands += [left, right]
    return pl.pallas_call(
        partial(weight_grad_kernel, len(pairs)),
        grid_spec=pltpu.PrefetchScalarGridSpec(
            num_scalar_prefetch=1,
            grid=(count,),
            in_specs=in_specs,
            out_specs=[pl.BlockSpec((height, cols), lambda n, p: (0, 0))] * count,
        ),
        out_shape=[struct((height, cols), jnp.bfloat16)] * count,
        compiler_params=pltpu.CompilerParams(vmem_limit_bytes=VMEM_LIMIT),
        cost_estimate=pl.CostEstimate(
            flops=4 * rows * height * D, bytes_accessed=4 * rows * D, transcendentals=0
        ),
        name="weight_grad",
    )(place.reshape(1), *operands)


def partial_sum_kernel(counts, cols, *refs):
    sides = len(counts)
    starts = refs[:sides]
    lefts = refs[sides : 2 * sides]
    refs = refs[2 * sides :]
    pieces = []
    for count in counts:
        pieces.append(refs[:count])
        refs = refs[count:]
    out_ref, refs = refs[0], refs[1:]
    weights, semaphores = refs[:sides], refs[sides:]

    @pl.when(pl.program_id(0) == 0)
    def _():
        for n in range(sides):
            fill(pieces[n], starts[n], weights[n], slice(*cols[n]), semaphores[n])

    width = out_ref.shape[3]
    for j in range(out_ref.shape[1]):
        rows = slice(j * width, (j + 1) * width)
        out = 0.0
        for left, weight in zip(lefts, weights):
            out = out + contract_cols(left[...], weight[rows, :])
        out_ref[0, j] = out.astype(jnp.bfloat16)


def partial_sum(sides, row_count, width, name, rows=512):
    total = sides[0][0].shape[0]
    lefts = [left for left, _, _ in sides]
    counts = [len(weight[0]) for _, weight, _ in sides]
    cols = [(start, start + left.shape[1]) for left, _, start in sides]
    pieces = [piece for _, weight, _ in sides for piece in weight[0]]
    depth = sum(left.shape[1] for left in lefts)
    return call(
        partial(partial_sum_kernel, counts, cols),
        name,
        (total // rows,),
        [SCALARS] * len(sides)
        + [band(rows, left.shape[1]) for left in lefts]
        + [ANY] * len(pieces),
        block_band(rows, row_count, D // width, width),
        struct((total // row_count, D // width, row_count, width), jnp.bfloat16),
        [pltpu.VMEM((D, left.shape[1]), jnp.bfloat16) for left in lefts]
        + [pltpu.SemaphoreType.DMA((count,)) for count in counts],
        flops=4 * total * depth * D,
        nbytes=4 * total * D,
    )(*[weight[1] for _, weight, _ in sides], *lefts, *pieces)


def gather_line_first(shard):
    rows = shard.shape[0]
    own_g, own_h = lax.axis_index("g"), lax.axis_index("h")
    split = shard.reshape(rows, 2, 2, -1).transpose(1, 2, 0, 3)
    same, cross = pick(split, own_g), pick(split, 1 - own_g)
    count, place = lax.axis_size(LINE), lax.axis_index(LINE)
    steps = [step for step in range(1, count) if step != 1] + [1]
    arrived = [same] + [shifted(cross if step % 2 else same, LINE, step) for step in steps]
    mine = [pick(piece, own_h) for piece in arrived]
    other = shifted(jnp.stack([pick(piece, 1 - own_h) for piece in arrived]), "h", 1)
    places = [(place - step) % count for step in [0] + steps]
    pieces = mine + [other[n] for n in range(count)]
    starts = [(2 * p + own_h) * rows for p in places] + [(2 * p + 1 - own_h) * rows for p in places]
    return pieces, jnp.stack(starts).astype(jnp.int32)


def gather_side_first(shard):
    rows = shard.shape[0]
    own_g, own_h = lax.axis_index("g"), lax.axis_index("h")
    split = shard.reshape(rows, 2, 2, -1)
    mine = pick(split, own_h, 2)
    other = shifted(pick(split, 1 - own_h, 2), "h", 1)
    pair = in_order(mine, other, own_h)
    same = jnp.concatenate([pick(part, own_g, 1) for part in pair], axis=0)
    cross = jnp.concatenate([pick(part, 1 - own_g, 1) for part in pair], axis=0)
    count, place = lax.axis_size(LINE), lax.axis_index(LINE)
    steps = [step for step in range(1, count) if step != 1] + [1]
    pieces = [same] + [shifted(cross if step % 2 else same, LINE, step) for step in steps]
    starts = [(place - step) % count * 2 * rows for step in [0] + steps]
    return pieces, jnp.stack(starts).astype(jnp.int32)


def scatter(parts):
    count = len(parts)
    own_g, own_h = lax.axis_index("g"), lax.axis_index("h")
    height, cols = parts[0].shape
    steps = [step for step in range(1, count) if step != 1] + [1]
    arrived = {step: shifted(parts[step], LINE, step) for step in steps}
    same, cross = parts[0].astype(jnp.float32), 0.0
    for step in range(1, count):
        if step % 2:
            cross = cross + arrived[step].astype(jnp.float32)
        else:
            same = same + arrived[step].astype(jnp.float32)

    def half(index):
        return [
            lax.dynamic_slice_in_dim(part, index * (cols // 2), cols // 2, 1)
            for part in (same, cross)
        ]

    other = shifted(jnp.stack(half(1 - own_h)).astype(jnp.bfloat16), "h", 1).astype(jnp.float32)
    first, second = [in_order(part, other[n], own_h) for n, part in enumerate(half(own_h))]
    low = [jnp.where(own_g == 0, a, b) for a, b in zip(first, second)]
    high = [jnp.where(own_g == 0, b, a) for a, b in zip(first, second)]
    return jnp.stack(low + high)


def reduce_by_permutes(blocks):
    _, _, rows, cols = blocks.shape
    value = blocks.reshape(2, 2, 2, 2, rows, cols)
    for axis, position in (("c", 3), ("m", 2), ("h", 1), ("g", 0)):
        index = lax.axis_index(axis)
        arrived = shifted(pick(value, 1 - index, position), axis, 1)
        value = pick(value, index, position).astype(jnp.float32) + arrived.astype(jnp.float32)
        if axis != "g":
            value = value.astype(jnp.bfloat16)
    return value


def gather_vectors(packed, shared):
    for axis in ("h", "g"):
        packed = jnp.stack(in_order(packed, shifted(packed, axis, 1), lax.axis_index(axis)))
    sequences, own_s = lax.axis_size("s"), lax.axis_index("s")
    table = jnp.zeros((sequences,) + packed.shape, packed.dtype)
    table = lax.dynamic_update_index_in_dim(table, packed, own_s, 0)
    for step in range(1, sequences):
        table = lax.dynamic_update_index_in_dim(
            table, shifted(packed, "s", step), (own_s - step) % sequences, 0
        )
    table = table.reshape(4 * sequences, -1)
    wide = table[:, :shared]
    for axis in ("c", "m"):
        wide = jnp.stack(in_order(wide, shifted(wide, axis, 1), lax.axis_index(axis)))
    return table, wide.reshape(4, 4 * sequences, shared)


def body(
    tokens,
    cotangent,
    ln_gain,
    ln_shift,
    w_query,
    b_query,
    w_key,
    b_key,
    w_value,
    b_value,
    w_dense,
    b_dense,
    w_fc1,
    b_fc1,
    w_fc2,
    b_fc2,
):
    row_count, feature_count = tokens.shape
    own_g, own_h = lax.axis_index("g"), lax.axis_index("h")
    own_n = lax.axis_index(NARROW)
    quarter = 2 * own_g + own_h
    wide = lax.axis_size(WIDE)
    count, place = lax.axis_size(LINE), lax.axis_index(LINE)
    weight_rows = w_fc1.shape[0]
    lanes = w_query.shape[1] // 4

    token_blocks = lax.all_gather(tokens, CUBE, axis=0, tiled=False)
    token_blocks = token_blocks.reshape(4, 4, row_count, feature_count)
    cot = lax.all_gather(cotangent, CUBE, axis=0, tiled=False)
    cot = cot.reshape(4, 4, row_count, feature_count)

    up_weight = gather_line_first(w_fc1)
    attention_shard = jnp.concatenate(
        [part.reshape(weight_rows, 4, lanes) for part in (w_query, w_key, w_value, w_dense.T)],
        axis=2,
    )
    head_weight = gather_side_first(attention_shard.reshape(weight_rows, -1))
    down_weight = gather_side_first(w_fc2.T)

    vectors = (ln_gain, ln_shift, b_query, b_key, b_value, b_dense, b_fc2, b_fc1)
    lengths = [vector.shape[0] for vector in vectors]
    table, shared = gather_vectors(jnp.concatenate(vectors), 2 * lengths[0])
    shared = shared.astype(jnp.float32)
    gain = shared[:, :, : lengths[0]].reshape(1, D)
    shift = shared[:, :, lengths[0] :].reshape(1, D)
    table = table.astype(jnp.float32)
    local, start = [], 0
    for length in lengths:
        local.append(table[:, start : start + length].reshape(-1))
        start += length

    def quarter_of(vector):
        return pick(vector.reshape(4, -1), quarter)

    qkv_bias = jnp.concatenate([quarter_of(vector) for vector in local[2:5]]).reshape(1, -1)
    up_bias = quarter_of(local[7]).reshape(1, -1)
    own_gain, out_bias = local[0], local[5] + local[6]

    normed, stats, up_low, up_slope = norm_up(token_blocks, gain, shift, up_bias, up_weight)
    qkv = project_heads(normed, qkv_bias, head_weight)
    grad_down = weight_grad([(up_low, cot)], place, count)
    attended_grad = attended_gradient(cot, head_weight, lanes, 3 * lanes)
    up_grad, up_sums = up_gradient(cot, up_slope, down_weight)
    grad_up = weight_grad([(up_grad, normed)], place, count)
    attended, qkv_grad, qkv_sums = attention(qkv, attended_grad)
    normed_grad = partial_sum(
        [(qkv_grad, head_weight, 0), (up_grad, up_weight, 0)],
        row_count,
        feature_count,
        "normed_gradient",
    )
    grad_heads = weight_grad([(qkv_grad, normed), (attended, cot)], place, count)
    branch = partial_sum(
        [(attended, head_weight, 3 * lanes), (up_low, down_weight, 0)],
        row_count,
        feature_count,
        "branch_sum",
    )

    local_x = tokens.astype(jnp.float32)
    branch_sum = lax.psum_scatter(
        branch.reshape(16, row_count, feature_count), CUBE, scatter_dimension=0, tiled=False
    ).astype(jnp.float32)
    output = (local_x + branch_sum + out_bias).astype(jnp.bfloat16)

    hidden = up_low.shape[1]
    grad_down = scatter(grad_down).reshape(4 * hidden, weight_rows)
    grad_up = scatter(grad_up).reshape(4 * hidden, weight_rows).T
    grad_heads = scatter(grad_heads).reshape(4, 4, lanes, weight_rows)
    grad_query, grad_key, grad_value = (
        grad_heads[:, n].reshape(4 * lanes, weight_rows).T for n in range(3)
    )
    grad_dense = grad_heads[:, 3].reshape(4 * lanes, weight_rows)

    standard_grad = reduce_by_permutes(normed_grad)
    own_stats = pick(stats.reshape(4, row_count, 128), quarter)
    row_mean, inverse_std = own_stats[:, :1], own_stats[:, 64:65]
    standard = (local_x - row_mean) * inverse_std
    scaled_grad = standard_grad * own_gain
    row_sums = lax.psum(
        (jnp.sum(scaled_grad, axis=1), jnp.sum(scaled_grad * standard, axis=1)), NARROW
    )
    input_grad = (
        scaled_grad - row_sums[0][:, None] / D - standard * (row_sums[1][:, None] / D)
    ) * inverse_std + cotangent.astype(jnp.float32)

    def spread(vector):
        placed = jnp.zeros((4, vector.shape[0]), jnp.float32)
        placed = lax.dynamic_update_index_in_dim(placed, vector, quarter, 0)
        return placed.reshape(wide, -1)

    terms = [
        jnp.sum(standard_grad * standard, axis=0).reshape(wide, -1),
        jnp.sum(standard_grad, axis=0).reshape(wide, -1),
        spread(qkv_sums[0, :lanes]),
        spread(qkv_sums[0, lanes : 2 * lanes]),
        spread(qkv_sums[0, 2 * lanes :]),
        jnp.sum(cotangent.astype(jnp.float32), axis=0).reshape(wide, -1),
        spread(up_sums[0]),
    ]
    vector_sums = jnp.sum(lax.all_to_all(jnp.concatenate(terms, axis=1), WIDE, 0, 0), axis=0)
    vector_grads, start = [], 0
    for term in terms:
        vector_grads.append(vector_sums[start : start + term.shape[1]])
        start += term.shape[1]
    return (
        output,
        input_grad,
        vector_grads[0],
        vector_grads[1],
        grad_query,
        vector_grads[2],
        grad_key,
        vector_grads[3],
        grad_value,
        vector_grads[4],
        grad_dense,
        vector_grads[5],
        grad_up,
        vector_grads[6],
        grad_down,
        vector_grads[5],
    )


def solution(mesh):
    wide = mesh.shape["wide"]
    inner = Mesh(mesh.devices.reshape(wide // 4, 2, 2, 2, 2), ("s", "g", "h", "m", "c"))
    acts = P(WIDE, NARROW)
    vector = P(NARROW + WIDE)
    by_rows = P(WIDE, NARROW)
    by_cols = P(NARROW, WIDE)
    specs = (
        (acts, acts, vector, vector)
        + (by_rows, vector) * 3
        + (by_cols, vector, by_rows, vector, by_cols, vector)
    )
    return jax.shard_map(body, mesh=inner, in_specs=specs, out_specs=specs, check_vma=False)
```

```python
from functools import partial
import math

import jax
import jax.numpy as jnp
import numpy as np
from jax import lax
from jax.experimental import pallas as pl
from jax.experimental.pallas import tpu as pltpu
from jax.sharding import Mesh, PartitionSpec as P

D = 2048
HEAD_DIM = 64
ROT = 32
EPSILON = 1e-05
VMEM_LIMIT = 56 * 2**20
COST = 1

WIDE = ("s", "g", "h")
LINE = ("s", "g")
NARROW = ("m", "c")
CUBE = ("g", "h", "m", "c")


def matmul(left_side, right_side):
    return jnp.dot(left_side, right_side, preferred_element_type=jnp.float32)


def contract_rows(left_side, right_side):
    return lax.dot_general(
        left_side, right_side, (((0,), (0,)), ((), ())), preferred_element_type=jnp.float32
    )


def contract_cols(left_side, right_side):
    return lax.dot_general(
        left_side, right_side, (((1,), (1,)), ((), ())), preferred_element_type=jnp.float32
    )


def pick(blocks, index, axis=0):
    return lax.dynamic_index_in_dim(blocks, index, axis, keepdims=False)


def shifted(value, axis, step):
    count = lax.axis_size(axis)
    return lax.ppermute(value, axis, [(source, (source + step) % count) for source in range(count)])


def in_order(mine, other, index):
    return (jnp.where(index == 0, mine, other), jnp.where(index == 0, other, mine))


def call(
    kernel, name, grid, in_specs, out_specs, out_shape, scratch=(), flops=0, after=()
):
    skipped = len(after)

    def ordered(*refs):
        kernel(*refs[skipped:])

    run = pl.pallas_call(
        ordered,
        grid=grid,
        in_specs=[ANY] * skipped + list(in_specs),
        out_specs=out_specs,
        out_shape=out_shape,
        scratch_shapes=list(scratch),
        compiler_params=pltpu.CompilerParams(vmem_limit_bytes=VMEM_LIMIT),
        cost_estimate=pl.CostEstimate(flops=COST * flops // 1000, bytes_accessed=0, transcendentals=0),
        name=name,
    )
    return lambda *operands: run(*after, *operands)


def whole(*shape):
    return pl.BlockSpec(shape, lambda i: (0,) * len(shape))


def band(rows, cols):
    return pl.BlockSpec((rows, cols), lambda i: (i, 0))


ANY = pl.BlockSpec(memory_space=pl.ANY)
SCALARS = pl.BlockSpec(memory_space=pltpu.SMEM)


def struct(shape, dtype):
    return jax.ShapeDtypeStruct(shape, dtype)


def rotary_tables(rows):
    lane = np.arange(2 * HEAD_DIM) % HEAD_DIM
    pair = (lane % (ROT // 2)).astype(np.float32)
    inverse = np.exp(pair * np.float32(-2.0 * math.log(10000.0) / ROT)).astype(np.float32)
    phase = np.arange(rows, dtype=np.float32)[:, None] * inverse[None, :]
    turned = (lane < ROT)[None, :]
    sign = np.where(lane < ROT // 2, -1.0, 1.0)[None, :]
    cosine = np.where(turned, np.cos(phase), 1.0).astype(np.float32)
    sine = np.where(turned, np.sin(phase) * sign, 0.0).astype(np.float32)
    return (cosine, sine)


def turn(values, cosine, sine):
    lane = lax.broadcasted_iota(jnp.int32, values.shape, 1) % HEAD_DIM
    width = values.shape[1]
    half = ROT // 2
    partner = jnp.where(
        lane < half, pltpu.roll(values, width - half, 1), pltpu.roll(values, half, 1)
    )
    return values * cosine + partner * sine


def norm_up_kernel(
    tokens_ref, gain_ref, shift_ref, bias_ref, weight_ref, normed_ref, stats_ref, low_ref, slope_ref
):
    parts = [tokens_ref[0, j].astype(jnp.float32) for j in range(tokens_ref.shape[1])]
    rows, width = parts[0].shape
    total = sum(jnp.sum(part, axis=1, keepdims=True) for part in parts)
    squares = sum(jnp.sum(part * part, axis=1, keepdims=True) for part in parts)
    mean = total / D
    inverse_std = lax.rsqrt(squares / D - mean * mean + EPSILON)
    up_input = bias_ref[...]
    for j, part in enumerate(parts):
        cols = slice(j * width, (j + 1) * width)
        standard = (part - mean) * inverse_std
        normed = (standard * gain_ref[:, cols] + shift_ref[:, cols]).astype(jnp.bfloat16)
        normed_ref[:, cols] = normed
        up_input = up_input + matmul(normed, weight_rows_of(weight_ref, j * width, width))
    stats_ref[...] = jnp.concatenate(
        [jnp.broadcast_to(mean, (rows, 64)), jnp.broadcast_to(inverse_std, (rows, 64))], axis=1
    )
    root = math.sqrt(2.0 / math.pi)
    square = up_input * up_input
    bend = jnp.tanh(root * (up_input + 0.044715 * square * up_input))
    half = 0.5 * (1.0 + bend)
    low_ref[...] = (up_input * half).astype(jnp.bfloat16)
    slope_ref[...] = half + 0.5 * up_input * (1.0 - bend * bend) * (
        root * (1.0 + 3 * 0.044715 * square)
    )


class Weight:
    def __init__(self, array, rows, start, width):
        self.array, self.rows, self.width = array, rows, width
        self.spec = pl.BlockSpec(
            (array.shape[0], rows, width), lambda *_: (0, 0, start // width)
        )


def weight_rows_of(weight_ref, start, count):
    _, rows, width = weight_ref.shape
    return weight_ref[pl.ds(start // rows, count // rows)].reshape(count, width)


def norm_up(blocks, gain, shift, bias, weight, rows=256, after=()):
    row_blocks, col_blocks, row_count, width = blocks.shape
    total, hidden = row_blocks * row_count, bias.shape[1]
    per = row_count // rows
    spec = pl.BlockSpec((1, col_blocks, rows, width), lambda i: (i // per, 0, i % per, 0))
    return call(
        norm_up_kernel,
        "norm_up",
        (total // rows,),
        [spec]
        + [whole(1, D), whole(1, D), whole(1, hidden), weight.spec],
        [band(rows, D), band(rows, 128), band(rows, hidden), band(rows, hidden)],
        [
            struct((total, D), jnp.bfloat16),
            struct((total, 128), jnp.float32),
            struct((total, hidden), jnp.bfloat16),
            struct((total, hidden), jnp.float32),
        ],
        flops=6 * total * D * hidden,
        after=after,
    )(blocks, gain, shift, bias, weight.array)


def heads_kernel(normed_ref, bias_ref, cosine_ref, sine_ref, weight_ref, heads_ref):
    pre = matmul(normed_ref[...], weight_rows_of(weight_ref, 0, D)) + bias_ref[...]
    lanes = 2 * HEAD_DIM
    cosine, sine = cosine_ref[...], sine_ref[...]
    factor = 1.0 / math.sqrt(HEAD_DIM)
    heads_ref[:, :lanes] = (turn(pre[:, :lanes], cosine, sine) * factor).astype(jnp.bfloat16)
    heads_ref[:, lanes : 2 * lanes] = turn(pre[:, lanes : 2 * lanes], cosine, sine).astype(
        jnp.bfloat16
    )
    heads_ref[:, 2 * lanes :] = pre[:, 2 * lanes :].astype(jnp.bfloat16)


def project_heads(normed, bias, weight, rows=512, after=()):
    total, width = normed.shape[0], bias.shape[1]
    cosine, sine = rotary_tables(total)
    lanes = 2 * HEAD_DIM
    return call(
        heads_kernel,
        "project_heads",
        (total // rows,),
        [band(rows, D), whole(1, width), band(rows, lanes), band(rows, lanes)]
        + [weight.spec],
        band(rows, width),
        struct((total, width), jnp.bfloat16),
        flops=4 * total * D * width,
        after=after,
    )(normed, bias, jnp.asarray(cosine), jnp.asarray(sine), weight.array)


def cot_spec(cot, rows):
    row_count, width = cot.shape[-2:]
    per = row_count // rows
    return pl.BlockSpec(
        (2, 2, 1, 1, rows, width), lambda i: (0, 0, i // per % 2, i // per // 2, i % per, 0)
    )


def cot_product(cot_ref, weight_ref):
    width = cot_ref.shape[5]
    total = 0.0
    for j in range(4):
        part = cot_ref[j % 2, j // 2, 0, 0]
        total = total + matmul(part, weight_rows_of(weight_ref, j * width, width))
    return total


def out_grad_kernel(cot_ref, weight_ref, out_ref):
    out_ref[...] = cot_product(cot_ref, weight_ref).astype(jnp.bfloat16)


def attended_gradient(cot, weight, width, rows=512, after=()):
    total = 4 * cot.shape[4]
    return call(
        out_grad_kernel,
        "attended_gradient",
        (total // rows,),
        [cot_spec(cot, rows), weight.spec],
        band(rows, width),
        struct((total, width), jnp.bfloat16),
        flops=8 * total * D * width,
        after=after,
    )(cot, weight.array)


def up_grad_kernel(cot_ref, slope_ref, weight_ref, up_ref, sums_ref):
    @pl.when(pl.program_id(0) == 0)
    def _():
        sums_ref[...] = jnp.zeros_like(sums_ref)

    up = (cot_product(cot_ref, weight_ref) * slope_ref[...]).astype(jnp.bfloat16)
    up_ref[...] = up
    sums_ref[...] += jnp.sum(up.astype(jnp.float32), axis=0, keepdims=True)


def up_gradient(cot, slope, weight, rows=512, after=()):
    total, hidden = slope.shape
    return call(
        up_grad_kernel,
        "up_gradient",
        (total // rows,),
        [cot_spec(cot, rows), band(rows, hidden), weight.spec],
        [band(rows, hidden), whole(1, hidden)],
        [struct((total, hidden), jnp.bfloat16), struct((1, hidden), jnp.float32)],
        flops=4 * total * D * hidden,
        after=after,
    )(cot, slope, weight.array)


def rows_of(index, size):
    return pl.ds(pl.multiple_of(index * size, size), size)


def attention_kernel(
    blocks,
    block,
    qkv_ref,
    grad_ref,
    cosine_ref,
    sine_ref,
    attended_ref,
    pre_grad_ref,
    sums_ref,
    qt_ref,
    kt_ref,
    vt_ref,
    gt_ref,
    score_ref,
    slope_ref,
    k_total,
    v_total,
):
    i = pl.program_id(0)
    width = 2 * HEAD_DIM
    factor = 1.0 / math.sqrt(HEAD_DIM)
    heads = [slice(n * HEAD_DIM, (n + 1) * HEAD_DIM) for n in range(2)]
    chunk = 256
    chunks = qkv_ref.shape[0] // chunk

    @pl.when(i == 0)
    def _():
        def prepare(b, carry):
            rows = rows_of(b, chunk)
            for n, ref in enumerate((qt_ref, kt_ref, vt_ref)):
                ref[:, rows] = qkv_ref[rows, n * width : (n + 1) * width].T
            gt_ref[:, rows] = grad_ref[rows, :].T
            return carry

        lax.fori_loop(0, chunks, prepare, 0)
        k_total[...] = jnp.zeros_like(k_total)
        v_total[...] = jnp.zeros_like(v_total)
        sums_ref[...] = jnp.zeros_like(sums_ref)

    own = rows_of(i, block)
    causal = lax.broadcasted_iota(jnp.int32, (block, block), 0) <= lax.broadcasted_iota(
        jnp.int32, (block, block), 1
    )

    def fold(values, combine):
        return combine(values.reshape(block // 8, 8, block), axis=0)

    def score(j, best, diagonal):
        rows = rows_of(j, block)
        new = []
        for n, head in enumerate(heads):
            start = width + n * HEAD_DIM
            part = matmul(qkv_ref[rows, start : start + HEAD_DIM], qt_ref[head, own])
            if diagonal:
                part = jnp.where(causal, part, -1e30)
            score_ref[n, j] = part
            new.append(jnp.maximum(best[n], fold(part, jnp.max)))
        return tuple(new)

    low = jnp.full((8, block), -1e30, jnp.float32)
    best = lax.fori_loop(0, i, lambda j, b: score(j, b, False), (low, low))
    best = score(i, best, True)
    top = [jnp.max(value, axis=0, keepdims=True) for value in best]

    def weigh(j, carry):
        rows = rows_of(j, block)
        new = []
        for n, head in enumerate(heads):
            total, dots = carry[n]
            begin = 2 * width + n * HEAD_DIM
            weights = jnp.exp(score_ref[n, j] - top[n])
            slope = matmul(qkv_ref[rows, begin : begin + HEAD_DIM], gt_ref[head, own])
            score_ref[n, j] = weights
            slope_ref[n, j] = slope
            new.append((total + fold(weights, jnp.sum), dots + fold(weights * slope, jnp.sum)))
        return tuple(new)

    zero = jnp.zeros((8, block), jnp.float32)
    weighed = lax.fori_loop(0, i + 1, weigh, ((zero, zero), (zero, zero)))
    scales = [1.0 / jnp.sum(total, axis=0, keepdims=True) for total, _ in weighed]
    dots = [
        jnp.sum(dot, axis=0, keepdims=True) * scale for (_, dot), scale in zip(weighed, scales)
    ]

    def push(j, carry):
        rows = rows_of(j, block)
        new = []
        for n, head in enumerate(heads):
            out, q_grad = carry[n]
            probs = score_ref[n, j] * scales[n]
            low = probs.astype(jnp.bfloat16)
            score_grad = (probs * (slope_ref[n, j] - dots[n])).astype(jnp.bfloat16)
            k_total[rows, head] += matmul(score_grad, qkv_ref[own, head])
            v_total[rows, head] += matmul(low, grad_ref[own, head])
            out = out + matmul(vt_ref[head, rows], low)
            new.append((out, q_grad + matmul(kt_ref[head, rows], score_grad)))
        return tuple(new)

    zero = jnp.zeros((HEAD_DIM, block), jnp.float32)
    pushed = lax.fori_loop(0, i + 1, push, ((zero, zero), (zero, zero)))
    attended_ref[own, :] = jnp.concatenate([out for out, _ in pushed], axis=0).T.astype(
        jnp.bfloat16
    )
    q_grad = jnp.concatenate([grad for _, grad in pushed], axis=0).T * factor
    q_pre = turn(q_grad, cosine_ref[own, :], -sine_ref[own, :]).astype(jnp.bfloat16)
    pre_grad_ref[own, :width] = q_pre
    sums_ref[:, :width] += jnp.sum(q_pre.astype(jnp.float32), axis=0, keepdims=True)

    @pl.when(i == blocks - 1)
    def _():
        def finish(b, carry):
            rows = rows_of(b, chunk)
            k_pre = turn(k_total[rows, :], cosine_ref[rows, :], -sine_ref[rows, :])
            k_pre = k_pre.astype(jnp.bfloat16)
            v_pre = v_total[rows, :].astype(jnp.bfloat16)
            pre_grad_ref[rows, width : 2 * width] = k_pre
            pre_grad_ref[rows, 2 * width :] = v_pre
            both = jnp.concatenate([k_pre, v_pre], axis=1).astype(jnp.float32)
            return carry + jnp.sum(both, axis=0, keepdims=True)

        sums_ref[:, width:] = lax.fori_loop(
            0, chunks, finish, jnp.zeros((1, 2 * width), jnp.float32)
        )


def attention(qkv, out_grad, block=512, after=()):
    rows, width = qkv.shape[0], 2 * HEAD_DIM
    blocks = rows // block
    cosine, sine = rotary_tables(rows)
    return call(
        partial(attention_kernel, blocks, block),
        "attention",
        (blocks,),
        [whole(rows, 3 * width), whole(rows, width), whole(rows, width), whole(rows, width)],
        [whole(rows, width), whole(rows, 3 * width), whole(1, 3 * width)],
        [
            struct((rows, width), jnp.bfloat16),
            struct((rows, 3 * width), jnp.bfloat16),
            struct((1, 3 * width), jnp.float32),
        ],
        [pltpu.VMEM((width, rows), jnp.bfloat16)] * 4
        + [
            pltpu.VMEM((2, blocks, block, block), jnp.float32),
            pltpu.VMEM((2, blocks, block, block), jnp.float32),
            pltpu.VMEM((rows, width), jnp.float32),
            pltpu.VMEM((rows, width), jnp.float32),
        ],
        flops=28 * 10**9,
        after=after,
    )(qkv, out_grad, jnp.asarray(cosine), jnp.asarray(sine))


def weight_grad_kernel(riders, *refs):
    out_ref, refs = refs[-1], refs[:-1]
    if riders:
        height = out_ref.shape[1] - refs[0].shape[1]
        out_ref[:, height:, :] = refs[0][...]
        refs = refs[1:]
    cols = out_ref.shape[2]
    start = 0
    for left_ref, right_ref in zip(refs[::2], refs[1::2]):
        if len(right_ref.shape) == 6:
            size = right_ref.shape[4]
            part = 0.0
            for b in range(4):
                rows = slice(b * size, (b + 1) * size)
                part = part + contract_rows(left_ref[rows, :], right_ref[0, 0, b % 2, b // 2])
        else:
            part = contract_rows(left_ref[...], right_ref[...])
        part = part.astype(jnp.bfloat16)
        stop = start + part.shape[0]
        for n in range(out_ref.shape[0]):
            out_ref[n, start:stop, :] = part[:, n * cols : (n + 1) * cols]
        start = stop


def weight_grad(pairs, parts, rider=None, after=()):
    cols = D // parts
    per = parts // 4
    rows = pairs[0][0].shape[0]
    height = sum(left.shape[1] for left, _ in pairs)
    in_specs, operands = [], []
    if rider is not None:
        in_specs.append(pl.BlockSpec((per,) + rider.shape[1:], lambda i: (i, 0, 0)))
        operands.append(rider)
        height += rider.shape[1]
    for left, right in pairs:
        in_specs.append(whole(*left.shape))
        if right.ndim == 6:
            in_specs.append(
                pl.BlockSpec(
                    (1, 1, 2, 2, right.shape[4], D // 4), lambda i: (i % 2, i // 2, 0, 0, 0, 0)
                )
            )
        else:
            in_specs.append(pl.BlockSpec((rows, D // 4), lambda i: (0, i)))
        operands += [left, right]
    return call(
        partial(weight_grad_kernel, rider is not None),
        "weight_grad",
        (4,),
        in_specs,
        pl.BlockSpec((per, height, cols), lambda i: (i, 0, 0)),
        struct((parts, height, cols), jnp.bfloat16),
        flops=4 * rows * height * D,
        after=after,
    )(*operands)


def partial_sum_kernel(sides, core_ref, *refs):
    lefts, weights, outs = refs[:sides], refs[sides : 2 * sides], refs[2 * sides :]
    width = outs[0].shape[3]
    for m in range(2):
        for core, out_ref in zip((core_ref[0], 1 - core_ref[0]), outs):
            start = (2 * m + core) * width
            out = 0.0
            for left, weight in zip(lefts, weights):
                out = out + contract_cols(left[...], weight_rows_of(weight, start, width))
            out_ref[m, 0] = out.astype(jnp.bfloat16)


def partial_sum(sides, core, row_count, width, name, rows=512, after=()):
    total = sides[0][0].shape[0]
    per = row_count // rows
    lefts = [left for left, _ in sides]
    depth = sum(left.shape[1] for left in lefts)
    spec = pl.BlockSpec((2, 1, rows, width), lambda i: (0, i // per, i % per, 0))
    shape = struct((2, total // row_count, row_count, width), jnp.bfloat16)
    return call(
        partial(partial_sum_kernel, len(sides)),
        name,
        (total // rows,),
        [SCALARS]
        + [band(rows, left.shape[1]) for left in lefts]
        + [
            weight.spec for _, weight in sides
        ],
        [spec, spec],
        [shape, shape],
        flops=4 * total * depth * D,
        after=after,
    )(core, *lefts, *[weight.array for _, weight in sides])


def switch_specs(count, block):
    zeros = (0,) * (len(block) - 1)
    return [
        pl.BlockSpec(block, lambda k, j, p: (j + k * (count - 1 - j),) + zeros),
        pl.BlockSpec(block, lambda k, j, p: (j * k,) + zeros),
    ]


def prefetch_call(kernel, name, index, grid, in_specs, out_specs, out_shape, after=()):
    skipped = len(after)

    def ordered(index_ref, *refs):
        kernel(index_ref, *refs[skipped:])

    run = pl.pallas_call(
        ordered,
        grid_spec=pltpu.PrefetchScalarGridSpec(
            num_scalar_prefetch=1,
            grid=grid,
            in_specs=[ANY] * skipped + list(in_specs),
            out_specs=out_specs,
        ),
        out_shape=out_shape,
        compiler_params=pltpu.CompilerParams(vmem_limit_bytes=VMEM_LIMIT),
        cost_estimate=pl.CostEstimate(flops=0, bytes_accessed=0, transcendentals=0),
        name=name,
    )
    return lambda *operands: run(index.astype(jnp.int32).reshape(1), *after, *operands)


def column_specs(shards, turned, block):
    specs, width = [], 0
    for flip, shard in zip(turned, shards):
        height, cols = shard.shape
        if flip:
            specs.append(pl.BlockSpec((height // 4, cols), lambda *at: (block(*at), 0)))
            rows, width = cols, width + height // 4
        else:
            specs.append(pl.BlockSpec((height, cols // 4), lambda *at: (0, block(*at))))
            rows, width = height, width + cols // 4
    return specs, rows, width


def write_columns(turned, refs, store):
    start = 0
    for flip, ref in zip(turned, refs):
        part = ref[...].T if flip else ref[...]
        store(slice(start, start + part.shape[1]), part)
        start += part.shape[1]


def pack_kernel(turned, rows, riders, *refs):
    out_ref, refs = refs[-1], refs[:-1]
    if riders:
        rider, refs = refs[0][...], refs[1:]

    def store(cols, part):
        for n in range(out_ref.shape[0]):
            out_ref[n, 0, :rows, cols] = part

    write_columns(turned, refs, store)
    if riders:
        for n in range(out_ref.shape[0]):
            out_ref[n, 0, rows:, :] = rider


def gathered(shards, turned, rider=None, after=()):
    wide = lax.axis_size(WIDE)
    specs, rows, width = column_specs(shards, turned, lambda i: i)
    height = rows
    if rider is not None:
        specs = [whole(*rider.shape)] + specs
        shards = [rider] + shards
        height += rider.shape[0]
    blocks = call(
        partial(pack_kernel, turned, rows, rider is not None),
        "pack",
        (4,),
        specs,
        pl.BlockSpec((wide // 4, 1, height, width), lambda i: (0, i, 0, 0)),
        struct((wide // 4, 4, height, width), jnp.bfloat16),
    )(*shards)
    blocks = lax.optimization_barrier((blocks, *after))[0]
    return lax.all_to_all(blocks.reshape(wide, height, width), WIDE, 0, 0)


def unpack_kernel(turned, arrived_ref, *outs):
    total = arrived_ref[0, 0].astype(jnp.float32)
    for n in range(1, arrived_ref.shape[0]):
        total = total + arrived_ref[n, 0].astype(jnp.float32)
    start = 0
    for flip, out_ref in zip(turned, outs):
        height = out_ref.shape[0] if flip else out_ref.shape[1]
        part = total[start : start + height]
        out_ref[...] = part if flip else part.T
        start += height


def scatter_columns(grad, heights, turned, after=()):
    sequences = lax.axis_size("s")
    _, height, rows = grad.shape
    arrived = lax.all_to_all(grad, WIDE, 0, 0)
    riders = arrived[:, sum(heights) :]
    arrived = arrived.reshape(sequences, 4, height, rows)
    height = sum(heights)
    specs, shapes = [], []
    for flip, part in zip(turned, heights):
        if flip:
            specs.append(pl.BlockSpec((part, rows), lambda i: (i, 0)))
            shapes.append(struct((4 * part, rows), jnp.float32))
        else:
            specs.append(pl.BlockSpec((rows, part), lambda i: (0, i)))
            shapes.append(struct((rows, 4 * part), jnp.float32))
    shards = call(
        partial(unpack_kernel, turned),
        "unpack",
        (4,),
        [pl.BlockSpec((sequences, 1, height, rows), lambda i: (0, i, 0, 0))],
        specs,
        shapes,
        after=after,
    )(arrived)
    return shards, riders


def fold_kernel(index_ref, mine_ref, arrived_ref, keep_ref, send_ref):
    total = mine_ref[0, 0, 0].astype(jnp.float32) + arrived_ref[0, 0, 0].astype(jnp.float32)
    total = total.astype(jnp.bfloat16)

    @pl.when(pl.program_id(0) == 0)
    def _():
        keep_ref[0] = total

    @pl.when(pl.program_id(0) == 1)
    def _():
        send_ref[0] = total


def folded(mine, arrived, axes, axis, after=()):
    position = axes.index(axis)
    high, low = 2**position, 2 ** (len(axes) - 1 - position)
    rows, cols = mine.shape[-2:]
    spec = pl.BlockSpec(
        (1, 1, 1, rows, cols),
        lambda k, j, p: (j // low, lax.rem(k + p[0], 2), lax.rem(j, low), 0, 0),
    )
    shape = (high, 2, low, rows, cols)
    count = high * low
    return prefetch_call(
        fold_kernel,
        "fold",
        lax.axis_index(axis),
        (2, count),
        [spec, spec],
        switch_specs(count, (1, rows, cols)),
        [struct((count, rows, cols), jnp.bfloat16)] * 2,
        after=after,
    )(mine.reshape(shape), arrived.reshape(shape))


def join_kernel(index_ref, mine_ref, other_ref, out_ref):
    @pl.when(pl.program_id(0) == 0)
    def _():
        out_ref[0, 0] = mine_ref[0]

    @pl.when(pl.program_id(0) == 1)
    def _():
        out_ref[0, 0] = other_ref[0]


def joined(mine, axis, after=()):
    other = shifted(mine, axis, 1)
    rows, cols = mine.shape[-2:]
    count = mine.size // (rows * cols)
    out = prefetch_call(
        join_kernel,
        "join",
        lax.axis_index(axis),
        (2, count),
        switch_specs(count, (1, rows, cols)),
        pl.BlockSpec((1, 1, rows, cols), lambda k, j, p: (lax.rem(k + p[0], 2), j, 0, 0)),
        struct((2, count, rows, cols), mine.dtype),
        after=after,
    )(mine.reshape(count, rows, cols), other.reshape(count, rows, cols))
    return out.reshape((2,) + mine.shape)


def gather_narrow(value):
    for axis in ("c", "m"):
        other = shifted(value, axis, 1)
        value = jnp.stack(in_order(value, other, lax.axis_index(axis)))
    return value.reshape((4,) + value.shape[2:])


def summed_along_wide(value):
    for axis in ("h", "g"):
        value = value + shifted(value, axis, 1)
    total = value
    for step in range(1, lax.axis_size("s")):
        total = total + shifted(value, "s", step)
    return total


def body(
    tokens,
    cotangent,
    ln_gain,
    ln_shift,
    w_query,
    b_query,
    w_key,
    b_key,
    w_value,
    b_value,
    w_dense,
    b_dense,
    w_fc1,
    b_fc1,
    w_fc2,
    b_fc2,
):
    row_count, feature_count = tokens.shape
    own_g, own_h = lax.axis_index("g"), lax.axis_index("h")
    own_n = lax.axis_index(NARROW)
    quarter = 2 * own_g + own_h
    wide = lax.axis_size(WIDE)
    weight_rows = w_fc1.shape[0]
    lanes = w_query.shape[1] // 4

    core = lax.axis_index("c").astype(jnp.int32).reshape(1)

    vectors = (ln_gain, ln_shift, b_query, b_key, b_value, b_dense, b_fc2, b_fc1)
    lengths = [vector.shape[0] for vector in vectors]
    hidden = w_fc1.shape[1] // 4
    width = 4 * lanes + hidden
    packed = jnp.concatenate(vectors)
    packed = jnp.pad(packed, (0, 16 * width - packed.shape[0])).reshape(16, width)

    tokens_full = lax.all_gather(tokens, CUBE, axis=0, tiled=False)
    tokens_full = tokens_full.reshape(4, 4, row_count, feature_count)
    cot = joined(cotangent, "g")
    arrived = gathered(
        [w_query, w_key, w_value, w_dense, w_fc1],
        [False, False, False, True, False],
        packed,
        after=[cot],
    )
    cot = joined(joined(cot, "h"), "m")
    cot = lax.all_gather(cot, "c", axis=0, tiled=False)
    down_weight = Weight(gathered([w_fc2], [True]), weight_rows, 0, hidden)
    qkv_weight = Weight(arrived, weight_rows, 0, 3 * lanes)
    dense_weight = Weight(arrived, weight_rows, 3 * lanes, lanes)
    up_weight = Weight(arrived, weight_rows, 4 * lanes, hidden)

    here = arrived[:, weight_rows:].reshape(wide, 16 * width)
    local, start = [], 0
    for length in lengths:
        local.append(here[:, start : start + length].astype(jnp.float32).reshape(-1))
        start += length
    shared = gather_narrow(here[:, : 2 * lengths[0]].astype(jnp.float32))
    gain = shared[:, :, : lengths[0]].reshape(1, D)
    shift = shared[:, :, lengths[0] :].reshape(1, D)

    def quarter_of(vector):
        return pick(vector.reshape(4, -1), quarter)

    qkv_bias = jnp.concatenate([quarter_of(vector) for vector in local[2:5]]).reshape(1, -1)
    up_bias = quarter_of(local[7]).reshape(1, -1)
    own_gain, out_bias = local[0], local[5] + local[6]

    normed, stats, up_low, up_slope = norm_up(tokens_full, gain, shift, up_bias, up_weight)
    qkv = project_heads(normed, qkv_bias, qkv_weight)
    attended_grad = attended_gradient(cot, dense_weight, lanes, after=[qkv])
    grad_down = weight_grad([(up_low, cot)], wide, after=[attended_grad])
    attended, qkv_grad, qkv_sums = attention(qkv, attended_grad, after=[grad_down])
    up_grad, up_sums = up_gradient(cot, up_slope, down_weight, after=[attended])
    normed_grad = partial_sum(
        [(qkv_grad, qkv_weight), (up_grad, up_weight)],
        core,
        row_count,
        feature_count,
        "normed_gradient",
    )
    grad_up = weight_grad([(up_grad, normed)], wide, after=normed_grad[:1])
    branch = partial_sum(
        [(attended, dense_weight), (up_low, down_weight)],
        core,
        row_count,
        feature_count,
        "branch_sum",
        after=[grad_up],
    )
    first = folded(normed_grad[0], shifted(normed_grad[1], "c", 1), "mgh", "m", after=branch[:1])
    second = folded(branch[0], shifted(branch[1], "c", 1), "mgh", "h", after=first[:1])
    def spread(vector):
        placed = jnp.zeros((4, vector.shape[0]), jnp.float32)
        placed = lax.dynamic_update_index_in_dim(placed, vector, quarter, 0)
        return placed.reshape(wide, -1)

    terms = [
        spread(qkv_sums[0, :lanes]),
        spread(qkv_sums[0, lanes : 2 * lanes]),
        spread(qkv_sums[0, 2 * lanes :]),
        jnp.sum(cotangent.astype(jnp.float32), axis=0).reshape(wide, -1),
        spread(up_sums[0]),
    ]
    rider = jnp.concatenate(terms, axis=1).astype(jnp.bfloat16)
    early_count = rider.shape[1]
    rider = jnp.pad(rider, ((0, 0), (0, 16 * weight_rows - early_count)))
    grad_heads = weight_grad(
        [(qkv_grad, normed), (attended, cot)],
        wide,
        rider.reshape(wide, 16, weight_rows),
        after=second[:1],
    )
    (grad_down,), _ = scatter_columns(grad_down, [hidden], [True], after=[grad_heads])
    first = folded(first[0], shifted(first[1], "m", 1), "gh", "h", after=[grad_down])
    second = folded(second[0], shifted(second[1], "h", 1), "mg", "m", after=first[:1])
    (grad_up,), _ = scatter_columns(grad_up, [hidden], [False], after=second[:1])
    first = folded(first[0], shifted(first[1], "h", 1), "g", "g", after=[grad_up])
    second = folded(second[0], shifted(second[1], "m", 1), "g", "g", after=first[:1])
    (grad_query, grad_key, grad_value, grad_dense), riders = scatter_columns(
        grad_heads, [lanes] * 4, [False, False, False, True]
    )
    early = jnp.sum(riders.astype(jnp.float32), axis=0).reshape(-1)[:early_count]

    def last(keep, send):
        return keep[0].astype(jnp.float32) + shifted(send[0], "g", 1).astype(jnp.float32)

    local_x = tokens.astype(jnp.float32)
    standard_grad = last(*first)
    output = (local_x + last(*second) + out_bias).astype(jnp.bfloat16)
    own_stats = pick(stats.reshape(4, row_count, 128), quarter)
    row_mean, inverse_std = own_stats[:, :1], own_stats[:, 64:65]
    standard = (local_x - row_mean) * inverse_std
    scaled_grad = standard_grad * own_gain
    row_sums = lax.psum(
        (jnp.sum(scaled_grad, axis=1), jnp.sum(scaled_grad * standard, axis=1)), NARROW
    )
    input_grad = (
        scaled_grad - row_sums[0][:, None] / D - standard * (row_sums[1][:, None] / D)
    ) * inverse_std + cotangent.astype(jnp.float32)

    own_terms = [jnp.sum(standard_grad * standard, axis=0), jnp.sum(standard_grad, axis=0)]
    own_terms = [term.reshape(wide, -1) for term in own_terms]
    late = summed_along_wide(jnp.concatenate(own_terms, axis=1))
    terms = own_terms + terms
    vector_sums = jnp.concatenate([pick(late, lax.axis_index(WIDE)), early])
    vector_grads, start = [], 0
    for term in terms:
        vector_grads.append(vector_sums[start : start + term.shape[1]])
        start += term.shape[1]
    return (
        output,
        input_grad,
        vector_grads[0],
        vector_grads[1],
        grad_query,
        vector_grads[2],
        grad_key,
        vector_grads[3],
        grad_value,
        vector_grads[4],
        grad_dense,
        vector_grads[5],
        grad_up,
        vector_grads[6],
        grad_down,
        vector_grads[5],
    )


def solution(mesh):
    wide = mesh.shape["wide"]
    inner = Mesh(mesh.devices.reshape(wide // 4, 2, 2, 2, 2), ("s", "g", "h", "m", "c"))
    acts = P(WIDE, NARROW)
    vector = P(NARROW + WIDE)
    by_rows = P(WIDE, NARROW)
    by_cols = P(NARROW, WIDE)
    specs = (
        (acts, acts, vector, vector)
        + (by_rows, vector) * 3
        + (by_cols, vector, by_rows, vector, by_cols, vector)
    )
    return jax.shard_map(body, mesh=inner, in_specs=specs, out_specs=specs, check_vma=False)
```

```python
from functools import partial
import math

import jax
import jax.numpy as jnp
import numpy as np
from jax import lax
from jax.experimental import pallas as pl
from jax.experimental.pallas import tpu as pltpu
from jax.sharding import Mesh, PartitionSpec as P

D = 2048
HEAD_DIM = 64
ROT = 32
EPSILON = 1e-05
VMEM_LIMIT = 56 * 2**20
COST = 1

WIDE = ("s", "g", "h")
LINE = ("s", "g")
NARROW = ("m", "c")
CUBE = ("g", "h", "m", "c")


def matmul(left_side, right_side):
    return jnp.dot(left_side, right_side, preferred_element_type=jnp.float32)


def contract_rows(left_side, right_side):
    return lax.dot_general(
        left_side, right_side, (((0,), (0,)), ((), ())), preferred_element_type=jnp.float32
    )


def contract_cols(left_side, right_side):
    return lax.dot_general(
        left_side, right_side, (((1,), (1,)), ((), ())), preferred_element_type=jnp.float32
    )


def pick(blocks, index, axis=0):
    return lax.dynamic_index_in_dim(blocks, index, axis, keepdims=False)


def shifted(value, axis, step):
    count = lax.axis_size(axis)
    return lax.ppermute(value, axis, [(source, (source + step) % count) for source in range(count)])


def in_order(mine, other, index):
    return (jnp.where(index == 0, mine, other), jnp.where(index == 0, other, mine))


def call(
    kernel, name, grid, in_specs, out_specs, out_shape, scratch=(), flops=0, after=()
):
    skipped = len(after)

    def ordered(*refs):
        kernel(*refs[skipped:])

    run = pl.pallas_call(
        ordered,
        grid=grid,
        in_specs=[ANY] * skipped + list(in_specs),
        out_specs=out_specs,
        out_shape=out_shape,
        scratch_shapes=list(scratch),
        compiler_params=pltpu.CompilerParams(vmem_limit_bytes=VMEM_LIMIT),
        cost_estimate=pl.CostEstimate(flops=COST * flops // 1000, bytes_accessed=0, transcendentals=0),
        name=name,
    )
    return lambda *operands: run(*after, *operands)


def whole(*shape):
    return pl.BlockSpec(shape, lambda i: (0,) * len(shape))


def band(rows, cols):
    return pl.BlockSpec((rows, cols), lambda i: (i, 0))


ANY = pl.BlockSpec(memory_space=pl.ANY)
SCALARS = pl.BlockSpec(memory_space=pltpu.SMEM)


def struct(shape, dtype):
    return jax.ShapeDtypeStruct(shape, dtype)


def rotary_tables(rows):
    lane = np.arange(2 * HEAD_DIM) % HEAD_DIM
    pair = (lane % (ROT // 2)).astype(np.float32)
    inverse = np.exp(pair * np.float32(-2.0 * math.log(10000.0) / ROT)).astype(np.float32)
    phase = np.arange(rows, dtype=np.float32)[:, None] * inverse[None, :]
    turned = (lane < ROT)[None, :]
    sign = np.where(lane < ROT // 2, -1.0, 1.0)[None, :]
    cosine = np.where(turned, np.cos(phase), 1.0).astype(np.float32)
    sine = np.where(turned, np.sin(phase) * sign, 0.0).astype(np.float32)
    return (cosine, sine)


def turn(values, cosine, sine):
    lane = lax.broadcasted_iota(jnp.int32, values.shape, 1) % HEAD_DIM
    width = values.shape[1]
    half = ROT // 2
    partner = jnp.where(
        lane < half, pltpu.roll(values, width - half, 1), pltpu.roll(values, half, 1)
    )
    return values * cosine + partner * sine


def norm_up_kernel(
    tokens_ref, gain_ref, shift_ref, bias_ref, weight_ref, normed_ref, stats_ref, low_ref, slope_ref
):
    parts = [tokens_ref[0, j].astype(jnp.float32) for j in range(tokens_ref.shape[1])]
    rows, width = parts[0].shape
    total = sum(jnp.sum(part, axis=1, keepdims=True) for part in parts)
    squares = sum(jnp.sum(part * part, axis=1, keepdims=True) for part in parts)
    mean = total / D
    inverse_std = lax.rsqrt(squares / D - mean * mean + EPSILON)
    up_input = bias_ref[...]
    for j, part in enumerate(parts):
        cols = slice(j * width, (j + 1) * width)
        standard = (part - mean) * inverse_std
        normed = (standard * gain_ref[:, cols] + shift_ref[:, cols]).astype(jnp.bfloat16)
        normed_ref[:, cols] = normed
        up_input = up_input + matmul(normed, weight_rows_of(weight_ref, j * width, width))
    stats_ref[...] = jnp.concatenate(
        [jnp.broadcast_to(mean, (rows, 64)), jnp.broadcast_to(inverse_std, (rows, 64))], axis=1
    )
    root = math.sqrt(2.0 / math.pi)
    square = up_input * up_input
    bend = jnp.tanh(root * (up_input + 0.044715 * square * up_input))
    half = 0.5 * (1.0 + bend)
    low_ref[...] = (up_input * half).astype(jnp.bfloat16)
    slope_ref[...] = half + 0.5 * up_input * (1.0 - bend * bend) * (
        root * (1.0 + 3 * 0.044715 * square)
    )


class Weight:
    def __init__(self, array, rows, start, width):
        self.array, self.rows, self.width = array, rows, width
        self.spec = pl.BlockSpec(
            array.shape[:-2] + (rows, width),
            lambda *_: (0,) * (len(array.shape) - 1) + (start // width,),
        )


def weight_rows_of(weight_ref, start, count):
    _, rows, width = weight_ref.shape
    return weight_ref[pl.ds(start // rows, count // rows)].reshape(count, width)


def norm_up(blocks, gain, shift, bias, weight, rows=256, after=()):
    row_blocks, col_blocks, row_count, width = blocks.shape
    total, hidden = row_blocks * row_count, bias.shape[1]
    per = row_count // rows
    spec = pl.BlockSpec((1, col_blocks, rows, width), lambda i: (i // per, 0, i % per, 0))
    return call(
        norm_up_kernel,
        "norm_up",
        (total // rows,),
        [spec]
        + [whole(1, D), whole(1, D), whole(1, hidden), weight.spec],
        [band(rows, D), band(rows, 128), band(rows, hidden), band(rows, hidden)],
        [
            struct((total, D), jnp.bfloat16),
            struct((total, 128), jnp.float32),
            struct((total, hidden), jnp.bfloat16),
            struct((total, hidden), jnp.float32),
        ],
        flops=6 * total * D * hidden,
        after=after,
    )(blocks, gain, shift, bias, weight.array)


def heads_kernel(normed_ref, bias_ref, cosine_ref, sine_ref, weight_ref, heads_ref):
    pre = matmul(normed_ref[...], weight_rows_of(weight_ref, 0, D)) + bias_ref[...]
    lanes = 2 * HEAD_DIM
    cosine, sine = cosine_ref[...], sine_ref[...]
    factor = 1.0 / math.sqrt(HEAD_DIM)
    heads_ref[:, :lanes] = (turn(pre[:, :lanes], cosine, sine) * factor).astype(jnp.bfloat16)
    heads_ref[:, lanes : 2 * lanes] = turn(pre[:, lanes : 2 * lanes], cosine, sine).astype(
        jnp.bfloat16
    )
    heads_ref[:, 2 * lanes :] = pre[:, 2 * lanes :].astype(jnp.bfloat16)


def project_heads(normed, bias, weight, rows=512, after=()):
    total, width = normed.shape[0], bias.shape[1]
    cosine, sine = rotary_tables(total)
    lanes = 2 * HEAD_DIM
    return call(
        heads_kernel,
        "project_heads",
        (total // rows,),
        [band(rows, D), whole(1, width), band(rows, lanes), band(rows, lanes)]
        + [weight.spec],
        band(rows, width),
        struct((total, width), jnp.bfloat16),
        flops=4 * total * D * width,
        after=after,
    )(normed, bias, jnp.asarray(cosine), jnp.asarray(sine), weight.array)


def cot_spec(cot, rows):
    row_count, width = cot.shape[-2:]
    per = row_count // rows
    return pl.BlockSpec(
        (1, 4, 1, rows, width), lambda i: (i // per % 2, 0, i // per // 2, i % per, 0)
    )


def back_kernel(
    cot_ref, slope_ref, dense_ref, down_ref, attended_ref, up_ref, sums_ref
):
    @pl.when(pl.program_id(0) == 0)
    def _():
        sums_ref[...] = jnp.zeros_like(sums_ref)

    width = cot_ref.shape[4]
    attended, up = 0.0, 0.0
    for j in range(4):
        part = cot_ref[0, j, 0]
        attended = attended + matmul(part, weight_rows_of(dense_ref, j * width, width))
        up = up + matmul(part, weight_rows_of(down_ref, j * width, width))
    attended_ref[...] = attended.astype(jnp.bfloat16)
    up = (up * slope_ref[...]).astype(jnp.bfloat16)
    up_ref[...] = up
    sums_ref[...] += jnp.sum(up.astype(jnp.float32), axis=0, keepdims=True)


def back_through(cot, slope, dense, down, rows=512, after=()):
    total, hidden = slope.shape
    lanes = dense.width
    return call(
        back_kernel,
        "back_through",
        (total // rows,),
        [cot_spec(cot, rows), band(rows, hidden), dense.spec, down.spec],
        [band(rows, lanes), band(rows, hidden), whole(1, hidden)],
        [
            struct((total, lanes), jnp.bfloat16),
            struct((total, hidden), jnp.bfloat16),
            struct((1, hidden), jnp.float32),
        ],
        flops=4 * total * D * (hidden + lanes),
        after=after,
    )(cot, slope, dense.array, down.array)


def rows_of(index, size):
    return pl.ds(pl.multiple_of(index * size, size), size)


HEADS_HERE = [slice(n * HEAD_DIM, (n + 1) * HEAD_DIM) for n in range(2)]


def turned_into(ref, source_ref, cols):
    chunk = 256

    def one(b, carry):
        rows = rows_of(b, chunk)
        ref[:, rows] = source_ref[rows, cols].T
        return carry

    lax.fori_loop(0, source_ref.shape[0] // chunk, one, 0)


def causal_block(block):
    return lax.broadcasted_iota(jnp.int32, (block, block), 0) <= lax.broadcasted_iota(
        jnp.int32, (block, block), 1
    )


def fold_rows(values, combine):
    rows, cols = values.shape
    return combine(values.reshape(rows // 8, 8, cols), axis=0)


def attention_kernel(block, qkv_ref, attended_ref, log_sums_ref, qt_ref, vt_ref, score_ref):
    i = pl.program_id(0)
    width = 2 * HEAD_DIM

    @pl.when(i == 0)
    def _():
        turned_into(qt_ref, qkv_ref, slice(0, width))
        turned_into(vt_ref, qkv_ref, slice(2 * width, 3 * width))
        log_sums_ref[...] = jnp.zeros_like(log_sums_ref)

    own = rows_of(i, block)
    causal = causal_block(block)

    def score(j, best, diagonal):
        rows = rows_of(j, block)
        new = []
        for n, head in enumerate(HEADS_HERE):
            start = width + n * HEAD_DIM
            part = matmul(qkv_ref[rows, start : start + HEAD_DIM], qt_ref[head, own])
            if diagonal:
                part = jnp.where(causal, part, -1e30)
            score_ref[n, j] = part
            new.append(jnp.maximum(best[n], fold_rows(part, jnp.max)))
        return tuple(new)

    low = jnp.full((8, block), -1e30, jnp.float32)
    best = lax.fori_loop(0, i, lambda j, b: score(j, b, False), (low, low))
    best = score(i, best, True)
    top = [jnp.max(value, axis=0, keepdims=True) for value in best]

    def weigh(j, carry):
        new = []
        for n in range(2):
            weights = jnp.exp(score_ref[n, j] - top[n])
            score_ref[n, j] = weights
            new.append(carry[n] + fold_rows(weights, jnp.sum))
        return tuple(new)

    zero = jnp.zeros((8, block), jnp.float32)
    totals = lax.fori_loop(0, i + 1, weigh, (zero, zero))
    totals = [jnp.sum(total, axis=0, keepdims=True) for total in totals]
    scales = [1.0 / total for total in totals]
    for n in range(2):
        log_sums_ref[n : n + 1, own] = top[n] + jnp.log(totals[n])

    def push(j, carry):
        rows = rows_of(j, block)
        new = []
        for n, head in enumerate(HEADS_HERE):
            probs = (score_ref[n, j] * scales[n]).astype(jnp.bfloat16)
            new.append(carry[n] + matmul(vt_ref[head, rows], probs))
        return tuple(new)

    zero = jnp.zeros((HEAD_DIM, block), jnp.float32)
    out = lax.fori_loop(0, i + 1, push, (zero, zero))
    attended_ref[own, :] = jnp.concatenate(out, axis=0).T.astype(jnp.bfloat16)


def attention(qkv, block=512, after=()):
    rows, width = qkv.shape[0], 2 * HEAD_DIM
    blocks = rows // block
    return call(
        partial(attention_kernel, block),
        "attention",
        (blocks,),
        [whole(rows, 3 * width)],
        [whole(rows, width), whole(8, rows)],
        [struct((rows, width), jnp.bfloat16), struct((8, rows), jnp.float32)],
        [pltpu.VMEM((width, rows), jnp.bfloat16)] * 2
        + [pltpu.VMEM((2, blocks, block, block), jnp.float32)],
        flops=10 * 10**9,
        after=after,
    )(qkv)


def attention_back_kernel(
    blocks,
    block,
    qkv_ref,
    grad_ref,
    log_sums_ref,
    cosine_ref,
    sine_ref,
    pre_grad_ref,
    sums_ref,
    qt_ref,
    kt_ref,
    gt_ref,
    prob_ref,
    slope_ref,
    k_total,
    v_total,
):
    i = pl.program_id(0)
    width = 2 * HEAD_DIM
    factor = 1.0 / math.sqrt(HEAD_DIM)
    chunk = 256

    @pl.when(i == 0)
    def _():
        turned_into(qt_ref, qkv_ref, slice(0, width))
        turned_into(kt_ref, qkv_ref, slice(width, 2 * width))
        turned_into(gt_ref, grad_ref, slice(0, width))
        k_total[...] = jnp.zeros_like(k_total)
        v_total[...] = jnp.zeros_like(v_total)
        sums_ref[...] = jnp.zeros_like(sums_ref)

    own = rows_of(i, block)
    causal = causal_block(block)
    log_sums = [log_sums_ref[n : n + 1, own] for n in range(2)]

    def weigh(j, carry, diagonal):
        rows = rows_of(j, block)
        new = []
        for n, head in enumerate(HEADS_HERE):
            start = width + n * HEAD_DIM
            scores = matmul(qkv_ref[rows, start : start + HEAD_DIM], qt_ref[head, own])
            probs = jnp.exp(scores - log_sums[n])
            if diagonal:
                probs = jnp.where(causal, probs, 0.0)
            start += width
            slope = matmul(qkv_ref[rows, start : start + HEAD_DIM], gt_ref[head, own])
            prob_ref[n, j] = probs
            slope_ref[n, j] = slope
            new.append(carry[n] + fold_rows(probs * slope, jnp.sum))
        return tuple(new)

    zero = jnp.zeros((8, block), jnp.float32)
    dots = lax.fori_loop(0, i, lambda j, c: weigh(j, c, False), (zero, zero))
    dots = weigh(i, dots, True)
    dots = [jnp.sum(dot, axis=0, keepdims=True) for dot in dots]

    def push(j, carry):
        rows = rows_of(j, block)
        new = []
        for n, head in enumerate(HEADS_HERE):
            probs = prob_ref[n, j]
            score_grad = (probs * (slope_ref[n, j] - dots[n])).astype(jnp.bfloat16)
            k_total[rows, head] += matmul(score_grad, qkv_ref[own, head])
            v_total[rows, head] += matmul(probs.astype(jnp.bfloat16), grad_ref[own, head])
            new.append(carry[n] + matmul(kt_ref[head, rows], score_grad))
        return tuple(new)

    zero = jnp.zeros((HEAD_DIM, block), jnp.float32)
    q_grad = lax.fori_loop(0, i + 1, push, (zero, zero))
    q_grad = jnp.concatenate(q_grad, axis=0).T * factor
    q_pre = turn(q_grad, cosine_ref[own, :], -sine_ref[own, :]).astype(jnp.bfloat16)
    pre_grad_ref[own, :width] = q_pre
    sums_ref[:, :width] += jnp.sum(q_pre.astype(jnp.float32), axis=0, keepdims=True)

    @pl.when(i == blocks - 1)
    def _():
        def finish(b, carry):
            rows = rows_of(b, chunk)
            k_pre = turn(k_total[rows, :], cosine_ref[rows, :], -sine_ref[rows, :])
            k_pre = k_pre.astype(jnp.bfloat16)
            v_pre = v_total[rows, :].astype(jnp.bfloat16)
            pre_grad_ref[rows, width : 2 * width] = k_pre
            pre_grad_ref[rows, 2 * width :] = v_pre
            both = jnp.concatenate([k_pre, v_pre], axis=1).astype(jnp.float32)
            return carry + jnp.sum(both, axis=0, keepdims=True)

        sums_ref[:, width:] = lax.fori_loop(
            0, qkv_ref.shape[0] // chunk, finish, jnp.zeros((1, 2 * width), jnp.float32)
        )


def attention_back(qkv, out_grad, log_sums, block=512, after=()):
    rows, width = qkv.shape[0], 2 * HEAD_DIM
    blocks = rows // block
    cosine, sine = rotary_tables(rows)
    return call(
        partial(attention_back_kernel, blocks, block),
        "attention_back",
        (blocks,),
        [whole(rows, 3 * width), whole(rows, width), whole(8, rows)]
        + [whole(rows, width), whole(rows, width)],
        [whole(rows, 3 * width), whole(1, 3 * width)],
        [struct((rows, 3 * width), jnp.bfloat16), struct((1, 3 * width), jnp.float32)],
        [pltpu.VMEM((width, rows), jnp.bfloat16)] * 3
        + [pltpu.VMEM((2, blocks, block, block), jnp.float32)] * 2
        + [pltpu.VMEM((rows, width), jnp.float32)] * 2,
        flops=20 * 10**9,
        after=after,
    )(qkv, out_grad, log_sums, jnp.asarray(cosine), jnp.asarray(sine))


def weight_grad_kernel(riders, *refs):
    out_ref, refs = refs[-1], refs[:-1]
    if riders:
        height = out_ref.shape[1] - refs[0].shape[1]
        out_ref[:, height:, :] = refs[0][...]
        refs = refs[1:]
    cols = out_ref.shape[2]
    start = 0
    for left_ref, right_ref in zip(refs[::2], refs[1::2]):
        if len(right_ref.shape) == 5:
            size = right_ref.shape[3]
            part = 0.0
            for b in range(4):
                rows = slice(b * size, (b + 1) * size)
                part = part + contract_rows(left_ref[rows, :], right_ref[b % 2, 0, b // 2])
        else:
            part = contract_rows(left_ref[...], right_ref[...])
        part = part.astype(jnp.bfloat16)
        stop = start + part.shape[0]
        for n in range(out_ref.shape[0]):
            out_ref[n, start:stop, :] = part[:, n * cols : (n + 1) * cols]
        start = stop


def weight_grad(pairs, parts, rider=None, after=()):
    cols = D // parts
    per = parts // 4
    rows = pairs[0][0].shape[0]
    height = sum(left.shape[1] for left, _ in pairs)
    in_specs, operands = [], []
    if rider is not None:
        in_specs.append(pl.BlockSpec((per,) + rider.shape[1:], lambda i: (i, 0, 0)))
        operands.append(rider)
        height += rider.shape[1]
    for left, right in pairs:
        in_specs.append(whole(*left.shape))
        if right.ndim == 5:
            in_specs.append(
                pl.BlockSpec((2, 1, 2, right.shape[3], D // 4), lambda i: (0, i, 0, 0, 0))
            )
        else:
            in_specs.append(pl.BlockSpec((rows, D // 4), lambda i: (0, i)))
        operands += [left, right]
    return call(
        partial(weight_grad_kernel, rider is not None),
        "weight_grad",
        (4,),
        in_specs,
        pl.BlockSpec((per, height, cols), lambda i: (i, 0, 0)),
        struct((parts, height, cols), jnp.bfloat16),
        flops=4 * rows * height * D,
        after=after,
    )(*operands)


def partial_sum_kernel(sides, halves, index_ref, *refs):
    lefts, refs = refs[: 2 * sides], refs[2 * sides :]
    weights, others, outs = refs[:sides], refs[sides : 2 * sides], refs[2 * sides :]
    rows, width = outs[0].shape[1:]
    own_m, core = index_ref[0], index_ref[1]
    for n_m, m in enumerate((own_m, 1 - own_m)):
        out = 0.0
        for n in range(sides):
            weight = weight_rows_of(weights[n], (2 * m + core) * width, width)
            out = out + contract_cols(lefts[n][...], weight)
            other = others[n][m].reshape(width, weight.shape[1])
            out = out + contract_cols(lefts[sides + n][...], other)
        out = out.astype(jnp.bfloat16)
        for half in range(halves):
            outs[2 * half + n_m][0] = out[half * rows : (half + 1) * rows]


def partial_sum(sides, row_count, width, name, halves, after=()):
    total = sides[0][0].shape[0]
    rows = row_count // halves
    lefts = [side[0] for side in sides] + [side[1] for side in sides]
    weights = [side[2] for side in sides]
    others = [side[3] for side in sides]
    depth = sum(left.shape[1] for left in lefts)
    outs = 2 * halves
    index = jnp.stack([lax.axis_index("m"), lax.axis_index("c")]).astype(jnp.int32)
    return call(
        partial(partial_sum_kernel, len(sides), halves),
        name,
        (total // row_count,),
        [SCALARS]
        + [band(row_count, left.shape[1]) for left in lefts]
        + [weight.spec for weight in weights]
        + [other.spec for other in others],
        [pl.BlockSpec((1, rows, width), lambda i: (i, 0, 0))] * outs,
        [struct((total // row_count, rows, width), jnp.bfloat16)] * outs,
        flops=2 * total * depth * D,
        after=after,
    )(index, *lefts, *[weight.array for weight in weights], *[other.array for other in others])


def switch_specs(count, block):
    zeros = (0,) * (len(block) - 1)
    return [
        pl.BlockSpec(block, lambda k, j, p: (j + k * (count - 1 - j),) + zeros),
        pl.BlockSpec(block, lambda k, j, p: (j * k,) + zeros),
    ]


def prefetch_call(kernel, name, index, grid, in_specs, out_specs, out_shape, after=()):
    skipped = len(after)

    def ordered(index_ref, *refs):
        kernel(index_ref, *refs[skipped:])

    run = pl.pallas_call(
        ordered,
        grid_spec=pltpu.PrefetchScalarGridSpec(
            num_scalar_prefetch=1,
            grid=grid,
            in_specs=[ANY] * skipped + list(in_specs),
            out_specs=out_specs,
        ),
        out_shape=out_shape,
        compiler_params=pltpu.CompilerParams(vmem_limit_bytes=VMEM_LIMIT),
        cost_estimate=pl.CostEstimate(flops=0, bytes_accessed=0, transcendentals=0),
        name=name,
    )
    return lambda *operands: run(index.astype(jnp.int32).reshape(1), *after, *operands)


def column_specs(shards, turned, block):
    specs, width = [], 0
    for flip, shard in zip(turned, shards):
        height, cols = shard.shape
        if flip:
            specs.append(pl.BlockSpec((height // 4, cols), lambda *at: (block(*at), 0)))
            rows, width = cols, width + height // 4
        else:
            specs.append(pl.BlockSpec((height, cols // 4), lambda *at: (0, block(*at))))
            rows, width = height, width + cols // 4
    return specs, rows, width


def write_columns(turned, refs, store):
    start = 0
    for flip, ref in zip(turned, refs):
        part = ref[...].T if flip else ref[...]
        store(slice(start, start + part.shape[1]), part)
        start += part.shape[1]


def pack_kernel(turned, rows, riders, *refs):
    out_ref, refs = refs[-1], refs[:-1]
    if riders:
        rider, refs = refs[0][...], refs[1:]

    def store(cols, part):
        for n in range(out_ref.shape[0]):
            out_ref[n, 0, :rows, cols] = part

    write_columns(turned, refs, store)
    if riders:
        for n in range(out_ref.shape[0]):
            out_ref[n, 0, rows:, :] = rider


def packed(shards, turned, rider=None):
    wide = lax.axis_size(WIDE)
    specs, rows, width = column_specs(shards, turned, lambda i: i)
    height = rows
    if rider is not None:
        specs = [whole(*rider.shape)] + specs
        shards = [rider] + shards
        height += rider.shape[0]
    blocks = call(
        partial(pack_kernel, turned, rows, rider is not None),
        "pack",
        (4,),
        specs,
        pl.BlockSpec((wide // 4, 1, height, width), lambda i: (0, i, 0, 0)),
        struct((wide // 4, 4, height, width), jnp.bfloat16),
    )(*shards)
    return blocks.reshape(wide, height, width)


def exchanged(blocks, after=()):
    blocks = lax.optimization_barrier((blocks, *after))[0]
    return lax.all_to_all(blocks, WIDE, 0, 0)


def unpack_kernel(turned, arrived_ref, *outs):
    total = arrived_ref[0, 0].astype(jnp.float32)
    for n in range(1, arrived_ref.shape[0]):
        total = total + arrived_ref[n, 0].astype(jnp.float32)
    start = 0
    for flip, out_ref in zip(turned, outs):
        height = out_ref.shape[0] if flip else out_ref.shape[1]
        part = total[start : start + height]
        out_ref[...] = part if flip else part.T
        start += height


def scatter_columns(grad, heights, turned, after=()):
    sequences = lax.axis_size("s")
    _, height, rows = grad.shape
    arrived = lax.all_to_all(grad, WIDE, 0, 0)
    riders = arrived[:, sum(heights) :]
    arrived = arrived.reshape(sequences, 4, height, rows)
    height = sum(heights)
    specs, shapes = [], []
    for flip, part in zip(turned, heights):
        if flip:
            specs.append(pl.BlockSpec((part, rows), lambda i: (i, 0)))
            shapes.append(struct((4 * part, rows), jnp.float32))
        else:
            specs.append(pl.BlockSpec((rows, part), lambda i: (0, i)))
            shapes.append(struct((rows, 4 * part), jnp.float32))
    shards = call(
        partial(unpack_kernel, turned),
        "unpack",
        (4,),
        [pl.BlockSpec((sequences, 1, height, rows), lambda i: (0, i, 0, 0))],
        specs,
        shapes,
        after=after,
    )(arrived)
    return shards, riders


def fold_kernel(index_ref, mine_keep, mine_send, arrived_keep, arrived_send, keep_ref, send_ref):
    keep_ref[...] = mine_keep[...] + arrived_keep[...]
    send_ref[...] = mine_send[...] + arrived_send[...]


def folded(mine, arrived, axes, axis, after=()):
    position = axes.index(axis)
    high, low = 2**position, 2 ** (len(axes) - 1 - position)
    rows, cols = mine.shape[-2:]
    shape = (high, 2, low * rows, cols)
    steps = 2 if low > 1 else 1
    block = low * rows // steps
    halves = [
        pl.BlockSpec((high, None, block, cols), lambda j, p: (0, p[0], j, 0)),
        pl.BlockSpec((high, None, block, cols), lambda j, p: (0, 1 - p[0], j, 0)),
    ]
    out = pl.BlockSpec((high, block, cols), lambda j, p: (0, j, 0))
    mine, arrived = mine.reshape(shape), arrived.reshape(shape)
    keep, send = prefetch_call(
        fold_kernel,
        "fold",
        lax.axis_index(axis),
        (steps,),
        halves * 2,
        [out, out],
        [struct((high, low * rows, cols), jnp.bfloat16)] * 2,
        after=after,
    )(mine, mine, arrived, arrived)
    return [part.reshape(high * low, rows, cols) for part in (keep, send)]


def join_kernel(index_ref, mine_ref, other_ref, out_ref):
    out_ref[index_ref[0]] = mine_ref[...]
    out_ref[1 - index_ref[0]] = other_ref[...]


def joined(mine, axis, after=()):
    other = shifted(mine, axis, 1)
    rows, cols = mine.size // mine.shape[-1] // 2, mine.shape[-1]
    spec = pl.BlockSpec((rows, cols), lambda j, p: (j, 0))
    out = prefetch_call(
        join_kernel,
        "join",
        lax.axis_index(axis),
        (2,),
        [spec, spec],
        pl.BlockSpec((2, rows, cols), lambda j, p: (0, j, 0)),
        struct((2, 2 * rows, cols), mine.dtype),
        after=after,
    )(mine.reshape(2 * rows, cols), other.reshape(2 * rows, cols))
    return out.reshape((2,) + mine.shape)


def finish_kernel(tokens_ref, keep_ref, arrived_ref, bias_ref, out_ref):
    total = tokens_ref[...].astype(jnp.float32) + keep_ref[...].astype(jnp.float32)
    total = total + arrived_ref[...].astype(jnp.float32) + bias_ref[...]
    out_ref[...] = total.astype(jnp.bfloat16)


def finished(tokens, keep, arrived, bias, after=()):
    spec = whole(*tokens.shape)
    return call(
        finish_kernel,
        "finish",
        (1,),
        [spec, spec, spec, whole(*bias.shape)],
        spec,
        struct(tokens.shape, tokens.dtype),
        after=after,
    )(tokens, keep, arrived, bias)


def gather_narrow(value):
    for axis in ("c", "m"):
        other = shifted(value, axis, 1)
        value = jnp.stack(in_order(value, other, lax.axis_index(axis)))
    return value.reshape((4,) + value.shape[2:])


def summed_along_wide(value):
    for axis in ("h", "g"):
        value = value + shifted(value, axis, 1)
    total = value
    for step in range(1, lax.axis_size("s")):
        total = total + shifted(value, "s", step)
    return total


def body(
    tokens,
    cotangent,
    ln_gain,
    ln_shift,
    w_query,
    b_query,
    w_key,
    b_key,
    w_value,
    b_value,
    w_dense,
    b_dense,
    w_fc1,
    b_fc1,
    w_fc2,
    b_fc2,
):
    row_count, feature_count = tokens.shape
    own_g, own_h = lax.axis_index("g"), lax.axis_index("h")
    own_n = lax.axis_index(NARROW)
    quarter = 2 * own_g + own_h
    wide = lax.axis_size(WIDE)
    weight_rows = w_fc1.shape[0]
    lanes = w_query.shape[1] // 4

    vectors = (ln_gain, ln_shift, b_query, b_key, b_value, b_dense, b_fc2, b_fc1)
    lengths = [vector.shape[0] for vector in vectors]
    hidden = w_fc1.shape[1] // 4
    rider = jnp.concatenate(vectors)
    rider = jnp.pad(rider, (0, 16 * hidden - rider.shape[0])).reshape(16, hidden)

    tokens_full = lax.all_gather(tokens, CUBE, axis=0, tiled=False)
    tokens_full = tokens_full.reshape(4, 4, row_count, feature_count)
    up_blocks = packed([w_fc1], [False], rider)
    head_blocks = packed([w_query, w_key, w_value, w_dense], [False, False, False, True])
    cot = joined(cotangent, "g", after=[up_blocks, head_blocks])
    arrived = exchanged(up_blocks, after=[cot])
    cot = lax.all_gather(cot, ("h", "m", "c"), axis=0, tiled=False)
    cot = cot.reshape(2, 4, 2, row_count, feature_count)
    head_arrived = exchanged(head_blocks)
    down_arrived = exchanged(packed([w_fc2], [True]))
    up_weight = Weight(arrived, weight_rows, 0, hidden)
    qkv_weight = Weight(head_arrived, weight_rows, 0, 3 * lanes)
    dense_weight = Weight(head_arrived, weight_rows, 3 * lanes, lanes)
    down_weight = Weight(down_arrived, weight_rows, 0, hidden)

    def from_other_core(array):
        split = array[:, :weight_rows].reshape(2, 2, wide // 4, weight_rows, -1)
        return shifted(pick(split, 1 - lax.axis_index("c"), 1), "c", 1)

    up_other = Weight(from_other_core(arrived), weight_rows, 0, hidden)
    head_other = from_other_core(head_arrived)
    qkv_other = Weight(head_other, weight_rows, 0, 3 * lanes)
    dense_other = Weight(head_other, weight_rows, 3 * lanes, lanes)
    down_other = Weight(from_other_core(down_arrived), weight_rows, 0, hidden)

    here = arrived[:, weight_rows:].reshape(wide, 16 * hidden)
    local, start = [], 0
    for length in lengths:
        local.append(here[:, start : start + length].astype(jnp.float32).reshape(-1))
        start += length
    shared = gather_narrow(here[:, : 2 * lengths[0]].astype(jnp.float32))
    gain = shared[:, :, : lengths[0]].reshape(1, D)
    shift = shared[:, :, lengths[0] :].reshape(1, D)

    def quarter_of(vector):
        return pick(vector.reshape(4, -1), quarter)

    qkv_bias = jnp.concatenate([quarter_of(vector) for vector in local[2:5]]).reshape(1, -1)
    up_bias = quarter_of(local[7]).reshape(1, -1)
    own_gain, out_bias = local[0], local[5] + local[6]

    normed, stats, up_low, up_slope = norm_up(
        tokens_full, gain, shift, up_bias, up_weight, after=[up_other.array]
    )
    qkv = project_heads(normed, qkv_bias, qkv_weight)
    attended, log_sums = attention(qkv)
    grad_down = weight_grad([(up_low, cot)], wide, after=[attended])
    attended_grad, up_grad, up_sums = back_through(
        cot, up_slope, dense_weight, down_weight, after=[grad_down]
    )
    branch = partial_sum(
        [
            (attended, shifted(attended, "c", 1), dense_weight, dense_other),
            (up_low, shifted(up_low, "c", 1), down_weight, down_other),
        ],
        row_count,
        feature_count,
        "branch_sum",
        1,
        after=[up_grad],
    )
    qkv_grad, qkv_sums = attention_back(qkv, attended_grad, log_sums, after=branch[:1])
    qkv_grad_other = shifted(qkv_grad, "c", 1)

    def spread(vector):
        placed = jnp.zeros((4, vector.shape[0]), jnp.float32)
        placed = lax.dynamic_update_index_in_dim(placed, vector, quarter, 0)
        return placed.reshape(wide, -1)

    terms = [
        spread(qkv_sums[0, :lanes]),
        spread(qkv_sums[0, lanes : 2 * lanes]),
        spread(qkv_sums[0, 2 * lanes :]),
        jnp.sum(cotangent.astype(jnp.float32), axis=0).reshape(wide, -1),
        spread(up_sums[0]),
    ]
    rider = jnp.concatenate(terms, axis=1).astype(jnp.bfloat16)
    early_count = rider.shape[1]
    rider = jnp.pad(rider, ((0, 0), (0, 16 * weight_rows - early_count)))
    grad_rest = weight_grad(
        [(up_grad, normed), (qkv_grad, normed), (attended, cot)],
        wide,
        rider.reshape(wide, 16, weight_rows),
    )
    second = folded(branch[0], shifted(branch[1], "m", 1), "gh", "h", after=[grad_rest, qkv_grad_other])
    grad_rest = lax.optimization_barrier((grad_rest, second[0]))[0]
    normed_grad = partial_sum(
        [
            (qkv_grad, qkv_grad_other, qkv_weight, qkv_other),
            (up_grad, shifted(up_grad, "c", 1), up_weight, up_other),
        ],
        row_count,
        feature_count,
        "normed_gradient",
        2,
        after=second[:1],
    )

    (grad_down,), _ = scatter_columns(grad_down, [hidden], [True], after=normed_grad[:1])
    first = [normed_grad[:2], normed_grad[2:]]
    first[0] = folded(first[0][0], shifted(first[0][1], "m", 1), "gh", "h", after=[grad_down])
    second = folded(second[0], shifted(second[1], "h", 1), "g", "g", after=first[0][:1])
    first[1] = folded(first[1][0], shifted(first[1][1], "m", 1), "gh", "h", after=second[:1])
    first[0] = folded(first[0][0], shifted(first[0][1], "h", 1), "g", "g", after=first[1][:1])
    first[1] = folded(first[1][0], shifted(first[1][1], "h", 1), "g", "g", after=first[0][:1])
    output = finished(
        tokens,
        second[0][0],
        shifted(second[1][0], "g", 1),
        out_bias.reshape(1, -1),
        after=first[1][:1],
    )
    (grad_up, grad_query, grad_key, grad_value, grad_dense), riders = scatter_columns(
        grad_rest,
        [hidden] + [lanes] * 4,
        [False, False, False, False, True],
        after=[output],
    )
    early = jnp.sum(riders.astype(jnp.float32), axis=0).reshape(-1)[:early_count]

    def last(keep, send):
        arrived = lax.optimization_barrier((shifted(send[0], "g", 1), grad_dense))[0]
        return keep[0].astype(jnp.float32) + arrived.astype(jnp.float32)

    local_x = tokens.astype(jnp.float32)
    standard_grad = jnp.concatenate([last(*part) for part in first], axis=0)
    own_stats = pick(stats.reshape(4, row_count, 128), quarter)
    row_mean, inverse_std = own_stats[:, :1], own_stats[:, 64:65]
    standard = (local_x - row_mean) * inverse_std
    scaled_grad = standard_grad * own_gain
    row_sums = jnp.stack([jnp.sum(scaled_grad, axis=1), jnp.sum(scaled_grad * standard, axis=1)])
    for axis in ("c", "m"):
        row_sums = row_sums + shifted(row_sums, axis, 1)
    input_grad = (
        scaled_grad - row_sums[0][:, None] / D - standard * (row_sums[1][:, None] / D)
    ) * inverse_std + cotangent.astype(jnp.float32)

    own_terms = [jnp.sum(standard_grad * standard, axis=0), jnp.sum(standard_grad, axis=0)]
    own_terms = [term.reshape(wide, -1) for term in own_terms]
    late = summed_along_wide(jnp.concatenate(own_terms, axis=1))
    terms = own_terms + terms
    vector_sums = jnp.concatenate([pick(late, lax.axis_index(WIDE)), early])
    vector_grads, start = [], 0
    for term in terms:
        vector_grads.append(vector_sums[start : start + term.shape[1]])
        start += term.shape[1]
    return (
        output,
        input_grad,
        vector_grads[0],
        vector_grads[1],
        grad_query,
        vector_grads[2],
        grad_key,
        vector_grads[3],
        grad_value,
        vector_grads[4],
        grad_dense,
        vector_grads[5],
        grad_up,
        vector_grads[6],
        grad_down,
        vector_grads[5],
    )


def solution(mesh):
    wide = mesh.shape["wide"]
    inner = Mesh(mesh.devices.reshape(wide // 4, 2, 2, 2, 2), ("s", "g", "h", "m", "c"))
    acts = P(WIDE, NARROW)
    vector = P(NARROW + WIDE)
    by_rows = P(WIDE, NARROW)
    by_cols = P(NARROW, WIDE)
    specs = (
        (acts, acts, vector, vector)
        + (by_rows, vector) * 3
        + (by_cols, vector, by_rows, vector, by_cols, vector)
    )
    return jax.shard_map(body, mesh=inner, in_specs=specs, out_specs=specs, check_vma=False)
```

```python
from functools import partial
import math

import jax
import jax.numpy as jnp
import numpy as np
from jax import lax
from jax.experimental import pallas as pl
from jax.experimental.pallas import tpu as pltpu
from jax.sharding import Mesh, PartitionSpec as P

D = 2048
HEAD_DIM = 64
ROT = 32
EPSILON = 1e-05
VMEM_LIMIT = 56 * 2**20
COST = 1

WIDE = ("s", "g", "h")
LINE = ("s", "g")
LINE = ("s", "g")
NARROW = ("m", "c")
CUBE = ("g", "h", "m", "c")


def matmul(left_side, right_side):
    return jnp.dot(left_side, right_side, preferred_element_type=jnp.float32)


def contract_rows(left_side, right_side):
    return lax.dot_general(
        left_side, right_side, (((0,), (0,)), ((), ())), preferred_element_type=jnp.float32
    )


def contract_cols(left_side, right_side):
    return lax.dot_general(
        left_side, right_side, (((1,), (1,)), ((), ())), preferred_element_type=jnp.float32
    )


def pick(blocks, index, axis=0):
    return lax.dynamic_index_in_dim(blocks, index, axis, keepdims=False)


def shifted(value, axis, step):
    count = lax.axis_size(axis)
    return lax.ppermute(value, axis, [(source, (source + step) % count) for source in range(count)])


def in_order(mine, other, index):
    return (jnp.where(index == 0, mine, other), jnp.where(index == 0, other, mine))


def call(
    kernel, name, grid, in_specs, out_specs, out_shape, scratch=(), flops=0, after=()
):
    skipped = len(after)

    def ordered(*refs):
        kernel(*refs[skipped:])

    run = pl.pallas_call(
        ordered,
        grid=grid,
        in_specs=[ANY] * skipped + list(in_specs),
        out_specs=out_specs,
        out_shape=out_shape,
        scratch_shapes=list(scratch),
        compiler_params=pltpu.CompilerParams(vmem_limit_bytes=VMEM_LIMIT),
        cost_estimate=pl.CostEstimate(flops=COST * flops // 1000, bytes_accessed=0, transcendentals=0),
        name=name,
    )
    return lambda *operands: run(*after, *operands)


def whole(*shape):
    return pl.BlockSpec(shape, lambda i: (0,) * len(shape))


def band(rows, cols):
    return pl.BlockSpec((rows, cols), lambda i: (i, 0))


ANY = pl.BlockSpec(memory_space=pl.ANY)
SCALARS = pl.BlockSpec(memory_space=pltpu.SMEM)


def struct(shape, dtype):
    return jax.ShapeDtypeStruct(shape, dtype)


def rotary_tables(rows):
    lane = np.arange(2 * HEAD_DIM) % HEAD_DIM
    pair = (lane % (ROT // 2)).astype(np.float32)
    inverse = np.exp(pair * np.float32(-2.0 * math.log(10000.0) / ROT)).astype(np.float32)
    phase = np.arange(rows, dtype=np.float32)[:, None] * inverse[None, :]
    turned = (lane < ROT)[None, :]
    sign = np.where(lane < ROT // 2, -1.0, 1.0)[None, :]
    cosine = np.where(turned, np.cos(phase), 1.0).astype(np.float32)
    sine = np.where(turned, np.sin(phase) * sign, 0.0).astype(np.float32)
    return (cosine, sine)


def turn(values, cosine, sine):
    lane = lax.broadcasted_iota(jnp.int32, values.shape, 1) % HEAD_DIM
    width = values.shape[1]
    half = ROT // 2
    partner = jnp.where(
        lane < half, pltpu.roll(values, width - half, 1), pltpu.roll(values, half, 1)
    )
    return values * cosine + partner * sine


def norm_up_kernel(
    tokens_ref, gain_ref, shift_ref, bias_ref, weight_ref, normed_ref, stats_ref, low_ref, slope_ref
):
    parts = [tokens_ref[0, j].astype(jnp.float32) for j in range(tokens_ref.shape[1])]
    rows, width = parts[0].shape
    total = sum(jnp.sum(part, axis=1, keepdims=True) for part in parts)
    squares = sum(jnp.sum(part * part, axis=1, keepdims=True) for part in parts)
    mean = total / D
    inverse_std = lax.rsqrt(squares / D - mean * mean + EPSILON)
    up_input = bias_ref[...]
    for j, part in enumerate(parts):
        cols = slice(j * width, (j + 1) * width)
        standard = (part - mean) * inverse_std
        normed = (standard * gain_ref[:, cols] + shift_ref[:, cols]).astype(jnp.bfloat16)
        normed_ref[:, cols] = normed
        up_input = up_input + matmul(normed, weight_rows_of(weight_ref, j * width, width))
    stats_ref[...] = jnp.concatenate(
        [jnp.broadcast_to(mean, (rows, 64)), jnp.broadcast_to(inverse_std, (rows, 64))], axis=1
    )
    root = math.sqrt(2.0 / math.pi)
    square = up_input * up_input
    bend = jnp.tanh(root * (up_input + 0.044715 * square * up_input))
    half = 0.5 * (1.0 + bend)
    low_ref[...] = (up_input * half).astype(jnp.bfloat16)
    slope_ref[...] = half + 0.5 * up_input * (1.0 - bend * bend) * (
        root * (1.0 + 3 * 0.044715 * square)
    )


class Weight:
    def __init__(self, array, rows, start, width):
        self.array, self.rows, self.width = array, rows, width
        self.spec = pl.BlockSpec(
            array.shape[:-2] + (rows, width),
            lambda *_: (0,) * (len(array.shape) - 1) + (start // width,),
        )


def weight_rows_of(weight_ref, start, count):
    _, rows, width = weight_ref.shape
    return weight_ref[pl.ds(start // rows, count // rows)].reshape(count, width)


def norm_up(blocks, gain, shift, bias, weight, rows=256, after=()):
    row_blocks, col_blocks, row_count, width = blocks.shape
    total, hidden = row_blocks * row_count, bias.shape[1]
    per = row_count // rows
    spec = pl.BlockSpec((1, col_blocks, rows, width), lambda i: (i // per, 0, i % per, 0))
    return call(
        norm_up_kernel,
        "norm_up",
        (total // rows,),
        [spec]
        + [whole(1, D), whole(1, D), whole(1, hidden), weight.spec],
        [band(rows, D), band(rows, 128), band(rows, hidden), band(rows, hidden)],
        [
            struct((total, D), jnp.bfloat16),
            struct((total, 128), jnp.float32),
            struct((total, hidden), jnp.bfloat16),
            struct((total, hidden), jnp.float32),
        ],
        flops=6 * total * D * hidden,
        after=after,
    )(blocks, gain, shift, bias, weight.array)


def heads_kernel(normed_ref, bias_ref, cosine_ref, sine_ref, weight_ref, heads_ref):
    pre = matmul(normed_ref[...], weight_rows_of(weight_ref, 0, D)) + bias_ref[...]
    lanes = 2 * HEAD_DIM
    cosine, sine = cosine_ref[...], sine_ref[...]
    factor = 1.0 / math.sqrt(HEAD_DIM)
    heads_ref[:, :lanes] = (turn(pre[:, :lanes], cosine, sine) * factor).astype(jnp.bfloat16)
    heads_ref[:, lanes : 2 * lanes] = turn(pre[:, lanes : 2 * lanes], cosine, sine).astype(
        jnp.bfloat16
    )
    heads_ref[:, 2 * lanes :] = pre[:, 2 * lanes :].astype(jnp.bfloat16)


def project_heads(normed, bias, weight, rows=512, after=()):
    total, width = normed.shape[0], bias.shape[1]
    cosine, sine = rotary_tables(total)
    lanes = 2 * HEAD_DIM
    return call(
        heads_kernel,
        "project_heads",
        (total // rows,),
        [band(rows, D), whole(1, width), band(rows, lanes), band(rows, lanes)]
        + [weight.spec],
        band(rows, width),
        struct((total, width), jnp.bfloat16),
        flops=4 * total * D * width,
        after=after,
    )(normed, bias, jnp.asarray(cosine), jnp.asarray(sine), weight.array)


def cot_spec(cot, rows):
    row_count, width = cot.shape[-2:]
    per = row_count // rows
    return pl.BlockSpec(
        (1, 4, 1, rows, width), lambda i: (i // per % 2, 0, i // per // 2, i % per, 0)
    )


def back_kernel(
    cot_ref, slope_ref, dense_ref, down_ref, attended_ref, up_ref, sums_ref
):
    @pl.when(pl.program_id(0) == 0)
    def _():
        sums_ref[...] = jnp.zeros_like(sums_ref)

    width = cot_ref.shape[4]
    attended, up = 0.0, 0.0
    for j in range(4):
        part = cot_ref[0, j, 0]
        attended = attended + matmul(part, weight_rows_of(dense_ref, j * width, width))
        up = up + matmul(part, weight_rows_of(down_ref, j * width, width))
    attended_ref[...] = attended.astype(jnp.bfloat16)
    up = (up * slope_ref[...]).astype(jnp.bfloat16)
    up_ref[...] = up
    sums_ref[...] += jnp.sum(up.astype(jnp.float32), axis=0, keepdims=True)


def back_through(cot, slope, dense, down, rows=512, after=()):
    total, hidden = slope.shape
    lanes = dense.width
    return call(
        back_kernel,
        "back_through",
        (total // rows,),
        [cot_spec(cot, rows), band(rows, hidden), dense.spec, down.spec],
        [band(rows, lanes), band(rows, hidden), whole(1, hidden)],
        [
            struct((total, lanes), jnp.bfloat16),
            struct((total, hidden), jnp.bfloat16),
            struct((1, hidden), jnp.float32),
        ],
        flops=4 * total * D * (hidden + lanes),
        after=after,
    )(cot, slope, dense.array, down.array)


def rows_of(index, size):
    return pl.ds(pl.multiple_of(index * size, size), size)


HEADS_HERE = [slice(n * HEAD_DIM, (n + 1) * HEAD_DIM) for n in range(2)]


def turned_into(ref, source_ref, cols):
    chunk = 256

    def one(b, carry):
        rows = rows_of(b, chunk)
        ref[:, rows] = source_ref[rows, cols].T
        return carry

    lax.fori_loop(0, source_ref.shape[0] // chunk, one, 0)


def causal_block(block):
    return lax.broadcasted_iota(jnp.int32, (block, block), 0) <= lax.broadcasted_iota(
        jnp.int32, (block, block), 1
    )


def fold_rows(values, combine):
    rows, cols = values.shape
    return combine(values.reshape(rows // 8, 8, cols), axis=0)


def attention_kernel(block, qkv_ref, attended_ref, log_sums_ref, qt_ref, vt_ref, score_ref):
    i = pl.program_id(0)
    width = 2 * HEAD_DIM

    @pl.when(i == 0)
    def _():
        turned_into(qt_ref, qkv_ref, slice(0, width))
        turned_into(vt_ref, qkv_ref, slice(2 * width, 3 * width))
        log_sums_ref[...] = jnp.zeros_like(log_sums_ref)

    own = rows_of(i, block)
    causal = causal_block(block)

    def score(j, best, diagonal):
        rows = rows_of(j, block)
        new = []
        for n, head in enumerate(HEADS_HERE):
            start = width + n * HEAD_DIM
            part = matmul(qkv_ref[rows, start : start + HEAD_DIM], qt_ref[head, own])
            if diagonal:
                part = jnp.where(causal, part, -1e30)
            score_ref[n, j] = part
            new.append(jnp.maximum(best[n], fold_rows(part, jnp.max)))
        return tuple(new)

    low = jnp.full((8, block), -1e30, jnp.float32)
    best = lax.fori_loop(0, i, lambda j, b: score(j, b, False), (low, low))
    best = score(i, best, True)
    top = [jnp.max(value, axis=0, keepdims=True) for value in best]

    def weigh(j, carry):
        new = []
        for n in range(2):
            weights = jnp.exp(score_ref[n, j] - top[n])
            score_ref[n, j] = weights
            new.append(carry[n] + fold_rows(weights, jnp.sum))
        return tuple(new)

    zero = jnp.zeros((8, block), jnp.float32)
    totals = lax.fori_loop(0, i + 1, weigh, (zero, zero))
    totals = [jnp.sum(total, axis=0, keepdims=True) for total in totals]
    scales = [1.0 / total for total in totals]
    for n in range(2):
        log_sums_ref[n : n + 1, own] = top[n] + jnp.log(totals[n])

    def push(j, carry):
        rows = rows_of(j, block)
        new = []
        for n, head in enumerate(HEADS_HERE):
            probs = (score_ref[n, j] * scales[n]).astype(jnp.bfloat16)
            new.append(carry[n] + matmul(vt_ref[head, rows], probs))
        return tuple(new)

    zero = jnp.zeros((HEAD_DIM, block), jnp.float32)
    out = lax.fori_loop(0, i + 1, push, (zero, zero))
    attended_ref[own, :] = jnp.concatenate(out, axis=0).T.astype(jnp.bfloat16)


def attention(qkv, block=512, after=()):
    rows, width = qkv.shape[0], 2 * HEAD_DIM
    blocks = rows // block
    return call(
        partial(attention_kernel, block),
        "attention",
        (blocks,),
        [whole(rows, 3 * width)],
        [whole(rows, width), whole(8, rows)],
        [struct((rows, width), jnp.bfloat16), struct((8, rows), jnp.float32)],
        [pltpu.VMEM((width, rows), jnp.bfloat16)] * 2
        + [pltpu.VMEM((2, blocks, block, block), jnp.float32)],
        flops=10 * 10**9,
        after=after,
    )(qkv)


def attention_back_kernel(
    blocks,
    block,
    qkv_ref,
    grad_ref,
    log_sums_ref,
    cosine_ref,
    sine_ref,
    pre_grad_ref,
    sums_ref,
    qt_ref,
    kt_ref,
    gt_ref,
    prob_ref,
    slope_ref,
    k_total,
    v_total,
):
    i = pl.program_id(0)
    width = 2 * HEAD_DIM
    factor = 1.0 / math.sqrt(HEAD_DIM)
    chunk = 256

    @pl.when(i == 0)
    def _():
        turned_into(qt_ref, qkv_ref, slice(0, width))
        turned_into(kt_ref, qkv_ref, slice(width, 2 * width))
        turned_into(gt_ref, grad_ref, slice(0, width))
        k_total[...] = jnp.zeros_like(k_total)
        v_total[...] = jnp.zeros_like(v_total)
        sums_ref[...] = jnp.zeros_like(sums_ref)

    own = rows_of(i, block)
    causal = causal_block(block)
    log_sums = [log_sums_ref[n : n + 1, own] for n in range(2)]

    def weigh(j, carry, diagonal):
        rows = rows_of(j, block)
        new = []
        for n, head in enumerate(HEADS_HERE):
            start = width + n * HEAD_DIM
            scores = matmul(qkv_ref[rows, start : start + HEAD_DIM], qt_ref[head, own])
            probs = jnp.exp(scores - log_sums[n])
            if diagonal:
                probs = jnp.where(causal, probs, 0.0)
            start += width
            slope = matmul(qkv_ref[rows, start : start + HEAD_DIM], gt_ref[head, own])
            prob_ref[n, j] = probs
            slope_ref[n, j] = slope
            new.append(carry[n] + fold_rows(probs * slope, jnp.sum))
        return tuple(new)

    zero = jnp.zeros((8, block), jnp.float32)
    dots = lax.fori_loop(0, i, lambda j, c: weigh(j, c, False), (zero, zero))
    dots = weigh(i, dots, True)
    dots = [jnp.sum(dot, axis=0, keepdims=True) for dot in dots]

    def push(j, carry):
        rows = rows_of(j, block)
        new = []
        for n, head in enumerate(HEADS_HERE):
            probs = prob_ref[n, j]
            score_grad = (probs * (slope_ref[n, j] - dots[n])).astype(jnp.bfloat16)
            k_total[rows, head] += matmul(score_grad, qkv_ref[own, head])
            v_total[rows, head] += matmul(probs.astype(jnp.bfloat16), grad_ref[own, head])
            new.append(carry[n] + matmul(kt_ref[head, rows], score_grad))
        return tuple(new)

    zero = jnp.zeros((HEAD_DIM, block), jnp.float32)
    q_grad = lax.fori_loop(0, i + 1, push, (zero, zero))
    q_grad = jnp.concatenate(q_grad, axis=0).T * factor
    q_pre = turn(q_grad, cosine_ref[own, :], -sine_ref[own, :]).astype(jnp.bfloat16)
    pre_grad_ref[own, :width] = q_pre
    sums_ref[:, :width] += jnp.sum(q_pre.astype(jnp.float32), axis=0, keepdims=True)

    @pl.when(i == blocks - 1)
    def _():
        def finish(b, carry):
            rows = rows_of(b, chunk)
            k_pre = turn(k_total[rows, :], cosine_ref[rows, :], -sine_ref[rows, :])
            k_pre = k_pre.astype(jnp.bfloat16)
            v_pre = v_total[rows, :].astype(jnp.bfloat16)
            pre_grad_ref[rows, width : 2 * width] = k_pre
            pre_grad_ref[rows, 2 * width :] = v_pre
            both = jnp.concatenate([k_pre, v_pre], axis=1).astype(jnp.float32)
            return carry + jnp.sum(both, axis=0, keepdims=True)

        sums_ref[:, width:] = lax.fori_loop(
            0, qkv_ref.shape[0] // chunk, finish, jnp.zeros((1, 2 * width), jnp.float32)
        )


def attention_back(qkv, out_grad, log_sums, block=512, after=()):
    rows, width = qkv.shape[0], 2 * HEAD_DIM
    blocks = rows // block
    cosine, sine = rotary_tables(rows)
    return call(
        partial(attention_back_kernel, blocks, block),
        "attention_back",
        (blocks,),
        [whole(rows, 3 * width), whole(rows, width), whole(8, rows)]
        + [whole(rows, width), whole(rows, width)],
        [whole(rows, 3 * width), whole(1, 3 * width)],
        [struct((rows, 3 * width), jnp.bfloat16), struct((1, 3 * width), jnp.float32)],
        [pltpu.VMEM((width, rows), jnp.bfloat16)] * 3
        + [pltpu.VMEM((2, blocks, block, block), jnp.float32)] * 2
        + [pltpu.VMEM((rows, width), jnp.float32)] * 2,
        flops=20 * 10**9,
        after=after,
    )(qkv, out_grad, log_sums, jnp.asarray(cosine), jnp.asarray(sine))


def weight_grad_kernel(riders, *refs):
    out_ref, refs = refs[-1], refs[:-1]
    if riders:
        height = out_ref.shape[1] - refs[0].shape[1]
        out_ref[:, height:, :] = refs[0][...]
        refs = refs[1:]
    cols = out_ref.shape[2]
    start = 0
    for left_ref, right_ref in zip(refs[::2], refs[1::2]):
        if len(right_ref.shape) == 5:
            size = right_ref.shape[3]
            part = 0.0
            for b in range(4):
                rows = slice(b * size, (b + 1) * size)
                part = part + contract_rows(left_ref[rows, :], right_ref[b % 2, 0, b // 2])
        else:
            part = contract_rows(left_ref[...], right_ref[...])
        part = part.astype(jnp.bfloat16)
        stop = start + part.shape[0]
        for n in range(out_ref.shape[0]):
            out_ref[n, start:stop, :] = part[:, n * cols : (n + 1) * cols]
        start = stop


def weight_grad(pairs, parts, rider=None, after=()):
    cols = D // parts
    per = parts // 4
    rows = pairs[0][0].shape[0]
    height = sum(left.shape[1] for left, _ in pairs)
    in_specs, operands = [], []
    if rider is not None:
        in_specs.append(pl.BlockSpec((per,) + rider.shape[1:], lambda i: (i, 0, 0)))
        operands.append(rider)
        height += rider.shape[1]
    for left, right in pairs:
        in_specs.append(whole(*left.shape))
        if right.ndim == 5:
            in_specs.append(
                pl.BlockSpec((2, 1, 2, right.shape[3], D // 4), lambda i: (0, i, 0, 0, 0))
            )
        else:
            in_specs.append(pl.BlockSpec((rows, D // 4), lambda i: (0, i)))
        operands += [left, right]
    return call(
        partial(weight_grad_kernel, rider is not None),
        "weight_grad",
        (4,),
        in_specs,
        pl.BlockSpec((per, height, cols), lambda i: (i, 0, 0)),
        struct((parts, height, cols), jnp.bfloat16),
        flops=4 * rows * height * D,
        after=after,
    )(*operands)


def partial_sum_kernel(sides, axes, index_ref, *refs):
    lefts, refs = refs[: 2 * sides], refs[2 * sides :]
    weights, others, outs = refs[:sides], refs[sides : 2 * sides], refs[2 * sides :]
    rows, width = outs[0].shape[-2:]
    own_m, own_h, core = index_ref[0], index_ref[1], index_ref[2]
    here = lax.rem(pl.program_id(0), 2) == own_h
    for n_m, m in enumerate((own_m, 1 - own_m)):
        out = 0.0
        for n in range(sides):
            weight = weight_rows_of(weights[n], (2 * m + core) * width, width)
            out = out + contract_cols(lefts[n][...], weight)
            other = others[n][m].reshape(width, weight.shape[1])
            out = out + contract_cols(lefts[sides + n][...], other)
        out = out.astype(jnp.bfloat16)
        for half, axis in enumerate(axes):
            part = out[half * rows : (half + 1) * rows]
            if axis == "m":
                outs[2 * half + n_m][0] = part
                continue
            for n_h, mine in enumerate((here, jnp.logical_not(here))):

                @pl.when(mine)
                def _(out_ref=outs[2 * half + n_h], m=m, part=part):
                    out_ref[0, m] = part


def partial_sum(sides, row_count, width, name, axes, after=()):
    total = sides[0][0].shape[0]
    rows = row_count // len(axes)
    blocks = total // row_count
    lefts = [side[0] for side in sides] + [side[1] for side in sides]
    weights = [side[2] for side in sides]
    others = [side[3] for side in sides]
    depth = sum(left.shape[1] for left in lefts)
    specs, shapes = [], []
    for axis in axes:
        if axis == "m":
            specs += [pl.BlockSpec((1, rows, width), lambda i: (i, 0, 0))] * 2
            shapes += [struct((blocks, rows, width), jnp.bfloat16)] * 2
        else:
            specs += [pl.BlockSpec((1, 2, rows, width), lambda i: (i // 2, 0, 0, 0))] * 2
            shapes += [struct((blocks // 2, 2, rows, width), jnp.bfloat16)] * 2
    index = jnp.stack([lax.axis_index(axis) for axis in "mhc"]).astype(jnp.int32)
    return call(
        partial(partial_sum_kernel, len(sides), axes),
        name,
        (blocks,),
        [SCALARS]
        + [band(row_count, left.shape[1]) for left in lefts]
        + [weight.spec for weight in weights]
        + [other.spec for other in others],
        specs,
        shapes,
        flops=2 * total * depth * D,
        after=after,
    )(index, *lefts, *[weight.array for weight in weights], *[other.array for other in others])


def switch_specs(count, block):
    zeros = (0,) * (len(block) - 1)
    return [
        pl.BlockSpec(block, lambda k, j, p: (j + k * (count - 1 - j),) + zeros),
        pl.BlockSpec(block, lambda k, j, p: (j * k,) + zeros),
    ]


def prefetch_call(kernel, name, index, grid, in_specs, out_specs, out_shape, after=()):
    skipped = len(after)

    def ordered(index_ref, *refs):
        kernel(index_ref, *refs[skipped:])

    run = pl.pallas_call(
        ordered,
        grid_spec=pltpu.PrefetchScalarGridSpec(
            num_scalar_prefetch=1,
            grid=grid,
            in_specs=[ANY] * skipped + list(in_specs),
            out_specs=out_specs,
        ),
        out_shape=out_shape,
        compiler_params=pltpu.CompilerParams(vmem_limit_bytes=VMEM_LIMIT),
        cost_estimate=pl.CostEstimate(flops=0, bytes_accessed=0, transcendentals=0),
        name=name,
    )
    return lambda *operands: run(index.astype(jnp.int32).reshape(1), *after, *operands)


def column_specs(shards, turned, block):
    specs, width = [], 0
    for flip, shard in zip(turned, shards):
        height, cols = shard.shape
        if flip:
            specs.append(pl.BlockSpec((height // 4, cols), lambda *at: (block(*at), 0)))
            rows, width = cols, width + height // 4
        else:
            specs.append(pl.BlockSpec((height, cols // 4), lambda *at: (0, block(*at))))
            rows, width = height, width + cols // 4
    return specs, rows, width


def write_columns(turned, refs, store):
    start = 0
    for flip, ref in zip(turned, refs):
        part = ref[...].T if flip else ref[...]
        store(slice(start, start + part.shape[1]), part)
        start += part.shape[1]


def pack_kernel(turned, rows, riders, *refs):
    out_ref, refs = refs[-1], refs[:-1]
    if riders:
        rider, refs = refs[0][...], refs[1:]

    def store(cols, part):
        for n in range(out_ref.shape[0]):
            out_ref[n, 0, :rows, cols] = part

    write_columns(turned, refs, store)
    if riders:
        for n in range(out_ref.shape[0]):
            out_ref[n, 0, rows:, :] = rider


def packed(shards, turned, rider=None):
    wide = lax.axis_size(WIDE)
    specs, rows, width = column_specs(shards, turned, lambda i: i)
    height = rows
    if rider is not None:
        specs = [whole(*rider.shape)] + specs
        shards = [rider] + shards
        height += rider.shape[0]
    blocks = call(
        partial(pack_kernel, turned, rows, rider is not None),
        "pack",
        (4,),
        specs,
        pl.BlockSpec((wide // 4, 1, height, width), lambda i: (0, i, 0, 0)),
        struct((wide // 4, 4, height, width), jnp.bfloat16),
    )(*shards)
    return blocks.reshape(wide, height, width)


def exchanged(blocks, after=()):
    blocks = lax.optimization_barrier((blocks, *after))[0]
    return lax.all_to_all(blocks, WIDE, 0, 0)


def sides_kernel(turned, index_ref, *refs):
    for out_ref, blocks in zip(refs[-2:], (refs[:-2][::2], refs[:-2][1::2])):

        def store(cols, part, out_ref=out_ref):
            out_ref[0, :, cols] = part

        write_columns(turned, blocks, store)


def packed_sides(shards, turned):
    specs, operands, width = [], [], 0
    for flip, shard in zip(turned, shards):
        height, cols = shard.shape
        if flip:
            rows, width = cols, width + height // 4
            shape, at = (height // 4, cols), lambda block: (block, 0)
        else:
            rows, width = height, width + cols // 4
            shape, at = (height, cols // 4), lambda block: (0, block)
        specs.append(pl.BlockSpec(shape, lambda j, p, at=at: at(2 * j + p[0])))
        specs.append(pl.BlockSpec(shape, lambda j, p, at=at: at(2 * j + 1 - p[0])))
        operands += [shard, shard]
    return prefetch_call(
        partial(sides_kernel, turned),
        "pack",
        lax.axis_index("h"),
        (2,),
        specs,
        [pl.BlockSpec((1, rows, width), lambda j, p: (j, 0, 0))] * 2,
        [struct((2, rows, width), jnp.bfloat16)] * 2,
    )(*operands)


def spread_kernel(index_ref, mine_ref, other_ref, out_ref):
    for n in range(out_ref.shape[0]):
        out_ref[n, 0, index_ref[0]] = mine_ref[0]
        out_ref[n, 0, 1 - index_ref[0]] = other_ref[0]


def spread_sides(sides, after=()):
    mine, send = sides
    sequences = lax.axis_size("s")
    _, rows, width = mine.shape
    spec = pl.BlockSpec((1, rows, width), lambda j, p: (j, 0, 0))
    blocks = prefetch_call(
        spread_kernel,
        "spread",
        lax.axis_index("h"),
        (2,),
        [spec, spec],
        pl.BlockSpec((sequences, 1, 2, rows, width), lambda j, p: (0, j, 0, 0, 0)),
        struct((sequences, 2, 2, rows, width), jnp.bfloat16),
        after=after,
    )(mine, shifted(send, "h", 1))
    return blocks.reshape(2 * sequences, 2 * rows, width)


def exchanged_along_line(blocks):
    count, rows, width = blocks.shape
    return lax.all_to_all(blocks, LINE, 0, 0).reshape(2 * count, rows // 2, width)


def unpack_kernel(turned, arrived_ref, *outs):
    total = arrived_ref[0, 0].astype(jnp.float32)
    for n in range(1, arrived_ref.shape[0]):
        total = total + arrived_ref[n, 0].astype(jnp.float32)
    start = 0
    for flip, out_ref in zip(turned, outs):
        height = out_ref.shape[0] if flip else out_ref.shape[1]
        part = total[start : start + height]
        out_ref[...] = part if flip else part.T
        start += height


def scatter_columns(grad, heights, turned, after=()):
    sequences = lax.axis_size("s")
    _, height, rows = grad.shape
    arrived = lax.all_to_all(grad, WIDE, 0, 0)
    riders = arrived[:, sum(heights) :]
    arrived = arrived.reshape(sequences, 4, height, rows)
    height = sum(heights)
    specs, shapes = [], []
    for flip, part in zip(turned, heights):
        if flip:
            specs.append(pl.BlockSpec((part, rows), lambda i: (i, 0)))
            shapes.append(struct((4 * part, rows), jnp.float32))
        else:
            specs.append(pl.BlockSpec((rows, part), lambda i: (0, i)))
            shapes.append(struct((rows, 4 * part), jnp.float32))
    shards = call(
        partial(unpack_kernel, turned),
        "unpack",
        (4,),
        [pl.BlockSpec((sequences, 1, height, rows), lambda i: (0, i, 0, 0))],
        specs,
        shapes,
        after=after,
    )(arrived)
    return shards, riders


def fold_kernel(index_ref, mine_keep, mine_send, arrived_keep, arrived_send, keep_ref, send_ref):
    keep_ref[...] = mine_keep[...] + arrived_keep[...]
    send_ref[...] = mine_send[...] + arrived_send[...]


def folded(mine, arrived, axes, axis, after=()):
    position = axes.index(axis)
    high, low = 2**position, 2 ** (len(axes) - 1 - position)
    rows, cols = mine.shape[-2:]
    shape = (high, 2, low * rows, cols)
    steps = 2 if low > 1 else 1
    block = low * rows // steps
    halves = [
        pl.BlockSpec((high, None, block, cols), lambda j, p: (0, p[0], j, 0)),
        pl.BlockSpec((high, None, block, cols), lambda j, p: (0, 1 - p[0], j, 0)),
    ]
    out = pl.BlockSpec((high, block, cols), lambda j, p: (0, j, 0))
    mine, arrived = mine.reshape(shape), arrived.reshape(shape)
    keep, send = prefetch_call(
        fold_kernel,
        "fold",
        lax.axis_index(axis),
        (steps,),
        halves * 2,
        [out, out],
        [struct((high, low * rows, cols), jnp.bfloat16)] * 2,
        after=after,
    )(mine, mine, arrived, arrived)
    return [part.reshape(high * low, rows, cols) for part in (keep, send)]


def join_kernel(index_ref, mine_ref, other_ref, out_ref):
    out_ref[index_ref[0]] = mine_ref[...]
    out_ref[1 - index_ref[0]] = other_ref[...]


def joined(mine, axis, after=()):
    other = shifted(mine, axis, 1)
    rows, cols = mine.size // mine.shape[-1] // 2, mine.shape[-1]
    spec = pl.BlockSpec((rows, cols), lambda j, p: (j, 0))
    out = prefetch_call(
        join_kernel,
        "join",
        lax.axis_index(axis),
        (2,),
        [spec, spec],
        pl.BlockSpec((2, rows, cols), lambda j, p: (0, j, 0)),
        struct((2, 2 * rows, cols), mine.dtype),
        after=after,
    )(mine.reshape(2 * rows, cols), other.reshape(2 * rows, cols))
    return out.reshape((2,) + mine.shape)


def finish_kernel(tokens_ref, *refs):
    bias_ref, out_ref = refs[-2:]
    parts = len(refs) // 2 - 1
    rows = refs[0].shape[0]
    for n, (keep_ref, arrived_ref) in enumerate(zip(refs[:parts], refs[parts : 2 * parts])):
        at = slice(n * rows, (n + 1) * rows)
        total = tokens_ref[at, :].astype(jnp.float32) + keep_ref[...].astype(jnp.float32)
        total = total + arrived_ref[...].astype(jnp.float32) + bias_ref[...]
        out_ref[at, :] = total.astype(jnp.bfloat16)


def finished(tokens, keep, arrived, bias, after=()):
    operands = [tokens, *keep, *arrived, bias]
    return call(
        finish_kernel,
        "finish",
        (1,),
        [whole(*operand.shape) for operand in operands],
        whole(*tokens.shape),
        struct(tokens.shape, tokens.dtype),
        after=after,
    )(*operands)


def gather_narrow(value):
    for axis in ("c", "m"):
        other = shifted(value, axis, 1)
        value = jnp.stack(in_order(value, other, lax.axis_index(axis)))
    return value.reshape((4,) + value.shape[2:])


def summed(value, axis):
    total = value
    for step in range(1, lax.axis_size(axis)):
        total = total + shifted(value, axis, step)
    return total


def body(
    tokens,
    cotangent,
    ln_gain,
    ln_shift,
    w_query,
    b_query,
    w_key,
    b_key,
    w_value,
    b_value,
    w_dense,
    b_dense,
    w_fc1,
    b_fc1,
    w_fc2,
    b_fc2,
):
    row_count, feature_count = tokens.shape
    own_g, own_h = lax.axis_index("g"), lax.axis_index("h")
    own_n = lax.axis_index(NARROW)
    quarter = 2 * own_g + own_h
    wide = lax.axis_size(WIDE)
    weight_rows = w_fc1.shape[0]
    lanes = w_query.shape[1] // 4

    vectors = (ln_gain, ln_shift, b_query, b_key, b_value, b_dense, b_fc2, b_fc1)
    lengths = [vector.shape[0] for vector in vectors]
    hidden = w_fc1.shape[1] // 4
    rider = jnp.concatenate(vectors)
    rider = jnp.pad(rider, (0, 16 * hidden - rider.shape[0])).reshape(16, hidden)

    tokens_full = lax.all_gather(tokens, CUBE, axis=0, tiled=False)
    tokens_full = tokens_full.reshape(4, 4, row_count, feature_count)
    up_blocks = packed([w_fc1], [False], rider)
    head_sides = packed_sides(
        [w_query, w_key, w_value, w_dense], [False, False, False, True]
    )
    down_sides = packed_sides([w_fc2], [True])
    cot = joined(cotangent, "g", after=[up_blocks, head_sides[0], down_sides[0]])
    arrived = exchanged(up_blocks, after=[cot])
    cot = lax.all_gather(cot, ("h", "m", "c"), axis=0, tiled=False)
    cot = cot.reshape(2, 4, 2, row_count, feature_count)
    head_blocks = spread_sides(head_sides, after=[arrived])
    head_arrived = exchanged_along_line(head_blocks)
    up_weight = Weight(arrived, weight_rows, 0, hidden)
    qkv_weight = Weight(head_arrived, weight_rows, 0, 3 * lanes)
    dense_weight = Weight(head_arrived, weight_rows, 3 * lanes, lanes)

    def from_other_core(array):
        split = array[:, :weight_rows].reshape(2, 2, wide // 4, weight_rows, -1)
        return shifted(pick(split, 1 - lax.axis_index("c"), 1), "c", 1)

    up_other = Weight(from_other_core(arrived), weight_rows, 0, hidden)
    head_other = from_other_core(head_arrived)
    qkv_other = Weight(head_other, weight_rows, 0, 3 * lanes)
    dense_other = Weight(head_other, weight_rows, 3 * lanes, lanes)

    here = arrived[:, weight_rows:].reshape(wide, 16 * hidden)
    local, start = [], 0
    for length in lengths:
        local.append(here[:, start : start + length].astype(jnp.float32).reshape(-1))
        start += length
    shared = gather_narrow(here[:, : 2 * lengths[0]].astype(jnp.float32))
    gain = shared[:, :, : lengths[0]].reshape(1, D)
    shift = shared[:, :, lengths[0] :].reshape(1, D)

    def quarter_of(vector):
        return pick(vector.reshape(4, -1), quarter)

    qkv_bias = jnp.concatenate([quarter_of(vector) for vector in local[2:5]]).reshape(1, -1)
    up_bias = quarter_of(local[7]).reshape(1, -1)
    own_gain, out_bias = local[0], local[5] + local[6]

    normed, stats, up_low, up_slope = norm_up(
        tokens_full, gain, shift, up_bias, up_weight, after=[up_other.array]
    )
    down_blocks = spread_sides(down_sides, after=[normed])
    down_arrived = exchanged_along_line(down_blocks)
    down_weight = Weight(down_arrived, weight_rows, 0, hidden)
    down_other = Weight(from_other_core(down_arrived), weight_rows, 0, hidden)
    qkv = project_heads(normed, qkv_bias, qkv_weight)
    attended, log_sums = attention(qkv)
    grad_down = weight_grad([(up_low, cot)], wide, after=[attended])
    attended_grad, up_grad, up_sums = back_through(
        cot, up_slope, dense_weight, down_weight, after=[grad_down]
    )
    qkv_grad, qkv_sums = attention_back(qkv, attended_grad, log_sums)
    qkv_grad_other = shifted(qkv_grad, "c", 1)

    grad_up = weight_grad([(up_grad, normed)], wide, after=[qkv_grad])
    normed_grad = partial_sum(
        [
            (qkv_grad, qkv_grad_other, qkv_weight, qkv_other),
            (up_grad, shifted(up_grad, "c", 1), up_weight, up_other),
        ],
        row_count,
        feature_count,
        "normed_gradient",
        "mh",
        after=[grad_up],
    )

    branch = partial_sum(
        [
            (attended, shifted(attended, "c", 1), dense_weight, dense_other),
            (up_low, shifted(up_low, "c", 1), down_weight, down_other),
        ],
        row_count,
        feature_count,
        "branch_sum",
        "mm",
        after=normed_grad[:1],
    )
    def spread(vector):
        placed = jnp.zeros((4, vector.shape[0]), jnp.float32)
        placed = lax.dynamic_update_index_in_dim(placed, vector, quarter, 0)
        return placed.reshape(wide, -1)

    terms = [
        spread(qkv_sums[0, :lanes]),
        spread(qkv_sums[0, lanes : 2 * lanes]),
        spread(qkv_sums[0, 2 * lanes :]),
        jnp.sum(cotangent.astype(jnp.float32), axis=0).reshape(wide, -1),
        spread(up_sums[0]),
    ]
    rider = jnp.concatenate(terms, axis=1).astype(jnp.bfloat16)
    early_count = rider.shape[1]
    rider = jnp.pad(rider, ((0, 0), (0, 16 * weight_rows - early_count)))
    grad_heads = weight_grad(
        [(qkv_grad, normed), (attended, cot)],
        wide,
        rider.reshape(wide, 16, weight_rows),
        after=branch[:1],
    )
    first = [normed_grad[:2], normed_grad[2:]]
    second = [branch[:2], branch[2:]]

    def fold(part, arrived, axes, after):
        return folded(part[0], shifted(part[1], arrived, 1), axes, axes[-1], after=[after])

    first[0] = fold(first[0], "m", "gh", grad_heads)
    (grad_down,), _ = scatter_columns(grad_down, [hidden], [True], after=first[0][:1])
    first[1] = fold(first[1], "h", "gm", grad_down)
    second[0] = fold(second[0], "m", "gh", first[1][0])
    first[0] = fold(first[0], "h", "g", second[0][0])
    first[1] = fold(first[1], "m", "g", first[0][0])
    (grad_up,), _ = scatter_columns(grad_up, [hidden], [False], after=first[1][:1])

    def last(keep, send):
        arrived = lax.optimization_barrier((shifted(send[0], "g", 1), grad_up))[0]
        return keep[0].astype(jnp.float32) + arrived.astype(jnp.float32)

    local_x = tokens.astype(jnp.float32)
    standard_grad = jnp.concatenate([last(*part) for part in first], axis=0)
    own_stats = pick(stats.reshape(4, row_count, 128), quarter)
    row_mean, inverse_std = own_stats[:, :1], own_stats[:, 64:65]
    standard = (local_x - row_mean) * inverse_std
    scaled_grad = standard_grad * own_gain
    row_sums = jnp.stack([jnp.sum(scaled_grad, axis=1), jnp.sum(scaled_grad * standard, axis=1)])
    for axis in ("c", "m"):
        row_sums = row_sums + shifted(row_sums, axis, 1)
    input_grad = (
        scaled_grad - row_sums[0][:, None] / D - standard * (row_sums[1][:, None] / D)
    ) * inverse_std + cotangent.astype(jnp.float32)

    own_terms = [jnp.sum(standard_grad * standard, axis=0), jnp.sum(standard_grad, axis=0)]
    own_terms = [term.reshape(wide, -1) for term in own_terms]
    late = summed(jnp.concatenate(own_terms, axis=1), "h")
    late = summed(summed(late, "g"), "s")
    second[1] = fold(second[1], "m", "gh", standard_grad)
    second[0] = fold(second[0], "h", "g", second[1][0])
    second[1] = fold(second[1], "h", "g", second[0][0])
    (grad_query, grad_key, grad_value, grad_dense), riders = scatter_columns(
        grad_heads, [lanes] * 4, [False, False, False, True], after=second[1][:1]
    )
    early = jnp.sum(riders.astype(jnp.float32), axis=0).reshape(-1)[:early_count]
    output = finished(
        tokens,
        [part[0][0] for part in second],
        [shifted(part[1][0], "g", 1) for part in second],
        out_bias.reshape(1, -1),
        after=[grad_dense],
    )
    terms = own_terms + terms
    vector_sums = jnp.concatenate([pick(late, lax.axis_index(WIDE)), early])
    vector_grads, start = [], 0
    for term in terms:
        vector_grads.append(vector_sums[start : start + term.shape[1]])
        start += term.shape[1]
    return (
        output,
        input_grad,
        vector_grads[0],
        vector_grads[1],
        grad_query,
        vector_grads[2],
        grad_key,
        vector_grads[3],
        grad_value,
        vector_grads[4],
        grad_dense,
        vector_grads[5],
        grad_up,
        vector_grads[6],
        grad_down,
        vector_grads[5],
    )


def solution(mesh):
    wide = mesh.shape["wide"]
    inner = Mesh(mesh.devices.reshape(wide // 4, 2, 2, 2, 2), ("s", "g", "h", "m", "c"))
    acts = P(WIDE, NARROW)
    vector = P(NARROW + WIDE)
    by_rows = P(WIDE, NARROW)
    by_cols = P(NARROW, WIDE)
    specs = (
        (acts, acts, vector, vector)
        + (by_rows, vector) * 3
        + (by_cols, vector, by_rows, vector, by_cols, vector)
    )
    return jax.shard_map(body, mesh=inner, in_specs=specs, out_specs=specs, check_vma=False)
```

```python
from functools import partial
import math

import jax
import jax.numpy as jnp
import numpy as np
from jax import lax
from jax.experimental import pallas as pl
from jax.experimental.pallas import tpu as pltpu
from jax.sharding import Mesh, PartitionSpec as P

D = 2048
HEAD_DIM = 64
ROT = 32
EPSILON = 1e-05
VMEM_LIMIT = 56 * 2**20
COST = 1

WIDE = ("s", "g", "h")
LINE = ("s", "g")
LINE = ("s", "g")
NARROW = ("m", "c")
CUBE = ("g", "h", "m", "c")


def matmul(left_side, right_side):
    return jnp.dot(left_side, right_side, preferred_element_type=jnp.float32)


def contract_rows(left_side, right_side):
    return lax.dot_general(
        left_side, right_side, (((0,), (0,)), ((), ())), preferred_element_type=jnp.float32
    )


def contract_cols(left_side, right_side):
    return lax.dot_general(
        left_side, right_side, (((1,), (1,)), ((), ())), preferred_element_type=jnp.float32
    )


def pick(blocks, index, axis=0):
    return lax.dynamic_index_in_dim(blocks, index, axis, keepdims=False)


def shifted(value, axis, step):
    count = lax.axis_size(axis)
    return lax.ppermute(value, axis, [(source, (source + step) % count) for source in range(count)])


def in_order(mine, other, index):
    return (jnp.where(index == 0, mine, other), jnp.where(index == 0, other, mine))


def call(
    kernel, name, grid, in_specs, out_specs, out_shape, scratch=(), flops=0, after=()
):
    skipped = len(after)

    def ordered(*refs):
        kernel(*refs[skipped:])

    run = pl.pallas_call(
        ordered,
        grid=grid,
        in_specs=[ANY] * skipped + list(in_specs),
        out_specs=out_specs,
        out_shape=out_shape,
        scratch_shapes=list(scratch),
        compiler_params=pltpu.CompilerParams(vmem_limit_bytes=VMEM_LIMIT),
        cost_estimate=pl.CostEstimate(flops=COST * flops // 1000, bytes_accessed=0, transcendentals=0),
        name=name,
    )
    return lambda *operands: run(*after, *operands)


def whole(*shape):
    return pl.BlockSpec(shape, lambda i: (0,) * len(shape))


def band(rows, cols):
    return pl.BlockSpec((rows, cols), lambda i: (i, 0))


ANY = pl.BlockSpec(memory_space=pl.ANY)
SCALARS = pl.BlockSpec(memory_space=pltpu.SMEM)


def struct(shape, dtype):
    return jax.ShapeDtypeStruct(shape, dtype)


def rotary_tables(rows):
    lane = np.arange(2 * HEAD_DIM) % HEAD_DIM
    pair = (lane % (ROT // 2)).astype(np.float32)
    inverse = np.exp(pair * np.float32(-2.0 * math.log(10000.0) / ROT)).astype(np.float32)
    phase = np.arange(rows, dtype=np.float32)[:, None] * inverse[None, :]
    turned = (lane < ROT)[None, :]
    sign = np.where(lane < ROT // 2, -1.0, 1.0)[None, :]
    cosine = np.where(turned, np.cos(phase), 1.0).astype(np.float32)
    sine = np.where(turned, np.sin(phase) * sign, 0.0).astype(np.float32)
    return (cosine, sine)


def turn(values, cosine, sine):
    lane = lax.broadcasted_iota(jnp.int32, values.shape, 1) % HEAD_DIM
    width = values.shape[1]
    half = ROT // 2
    partner = jnp.where(
        lane < half, pltpu.roll(values, width - half, 1), pltpu.roll(values, half, 1)
    )
    return values * cosine + partner * sine


def norm_up_kernel(
    tokens_ref, gain_ref, shift_ref, bias_ref, weight_ref, normed_ref, stats_ref, low_ref, slope_ref
):
    parts = [tokens_ref[0, j].astype(jnp.float32) for j in range(tokens_ref.shape[1])]
    rows, width = parts[0].shape
    total = sum(jnp.sum(part, axis=1, keepdims=True) for part in parts)
    squares = sum(jnp.sum(part * part, axis=1, keepdims=True) for part in parts)
    mean = total / D
    inverse_std = lax.rsqrt(squares / D - mean * mean + EPSILON)
    up_input = bias_ref[...]
    for j, part in enumerate(parts):
        cols = slice(j * width, (j + 1) * width)
        standard = (part - mean) * inverse_std
        normed = (standard * gain_ref[:, cols] + shift_ref[:, cols]).astype(jnp.bfloat16)
        normed_ref[:, cols] = normed
        up_input = up_input + matmul(normed, weight_rows_of(weight_ref, j * width, width))
    stats_ref[...] = jnp.concatenate(
        [jnp.broadcast_to(mean, (rows, 64)), jnp.broadcast_to(inverse_std, (rows, 64))], axis=1
    )
    root = math.sqrt(2.0 / math.pi)
    square = up_input * up_input
    bend = jnp.tanh(root * (up_input + 0.044715 * square * up_input))
    half = 0.5 * (1.0 + bend)
    low_ref[...] = (up_input * half).astype(jnp.bfloat16)
    slope_ref[...] = half + 0.5 * up_input * (1.0 - bend * bend) * (
        root * (1.0 + 3 * 0.044715 * square)
    )


class Weight:
    def __init__(self, array, rows, start, width):
        self.array, self.rows, self.width = array, rows, width
        self.spec = pl.BlockSpec(
            array.shape[:-2] + (rows, width),
            lambda *_: (0,) * (len(array.shape) - 1) + (start // width,),
        )


def weight_rows_of(weight_ref, start, count):
    _, rows, width = weight_ref.shape
    return weight_ref[pl.ds(start // rows, count // rows)].reshape(count, width)


def norm_up(blocks, gain, shift, bias, weight, rows=256, after=()):
    row_blocks, col_blocks, row_count, width = blocks.shape
    total, hidden = row_blocks * row_count, bias.shape[1]
    per = row_count // rows
    spec = pl.BlockSpec((1, col_blocks, rows, width), lambda i: (i // per, 0, i % per, 0))
    return call(
        norm_up_kernel,
        "norm_up",
        (total // rows,),
        [spec]
        + [whole(1, D), whole(1, D), whole(1, hidden), weight.spec],
        [band(rows, D), band(rows, 128), band(rows, hidden), band(rows, hidden)],
        [
            struct((total, D), jnp.bfloat16),
            struct((total, 128), jnp.float32),
            struct((total, hidden), jnp.bfloat16),
            struct((total, hidden), jnp.float32),
        ],
        flops=6 * total * D * hidden,
        after=after,
    )(blocks, gain, shift, bias, weight.array)


def heads_kernel(normed_ref, bias_ref, cosine_ref, sine_ref, weight_ref, heads_ref):
    pre = matmul(normed_ref[...], weight_rows_of(weight_ref, 0, D)) + bias_ref[...]
    lanes = 2 * HEAD_DIM
    cosine, sine = cosine_ref[...], sine_ref[...]
    factor = 1.0 / math.sqrt(HEAD_DIM)
    heads_ref[:, :lanes] = (turn(pre[:, :lanes], cosine, sine) * factor).astype(jnp.bfloat16)
    heads_ref[:, lanes : 2 * lanes] = turn(pre[:, lanes : 2 * lanes], cosine, sine).astype(
        jnp.bfloat16
    )
    heads_ref[:, 2 * lanes :] = pre[:, 2 * lanes :].astype(jnp.bfloat16)


def project_heads(normed, bias, weight, rows=512, after=()):
    total, width = normed.shape[0], bias.shape[1]
    cosine, sine = rotary_tables(total)
    lanes = 2 * HEAD_DIM
    return call(
        heads_kernel,
        "project_heads",
        (total // rows,),
        [band(rows, D), whole(1, width), band(rows, lanes), band(rows, lanes)]
        + [weight.spec],
        band(rows, width),
        struct((total, width), jnp.bfloat16),
        flops=4 * total * D * width,
        after=after,
    )(normed, bias, jnp.asarray(cosine), jnp.asarray(sine), weight.array)


def cot_spec(cot, rows):
    row_count, width = cot.shape[-2:]
    per = row_count // rows
    return pl.BlockSpec(
        (1, 4, 1, rows, width), lambda i: (i // per % 2, 0, i // per // 2, i % per, 0)
    )


def back_kernel(
    cot_ref, slope_ref, dense_ref, down_ref, attended_ref, up_ref, sums_ref
):
    @pl.when(pl.program_id(0) == 0)
    def _():
        sums_ref[...] = jnp.zeros_like(sums_ref)

    width = cot_ref.shape[4]
    attended, up = 0.0, 0.0
    for j in range(4):
        part = cot_ref[0, j, 0]
        attended = attended + matmul(part, weight_rows_of(dense_ref, j * width, width))
        up = up + matmul(part, weight_rows_of(down_ref, j * width, width))
    attended_ref[...] = attended.astype(jnp.bfloat16)
    up = (up * slope_ref[...]).astype(jnp.bfloat16)
    up_ref[...] = up
    sums_ref[...] += jnp.sum(up.astype(jnp.float32), axis=0, keepdims=True)


def back_through(cot, slope, dense, down, rows=512, after=()):
    total, hidden = slope.shape
    lanes = dense.width
    return call(
        back_kernel,
        "back_through",
        (total // rows,),
        [cot_spec(cot, rows), band(rows, hidden), dense.spec, down.spec],
        [band(rows, lanes), band(rows, hidden), whole(1, hidden)],
        [
            struct((total, lanes), jnp.bfloat16),
            struct((total, hidden), jnp.bfloat16),
            struct((1, hidden), jnp.float32),
        ],
        flops=4 * total * D * (hidden + lanes),
        after=after,
    )(cot, slope, dense.array, down.array)


def rows_of(index, size):
    return pl.ds(pl.multiple_of(index * size, size), size)


HEADS_HERE = [slice(n * HEAD_DIM, (n + 1) * HEAD_DIM) for n in range(2)]


def turned_into(ref, source_ref, cols):
    chunk = 256

    def one(b, carry):
        rows = rows_of(b, chunk)
        ref[:, rows] = source_ref[rows, cols].T
        return carry

    lax.fori_loop(0, source_ref.shape[0] // chunk, one, 0)


def causal_block(block):
    return lax.broadcasted_iota(jnp.int32, (block, block), 0) <= lax.broadcasted_iota(
        jnp.int32, (block, block), 1
    )


def fold_rows(values, combine):
    rows, cols = values.shape
    return combine(values.reshape(rows // 8, 8, cols), axis=0)


def attention_kernel(block, qkv_ref, attended_ref, log_sums_ref, qt_ref, vt_ref, score_ref):
    i = pl.program_id(0)
    width = 2 * HEAD_DIM

    @pl.when(i == 0)
    def _():
        turned_into(qt_ref, qkv_ref, slice(0, width))
        turned_into(vt_ref, qkv_ref, slice(2 * width, 3 * width))
        log_sums_ref[...] = jnp.zeros_like(log_sums_ref)

    own = rows_of(i, block)
    causal = causal_block(block)

    def score(j, best, diagonal):
        rows = rows_of(j, block)
        new = []
        for n, head in enumerate(HEADS_HERE):
            start = width + n * HEAD_DIM
            part = matmul(qkv_ref[rows, start : start + HEAD_DIM], qt_ref[head, own])
            if diagonal:
                part = jnp.where(causal, part, -1e30)
            score_ref[n, j] = part
            new.append(jnp.maximum(best[n], fold_rows(part, jnp.max)))
        return tuple(new)

    low = jnp.full((8, block), -1e30, jnp.float32)
    best = lax.fori_loop(0, i, lambda j, b: score(j, b, False), (low, low))
    best = score(i, best, True)
    top = [jnp.max(value, axis=0, keepdims=True) for value in best]

    def weigh(j, carry):
        new = []
        for n in range(2):
            weights = jnp.exp(score_ref[n, j] - top[n])
            score_ref[n, j] = weights
            new.append(carry[n] + fold_rows(weights, jnp.sum))
        return tuple(new)

    zero = jnp.zeros((8, block), jnp.float32)
    totals = lax.fori_loop(0, i + 1, weigh, (zero, zero))
    totals = [jnp.sum(total, axis=0, keepdims=True) for total in totals]
    scales = [1.0 / total for total in totals]
    for n in range(2):
        log_sums_ref[n : n + 1, own] = top[n] + jnp.log(totals[n])

    def push(j, carry):
        rows = rows_of(j, block)
        new = []
        for n, head in enumerate(HEADS_HERE):
            probs = (score_ref[n, j] * scales[n]).astype(jnp.bfloat16)
            new.append(carry[n] + matmul(vt_ref[head, rows], probs))
        return tuple(new)

    zero = jnp.zeros((HEAD_DIM, block), jnp.float32)
    out = lax.fori_loop(0, i + 1, push, (zero, zero))
    attended_ref[own, :] = jnp.concatenate(out, axis=0).T.astype(jnp.bfloat16)


def attention(qkv, block=512, after=()):
    rows, width = qkv.shape[0], 2 * HEAD_DIM
    blocks = rows // block
    return call(
        partial(attention_kernel, block),
        "attention",
        (blocks,),
        [whole(rows, 3 * width)],
        [whole(rows, width), whole(8, rows)],
        [struct((rows, width), jnp.bfloat16), struct((8, rows), jnp.float32)],
        [pltpu.VMEM((width, rows), jnp.bfloat16)] * 2
        + [pltpu.VMEM((2, blocks, block, block), jnp.float32)],
        flops=10 * 10**9,
        after=after,
    )(qkv)


def attention_back_kernel(
    blocks,
    block,
    qkv_ref,
    grad_ref,
    log_sums_ref,
    cosine_ref,
    sine_ref,
    pre_grad_ref,
    sums_ref,
    qt_ref,
    kt_ref,
    gt_ref,
    prob_ref,
    slope_ref,
    k_total,
    v_total,
):
    i = pl.program_id(0)
    width = 2 * HEAD_DIM
    factor = 1.0 / math.sqrt(HEAD_DIM)
    chunk = 256

    @pl.when(i == 0)
    def _():
        turned_into(qt_ref, qkv_ref, slice(0, width))
        turned_into(kt_ref, qkv_ref, slice(width, 2 * width))
        turned_into(gt_ref, grad_ref, slice(0, width))
        k_total[...] = jnp.zeros_like(k_total)
        v_total[...] = jnp.zeros_like(v_total)
        sums_ref[...] = jnp.zeros_like(sums_ref)

    own = rows_of(i, block)
    causal = causal_block(block)
    log_sums = [log_sums_ref[n : n + 1, own] for n in range(2)]

    def weigh(j, carry, diagonal):
        rows = rows_of(j, block)
        new = []
        for n, head in enumerate(HEADS_HERE):
            start = width + n * HEAD_DIM
            scores = matmul(qkv_ref[rows, start : start + HEAD_DIM], qt_ref[head, own])
            probs = jnp.exp(scores - log_sums[n])
            if diagonal:
                probs = jnp.where(causal, probs, 0.0)
            start += width
            slope = matmul(qkv_ref[rows, start : start + HEAD_DIM], gt_ref[head, own])
            prob_ref[n, j] = probs
            slope_ref[n, j] = slope
            new.append(carry[n] + fold_rows(probs * slope, jnp.sum))
        return tuple(new)

    zero = jnp.zeros((8, block), jnp.float32)
    dots = lax.fori_loop(0, i, lambda j, c: weigh(j, c, False), (zero, zero))
    dots = weigh(i, dots, True)
    dots = [jnp.sum(dot, axis=0, keepdims=True) for dot in dots]

    def push(j, carry):
        rows = rows_of(j, block)
        new = []
        for n, head in enumerate(HEADS_HERE):
            probs = prob_ref[n, j]
            score_grad = (probs * (slope_ref[n, j] - dots[n])).astype(jnp.bfloat16)
            k_total[rows, head] += matmul(score_grad, qkv_ref[own, head])
            v_total[rows, head] += matmul(probs.astype(jnp.bfloat16), grad_ref[own, head])
            new.append(carry[n] + matmul(kt_ref[head, rows], score_grad))
        return tuple(new)

    zero = jnp.zeros((HEAD_DIM, block), jnp.float32)
    q_grad = lax.fori_loop(0, i + 1, push, (zero, zero))
    q_grad = jnp.concatenate(q_grad, axis=0).T * factor
    q_pre = turn(q_grad, cosine_ref[own, :], -sine_ref[own, :]).astype(jnp.bfloat16)
    pre_grad_ref[own, :width] = q_pre
    sums_ref[:, :width] += jnp.sum(q_pre.astype(jnp.float32), axis=0, keepdims=True)

    @pl.when(i == blocks - 1)
    def _():
        def finish(b, carry):
            rows = rows_of(b, chunk)
            k_pre = turn(k_total[rows, :], cosine_ref[rows, :], -sine_ref[rows, :])
            k_pre = k_pre.astype(jnp.bfloat16)
            v_pre = v_total[rows, :].astype(jnp.bfloat16)
            pre_grad_ref[rows, width : 2 * width] = k_pre
            pre_grad_ref[rows, 2 * width :] = v_pre
            both = jnp.concatenate([k_pre, v_pre], axis=1).astype(jnp.float32)
            return carry + jnp.sum(both, axis=0, keepdims=True)

        sums_ref[:, width:] = lax.fori_loop(
            0, qkv_ref.shape[0] // chunk, finish, jnp.zeros((1, 2 * width), jnp.float32)
        )


def attention_back(qkv, out_grad, log_sums, block=512, after=()):
    rows, width = qkv.shape[0], 2 * HEAD_DIM
    blocks = rows // block
    cosine, sine = rotary_tables(rows)
    return call(
        partial(attention_back_kernel, blocks, block),
        "attention_back",
        (blocks,),
        [whole(rows, 3 * width), whole(rows, width), whole(8, rows)]
        + [whole(rows, width), whole(rows, width)],
        [whole(rows, 3 * width), whole(1, 3 * width)],
        [struct((rows, 3 * width), jnp.bfloat16), struct((1, 3 * width), jnp.float32)],
        [pltpu.VMEM((width, rows), jnp.bfloat16)] * 3
        + [pltpu.VMEM((2, blocks, block, block), jnp.float32)] * 2
        + [pltpu.VMEM((rows, width), jnp.float32)] * 2,
        flops=20 * 10**9,
        after=after,
    )(qkv, out_grad, log_sums, jnp.asarray(cosine), jnp.asarray(sine))


def weight_grad_kernel(riders, *refs):
    out_ref, refs = refs[-1], refs[:-1]
    if riders:
        height = out_ref.shape[1] - refs[0].shape[1]
        out_ref[:, height:, :] = refs[0][...]
        refs = refs[1:]
    cols = out_ref.shape[2]
    start = 0
    for left_ref, right_ref in zip(refs[::2], refs[1::2]):
        if len(right_ref.shape) == 5:
            size = right_ref.shape[3]
            part = 0.0
            for b in range(4):
                rows = slice(b * size, (b + 1) * size)
                part = part + contract_rows(left_ref[rows, :], right_ref[b % 2, 0, b // 2])
        else:
            part = contract_rows(left_ref[...], right_ref[...])
        part = part.astype(jnp.bfloat16)
        stop = start + part.shape[0]
        for n in range(out_ref.shape[0]):
            out_ref[n, start:stop, :] = part[:, n * cols : (n + 1) * cols]
        start = stop


def weight_grad(pairs, parts, rider=None, after=()):
    cols = D // parts
    per = parts // 4
    rows = pairs[0][0].shape[0]
    height = sum(left.shape[1] for left, _ in pairs)
    in_specs, operands = [], []
    if rider is not None:
        in_specs.append(pl.BlockSpec((per,) + rider.shape[1:], lambda i: (i, 0, 0)))
        operands.append(rider)
        height += rider.shape[1]
    for left, right in pairs:
        in_specs.append(whole(*left.shape))
        if right.ndim == 5:
            in_specs.append(
                pl.BlockSpec((2, 1, 2, right.shape[3], D // 4), lambda i: (0, i, 0, 0, 0))
            )
        else:
            in_specs.append(pl.BlockSpec((rows, D // 4), lambda i: (0, i)))
        operands += [left, right]
    return call(
        partial(weight_grad_kernel, rider is not None),
        "weight_grad",
        (4,),
        in_specs,
        pl.BlockSpec((per, height, cols), lambda i: (i, 0, 0)),
        struct((parts, height, cols), jnp.bfloat16),
        flops=4 * rows * height * D,
        after=after,
    )(*operands)


def partial_sum_kernel(sides, axes, index_ref, *refs):
    lefts, refs = refs[: 2 * sides], refs[2 * sides :]
    weights, others, outs = refs[:sides], refs[sides : 2 * sides], refs[2 * sides :]
    rows, width = outs[0].shape[-2:]
    own_m, own_h, core = index_ref[0], index_ref[1], index_ref[2]
    here = lax.rem(pl.program_id(0), 2) == own_h
    for n_m, m in enumerate((own_m, 1 - own_m)):
        out = 0.0
        for n in range(sides):
            weight = weight_rows_of(weights[n], (2 * m + core) * width, width)
            out = out + contract_cols(lefts[n][...], weight)
            other = others[n][m].reshape(width, weight.shape[1])
            out = out + contract_cols(lefts[sides + n][...], other)
        out = out.astype(jnp.bfloat16)
        for half, axis in enumerate(axes):
            part = out[half * rows : (half + 1) * rows]
            if axis == "m":
                outs[2 * half + n_m][0] = part
                continue
            for n_h, mine in enumerate((here, jnp.logical_not(here))):

                @pl.when(mine)
                def _(out_ref=outs[2 * half + n_h], m=m, part=part):
                    out_ref[0, m] = part


def partial_sum(sides, row_count, width, name, axes, after=()):
    total = sides[0][0].shape[0]
    rows = row_count // len(axes)
    blocks = total // row_count
    lefts = [side[0] for side in sides] + [side[1] for side in sides]
    weights = [side[2] for side in sides]
    others = [side[3] for side in sides]
    depth = sum(left.shape[1] for left in lefts)
    specs, shapes = [], []
    for axis in axes:
        if axis == "m":
            specs += [pl.BlockSpec((1, rows, width), lambda i: (i, 0, 0))] * 2
            shapes += [struct((blocks, rows, width), jnp.bfloat16)] * 2
        else:
            specs += [pl.BlockSpec((1, 2, rows, width), lambda i: (i // 2, 0, 0, 0))] * 2
            shapes += [struct((blocks // 2, 2, rows, width), jnp.bfloat16)] * 2
    index = jnp.stack([lax.axis_index(axis) for axis in "mhc"]).astype(jnp.int32)
    return call(
        partial(partial_sum_kernel, len(sides), axes),
        name,
        (blocks,),
        [SCALARS]
        + [band(row_count, left.shape[1]) for left in lefts]
        + [weight.spec for weight in weights]
        + [other.spec for other in others],
        specs,
        shapes,
        flops=2 * total * depth * D,
        after=after,
    )(index, *lefts, *[weight.array for weight in weights], *[other.array for other in others])


def switch_specs(count, block):
    zeros = (0,) * (len(block) - 1)
    return [
        pl.BlockSpec(block, lambda k, j, p: (j + k * (count - 1 - j),) + zeros),
        pl.BlockSpec(block, lambda k, j, p: (j * k,) + zeros),
    ]


def prefetch_call(kernel, name, index, grid, in_specs, out_specs, out_shape, after=()):
    skipped = len(after)

    def ordered(index_ref, *refs):
        kernel(index_ref, *refs[skipped:])

    run = pl.pallas_call(
        ordered,
        grid_spec=pltpu.PrefetchScalarGridSpec(
            num_scalar_prefetch=1,
            grid=grid,
            in_specs=[ANY] * skipped + list(in_specs),
            out_specs=out_specs,
        ),
        out_shape=out_shape,
        compiler_params=pltpu.CompilerParams(vmem_limit_bytes=VMEM_LIMIT),
        cost_estimate=pl.CostEstimate(flops=0, bytes_accessed=0, transcendentals=0),
        name=name,
    )
    return lambda *operands: run(index.astype(jnp.int32).reshape(1), *after, *operands)


def column_specs(shards, turned, block):
    specs, width = [], 0
    for flip, shard in zip(turned, shards):
        height, cols = shard.shape
        if flip:
            specs.append(pl.BlockSpec((height // 4, cols), lambda *at: (block(*at), 0)))
            rows, width = cols, width + height // 4
        else:
            specs.append(pl.BlockSpec((height, cols // 4), lambda *at: (0, block(*at))))
            rows, width = height, width + cols // 4
    return specs, rows, width


def write_columns(turned, refs, store):
    start = 0
    for flip, ref in zip(turned, refs):
        part = ref[...].T if flip else ref[...]
        store(slice(start, start + part.shape[1]), part)
        start += part.shape[1]


def pack_kernel(turned, rows, riders, *refs):
    out_ref, refs = refs[-1], refs[:-1]
    if riders:
        rider, refs = refs[0][...], refs[1:]

    def store(cols, part):
        for n in range(out_ref.shape[0]):
            out_ref[n, 0, :rows, cols] = part

    write_columns(turned, refs, store)
    if riders:
        for n in range(out_ref.shape[0]):
            out_ref[n, 0, rows:, :] = rider


def packed(shards, turned, rider=None):
    wide = lax.axis_size(WIDE)
    specs, rows, width = column_specs(shards, turned, lambda i: i)
    height = rows
    if rider is not None:
        specs = [whole(*rider.shape)] + specs
        shards = [rider] + shards
        height += rider.shape[0]
    blocks = call(
        partial(pack_kernel, turned, rows, rider is not None),
        "pack",
        (4,),
        specs,
        pl.BlockSpec((wide // 4, 1, height, width), lambda i: (0, i, 0, 0)),
        struct((wide // 4, 4, height, width), jnp.bfloat16),
    )(*shards)
    return blocks.reshape(wide, height, width)


def exchanged(blocks, after=()):
    blocks = lax.optimization_barrier((blocks, *after))[0]
    return lax.all_to_all(blocks, WIDE, 0, 0)


def sides_kernel(turned, index_ref, *refs):
    for out_ref, blocks in zip(refs[-2:], (refs[:-2][::2], refs[:-2][1::2])):

        def store(cols, part, out_ref=out_ref):
            out_ref[0, :, cols] = part

        write_columns(turned, blocks, store)


def packed_sides(shards, turned):
    specs, operands, width = [], [], 0
    for flip, shard in zip(turned, shards):
        height, cols = shard.shape
        if flip:
            rows, width = cols, width + height // 4
            shape, at = (height // 4, cols), lambda block: (block, 0)
        else:
            rows, width = height, width + cols // 4
            shape, at = (height, cols // 4), lambda block: (0, block)
        specs.append(pl.BlockSpec(shape, lambda j, p, at=at: at(2 * j + p[0])))
        specs.append(pl.BlockSpec(shape, lambda j, p, at=at: at(2 * j + 1 - p[0])))
        operands += [shard, shard]
    return prefetch_call(
        partial(sides_kernel, turned),
        "pack",
        lax.axis_index("h"),
        (2,),
        specs,
        [pl.BlockSpec((1, rows, width), lambda j, p: (j, 0, 0))] * 2,
        [struct((2, rows, width), jnp.bfloat16)] * 2,
    )(*operands)


def spread_kernel(index_ref, mine_ref, other_ref, out_ref):
    for n in range(out_ref.shape[0]):
        out_ref[n, 0, index_ref[0]] = mine_ref[0]
        out_ref[n, 0, 1 - index_ref[0]] = other_ref[0]


def spread_sides(sides, after=()):
    mine, send = sides
    sequences = lax.axis_size("s")
    _, rows, width = mine.shape
    spec = pl.BlockSpec((1, rows, width), lambda j, p: (j, 0, 0))
    blocks = prefetch_call(
        spread_kernel,
        "spread",
        lax.axis_index("h"),
        (2,),
        [spec, spec],
        pl.BlockSpec((sequences, 1, 2, rows, width), lambda j, p: (0, j, 0, 0, 0)),
        struct((sequences, 2, 2, rows, width), jnp.bfloat16),
        after=after,
    )(mine, shifted(send, "h", 1))
    return blocks.reshape(2 * sequences, 2 * rows, width)


def exchanged_along_line(blocks):
    count, rows, width = blocks.shape
    return lax.all_to_all(blocks, LINE, 0, 0).reshape(2 * count, rows // 2, width)


def unpack_kernel(turned, arrived_ref, *outs):
    total = arrived_ref[0, 0].astype(jnp.float32)
    for n in range(1, arrived_ref.shape[0]):
        total = total + arrived_ref[n, 0].astype(jnp.float32)
    start = 0
    for flip, out_ref in zip(turned, outs):
        height = out_ref.shape[0] if flip else out_ref.shape[1]
        part = total[start : start + height]
        out_ref[...] = part if flip else part.T
        start += height


def scatter_columns(grad, heights, turned, after=()):
    sequences = lax.axis_size("s")
    _, height, rows = grad.shape
    arrived = lax.all_to_all(grad, WIDE, 0, 0)
    riders = arrived[:, sum(heights) :]
    arrived = arrived.reshape(sequences, 4, height, rows)
    height = sum(heights)
    specs, shapes = [], []
    for flip, part in zip(turned, heights):
        if flip:
            specs.append(pl.BlockSpec((part, rows), lambda i: (i, 0)))
            shapes.append(struct((4 * part, rows), jnp.float32))
        else:
            specs.append(pl.BlockSpec((rows, part), lambda i: (0, i)))
            shapes.append(struct((rows, 4 * part), jnp.float32))
    shards = call(
        partial(unpack_kernel, turned),
        "unpack",
        (4,),
        [pl.BlockSpec((sequences, 1, height, rows), lambda i: (0, i, 0, 0))],
        specs,
        shapes,
        after=after,
    )(arrived)
    return shards, riders


def side_sums_kernel(index_ref, arrived_ref, keep_ref, send_ref):
    for out_ref, side in ((keep_ref, index_ref[0]), (send_ref, 1 - index_ref[0])):
        total = arrived_ref[0, 0, side].astype(jnp.float32)
        for n in range(1, arrived_ref.shape[0]):
            total = total + arrived_ref[n, 0, side].astype(jnp.float32)
        out_ref[0] = total.astype(out_ref.dtype)


def unpack_sides_kernel(turned, index_ref, keep_ref, other_ref, *outs):
    def write(total):
        start = 0
        for flip, out_ref in zip(turned, outs):
            height = out_ref.shape[0] if flip else out_ref.shape[1]
            part = total[start : start + height]
            out_ref[...] = part if flip else part.T
            start += height

    @pl.when(pl.program_id(1) == 0)
    def _():
        write(keep_ref[0])

    @pl.when(pl.program_id(1) == 1)
    def _():
        write(other_ref[0].astype(jnp.float32))


def scatter_along_line(grad, heights, turned, after=(), late_after=()):
    sequences, side = lax.axis_size("s"), lax.axis_index("h")
    wide, height, rows = grad.shape
    arrived = lax.all_to_all(grad.reshape(wide // 2, 2 * height, rows), LINE, 0, 0)
    band_of = pl.BlockSpec((1, height, rows), lambda j, p: (j, 0, 0))
    keep, send = prefetch_call(
        side_sums_kernel,
        "side_sums",
        side,
        (2,),
        [pl.BlockSpec((sequences, 1, 2, height, rows), lambda j, p: (0, j, 0, 0, 0))],
        [band_of, band_of],
        [struct((2, height, rows), jnp.float32), struct((2, height, rows), jnp.bfloat16)],
        after=after,
    )(arrived.reshape(sequences, 2, 2, height, rows))
    other = shifted(send, "h", 1)
    riders = keep[:, sum(heights) :] + other[:, sum(heights) :].astype(jnp.float32)
    specs, shapes = [], []
    block = lambda j, n, p: 2 * j + p[0] + n - 2 * n * p[0]
    for flip, part in zip(turned, heights):
        if flip:
            specs.append(pl.BlockSpec((part, rows), lambda j, n, p: (block(j, n, p), 0)))
            shapes.append(struct((4 * part, rows), jnp.float32))
        else:
            specs.append(pl.BlockSpec((rows, part), lambda j, n, p: (0, block(j, n, p))))
            shapes.append(struct((rows, 4 * part), jnp.float32))
    part_of = pl.BlockSpec((1, sum(heights), rows), lambda j, n, p: (j, 0, 0))
    shards = prefetch_call(
        partial(unpack_sides_kernel, turned),
        "unpack",
        side,
        (2, 2),
        [part_of, part_of],
        specs,
        shapes,
        after=late_after,
    )(keep, other)
    return shards, riders


def fold_kernel(index_ref, mine_keep, mine_send, arrived_keep, arrived_send, keep_ref, send_ref):
    keep_ref[...] = mine_keep[...] + arrived_keep[...]
    send_ref[...] = mine_send[...] + arrived_send[...]


def folded(mine, arrived, axes, axis, after=()):
    position = axes.index(axis)
    high, low = 2**position, 2 ** (len(axes) - 1 - position)
    rows, cols = mine.shape[-2:]
    shape = (high, 2, low * rows, cols)
    steps = 2 if low > 1 else 1
    block = low * rows // steps
    halves = [
        pl.BlockSpec((high, None, block, cols), lambda j, p: (0, p[0], j, 0)),
        pl.BlockSpec((high, None, block, cols), lambda j, p: (0, 1 - p[0], j, 0)),
    ]
    out = pl.BlockSpec((high, block, cols), lambda j, p: (0, j, 0))
    mine, arrived = mine.reshape(shape), arrived.reshape(shape)
    keep, send = prefetch_call(
        fold_kernel,
        "fold",
        lax.axis_index(axis),
        (steps,),
        halves * 2,
        [out, out],
        [struct((high, low * rows, cols), jnp.bfloat16)] * 2,
        after=after,
    )(mine, mine, arrived, arrived)
    return [part.reshape(high * low, rows, cols) for part in (keep, send)]


def join_kernel(index_ref, mine_ref, other_ref, out_ref):
    out_ref[index_ref[0]] = mine_ref[...]
    out_ref[1 - index_ref[0]] = other_ref[...]


def joined(mine, axis, after=()):
    other = shifted(mine, axis, 1)
    rows, cols = mine.size // mine.shape[-1] // 2, mine.shape[-1]
    spec = pl.BlockSpec((rows, cols), lambda j, p: (j, 0))
    out = prefetch_call(
        join_kernel,
        "join",
        lax.axis_index(axis),
        (2,),
        [spec, spec],
        pl.BlockSpec((2, rows, cols), lambda j, p: (0, j, 0)),
        struct((2, 2 * rows, cols), mine.dtype),
        after=after,
    )(mine.reshape(2 * rows, cols), other.reshape(2 * rows, cols))
    return out.reshape((2,) + mine.shape)


def finish_kernel(tokens_ref, *refs):
    bias_ref, out_ref = refs[-2:]
    parts = len(refs) // 2 - 1
    rows = refs[0].shape[0]
    for n, (keep_ref, arrived_ref) in enumerate(zip(refs[:parts], refs[parts : 2 * parts])):
        at = slice(n * rows, (n + 1) * rows)
        total = tokens_ref[at, :].astype(jnp.float32) + keep_ref[...].astype(jnp.float32)
        total = total + arrived_ref[...].astype(jnp.float32) + bias_ref[...]
        out_ref[at, :] = total.astype(jnp.bfloat16)


def finished(tokens, keep, arrived, bias, after=()):
    operands = [tokens, *keep, *arrived, bias]
    return call(
        finish_kernel,
        "finish",
        (1,),
        [whole(*operand.shape) for operand in operands],
        whole(*tokens.shape),
        struct(tokens.shape, tokens.dtype),
        after=after,
    )(*operands)


def gather_narrow(value):
    for axis in ("c", "m"):
        other = shifted(value, axis, 1)
        value = jnp.stack(in_order(value, other, lax.axis_index(axis)))
    return value.reshape((4,) + value.shape[2:])


def summed(value, axis):
    total = value
    for step in range(1, lax.axis_size(axis)):
        total = total + shifted(value, axis, step)
    return total


def body(
    tokens,
    cotangent,
    ln_gain,
    ln_shift,
    w_query,
    b_query,
    w_key,
    b_key,
    w_value,
    b_value,
    w_dense,
    b_dense,
    w_fc1,
    b_fc1,
    w_fc2,
    b_fc2,
):
    row_count, feature_count = tokens.shape
    own_g, own_h = lax.axis_index("g"), lax.axis_index("h")
    own_n = lax.axis_index(NARROW)
    quarter = 2 * own_g + own_h
    wide = lax.axis_size(WIDE)
    weight_rows = w_fc1.shape[0]
    lanes = w_query.shape[1] // 4

    vectors = (ln_gain, ln_shift, b_query, b_key, b_value, b_dense, b_fc2, b_fc1)
    lengths = [vector.shape[0] for vector in vectors]
    hidden = w_fc1.shape[1] // 4
    rider = jnp.concatenate(vectors)
    rider = jnp.pad(rider, (0, 16 * hidden - rider.shape[0])).reshape(16, hidden)

    tokens_full = lax.all_gather(tokens, CUBE, axis=0, tiled=False)
    tokens_full = tokens_full.reshape(4, 4, row_count, feature_count)
    up_blocks = packed([w_fc1], [False], rider)
    head_sides = packed_sides(
        [w_query, w_key, w_value, w_dense], [False, False, False, True]
    )
    down_sides = packed_sides([w_fc2], [True])
    cot = joined(cotangent, "g", after=[up_blocks, head_sides[0], down_sides[0]])
    arrived = exchanged(up_blocks, after=[cot])
    cot = lax.all_gather(cot, ("h", "m", "c"), axis=0, tiled=False)
    cot = cot.reshape(2, 4, 2, row_count, feature_count)
    head_blocks = spread_sides(head_sides, after=[arrived])
    head_arrived = exchanged_along_line(head_blocks)
    up_weight = Weight(arrived, weight_rows, 0, hidden)
    qkv_weight = Weight(head_arrived, weight_rows, 0, 3 * lanes)
    dense_weight = Weight(head_arrived, weight_rows, 3 * lanes, lanes)

    def from_other_core(array):
        split = array[:, :weight_rows].reshape(2, 2, wide // 4, weight_rows, -1)
        return shifted(pick(split, 1 - lax.axis_index("c"), 1), "c", 1)

    up_other = Weight(from_other_core(arrived), weight_rows, 0, hidden)
    head_other = from_other_core(head_arrived)
    qkv_other = Weight(head_other, weight_rows, 0, 3 * lanes)
    dense_other = Weight(head_other, weight_rows, 3 * lanes, lanes)

    here = arrived[:, weight_rows:].reshape(wide, 16 * hidden)
    local, start = [], 0
    for length in lengths:
        local.append(here[:, start : start + length].astype(jnp.float32).reshape(-1))
        start += length
    shared = gather_narrow(here[:, : 2 * lengths[0]].astype(jnp.float32))
    gain = shared[:, :, : lengths[0]].reshape(1, D)
    shift = shared[:, :, lengths[0] :].reshape(1, D)

    def quarter_of(vector):
        return pick(vector.reshape(4, -1), quarter)

    qkv_bias = jnp.concatenate([quarter_of(vector) for vector in local[2:5]]).reshape(1, -1)
    up_bias = quarter_of(local[7]).reshape(1, -1)
    own_gain, out_bias = local[0], local[5] + local[6]

    normed, stats, up_low, up_slope = norm_up(
        tokens_full, gain, shift, up_bias, up_weight, after=[up_other.array]
    )
    down_blocks = spread_sides(down_sides, after=[normed])
    down_arrived = exchanged_along_line(down_blocks)
    down_weight = Weight(down_arrived, weight_rows, 0, hidden)
    qkv = project_heads(normed, qkv_bias, qkv_weight, after=[head_other])
    attended, log_sums = attention(qkv)
    grad_down = weight_grad([(up_low, cot)], wide, after=[attended])
    attended_grad, up_grad, up_sums = back_through(
        cot, up_slope, dense_weight, down_weight, after=[grad_down]
    )
    qkv_grad, qkv_sums = attention_back(qkv, attended_grad, log_sums)
    qkv_grad_other = shifted(qkv_grad, "c", 1)

    grad_up = weight_grad([(up_grad, normed)], wide, after=[qkv_grad])
    up_grad_other = shifted(up_grad, "c", 1)
    grad_up = lax.optimization_barrier((grad_up, qkv_grad_other, up_grad_other))[0]
    normed_grad = partial_sum(
        [
            (qkv_grad, qkv_grad_other, qkv_weight, qkv_other),
            (up_grad, up_grad_other, up_weight, up_other),
        ],
        row_count,
        feature_count,
        "normed_gradient",
        "mh",
        after=[grad_up],
    )

    down_other = lax.optimization_barrier((down_arrived, normed_grad[0]))[0]
    down_other = Weight(from_other_core(down_other), weight_rows, 0, hidden)
    branch = partial_sum(
        [
            (attended, shifted(attended, "c", 1), dense_weight, dense_other),
            (up_low, shifted(up_low, "c", 1), down_weight, down_other),
        ],
        row_count,
        feature_count,
        "branch_sum",
        "mm",
        after=normed_grad[:1],
    )
    def spread(vector):
        placed = jnp.zeros((4, vector.shape[0]), jnp.float32)
        placed = lax.dynamic_update_index_in_dim(placed, vector, quarter, 0)
        return placed.reshape(wide, -1)

    terms = [
        spread(qkv_sums[0, :lanes]),
        spread(qkv_sums[0, lanes : 2 * lanes]),
        spread(qkv_sums[0, 2 * lanes :]),
        jnp.sum(cotangent.astype(jnp.float32), axis=0).reshape(wide, -1),
        spread(up_sums[0]),
    ]
    rider = jnp.concatenate(terms, axis=1).astype(jnp.bfloat16)
    early_count = rider.shape[1]
    rider = jnp.pad(rider, ((0, 0), (0, 16 * weight_rows - early_count)))
    grad_heads = weight_grad(
        [(qkv_grad, normed), (attended, cot)],
        wide,
        rider.reshape(wide, 16, weight_rows),
        after=branch[:1],
    )
    first = [normed_grad[:2], normed_grad[2:]]
    second = [branch[:2], branch[2:]]

    def fold(part, arrived, axes, after, axis=None):
        other = shifted(part[1], arrived, 1)
        return folded(part[0], other, axes, axis or axes[-1], after=[after])

    first[0] = fold(first[0], "m", "gh", grad_heads)
    (grad_down,), _ = scatter_columns(grad_down, [hidden], [True], after=first[0][:1])
    first[1] = fold(first[1], "h", "gm", grad_down)
    second[0] = fold(second[0], "m", "gh", first[1][0])
    later = lax.optimization_barrier((branch[3], first[1][0]))[0]
    second[1] = [branch[2], later]
    first[0] = fold(first[0], "h", "g", second[0][0])
    first[1] = fold(first[1], "m", "g", first[0][0])
    (grad_up,), _ = scatter_columns(grad_up, [hidden], [False], after=first[1][:1])

    def last(keep, send):
        arrived = lax.optimization_barrier((shifted(send[0], "g", 1), grad_up))[0]
        return keep[0].astype(jnp.float32) + arrived.astype(jnp.float32)

    local_x = tokens.astype(jnp.float32)
    standard_grad = jnp.concatenate([last(*part) for part in first], axis=0)
    own_stats = pick(stats.reshape(4, row_count, 128), quarter)
    row_mean, inverse_std = own_stats[:, :1], own_stats[:, 64:65]
    standard = (local_x - row_mean) * inverse_std
    scaled_grad = standard_grad * own_gain
    row_sums = jnp.stack([jnp.sum(scaled_grad, axis=1), jnp.sum(scaled_grad * standard, axis=1)])
    for axis in ("c", "m"):
        row_sums = row_sums + shifted(row_sums, axis, 1)
    input_grad = (
        scaled_grad - row_sums[0][:, None] / D - standard * (row_sums[1][:, None] / D)
    ) * inverse_std + cotangent.astype(jnp.float32)

    own_terms = [jnp.sum(standard_grad * standard, axis=0), jnp.sum(standard_grad, axis=0)]
    own_terms = [term.reshape(wide, -1) for term in own_terms]
    late = summed(jnp.concatenate(own_terms, axis=1), "h")
    late = summed(summed(late, "g"), "s")
    second[1] = fold(second[1], "m", "gh", standard_grad, "g")
    second[0] = fold(second[0], "h", "g", second[1][0])
    second[1] = fold(second[1], "g", "h", second[0][0])
    (grad_query, grad_key, grad_value, grad_dense), riders = scatter_along_line(
        grad_heads,
        [lanes] * 4,
        [False, False, False, True],
        after=[standard_grad],
        late_after=second[1][:1],
    )
    early = jnp.sum(riders.astype(jnp.float32), axis=0).reshape(-1)[:early_count]
    output = finished(
        tokens,
        [part[0][0] for part in second],
        [shifted(part[1][0], axis, 1) for part, axis in zip(second, "gh")],
        out_bias.reshape(1, -1),
        after=[grad_dense],
    )
    terms = own_terms + terms
    vector_sums = jnp.concatenate([pick(late, lax.axis_index(WIDE)), early])
    vector_grads, start = [], 0
    for term in terms:
        vector_grads.append(vector_sums[start : start + term.shape[1]])
        start += term.shape[1]
    return (
        output,
        input_grad,
        vector_grads[0],
        vector_grads[1],
        grad_query,
        vector_grads[2],
        grad_key,
        vector_grads[3],
        grad_value,
        vector_grads[4],
        grad_dense,
        vector_grads[5],
        grad_up,
        vector_grads[6],
        grad_down,
        vector_grads[5],
    )


def solution(mesh):
    wide = mesh.shape["wide"]
    inner = Mesh(mesh.devices.reshape(wide // 4, 2, 2, 2, 2), ("s", "g", "h", "m", "c"))
    acts = P(WIDE, NARROW)
    vector = P(NARROW + WIDE)
    by_rows = P(WIDE, NARROW)
    by_cols = P(NARROW, WIDE)
    specs = (
        (acts, acts, vector, vector)
        + (by_rows, vector) * 3
        + (by_cols, vector, by_rows, vector, by_cols, vector)
    )
    return jax.shard_map(body, mesh=inner, in_specs=specs, out_specs=specs, check_vma=False)
```

```python
from functools import partial
import math

import jax
import jax.numpy as jnp
import numpy as np
from jax import lax
from jax.experimental import pallas as pl
from jax.experimental.pallas import tpu as pltpu
from jax.sharding import Mesh, PartitionSpec as P

D = 2048
HEAD_DIM = 64
ROT = 32
EPSILON = 1e-05
VMEM_LIMIT = 56 * 2**20
COST = 1

WIDE = ("s", "g", "h")
LINE = ("s", "g")
LINE = ("s", "g")
NARROW = ("m", "c")
CUBE = ("g", "h", "m", "c")


def matmul(left_side, right_side):
    return jnp.dot(left_side, right_side, preferred_element_type=jnp.float32)


def contract_rows(left_side, right_side):
    return lax.dot_general(
        left_side, right_side, (((0,), (0,)), ((), ())), preferred_element_type=jnp.float32
    )


def contract_cols(left_side, right_side):
    return lax.dot_general(
        left_side, right_side, (((1,), (1,)), ((), ())), preferred_element_type=jnp.float32
    )


def pick(blocks, index, axis=0):
    return lax.dynamic_index_in_dim(blocks, index, axis, keepdims=False)


def shifted(value, axis, step):
    count = lax.axis_size(axis)
    return lax.ppermute(value, axis, [(source, (source + step) % count) for source in range(count)])


def in_order(mine, other, index):
    return (jnp.where(index == 0, mine, other), jnp.where(index == 0, other, mine))


def call(
    kernel, name, grid, in_specs, out_specs, out_shape, scratch=(), flops=0, after=()
):
    skipped = len(after)

    def ordered(*refs):
        kernel(*refs[skipped:])

    run = pl.pallas_call(
        ordered,
        grid=grid,
        in_specs=[ANY] * skipped + list(in_specs),
        out_specs=out_specs,
        out_shape=out_shape,
        scratch_shapes=list(scratch),
        compiler_params=pltpu.CompilerParams(vmem_limit_bytes=VMEM_LIMIT),
        cost_estimate=pl.CostEstimate(flops=COST * flops // 1000, bytes_accessed=0, transcendentals=0),
        name=name,
    )
    return lambda *operands: run(*after, *operands)


def whole(*shape):
    return pl.BlockSpec(shape, lambda i: (0,) * len(shape))


def band(rows, cols):
    return pl.BlockSpec((rows, cols), lambda i: (i, 0))


ANY = pl.BlockSpec(memory_space=pl.ANY)
SCALARS = pl.BlockSpec(memory_space=pltpu.SMEM)


def struct(shape, dtype):
    return jax.ShapeDtypeStruct(shape, dtype)


def rotary_tables(rows):
    lane = np.arange(2 * HEAD_DIM) % HEAD_DIM
    pair = (lane % (ROT // 2)).astype(np.float32)
    inverse = np.exp(pair * np.float32(-2.0 * math.log(10000.0) / ROT)).astype(np.float32)
    phase = np.arange(rows, dtype=np.float32)[:, None] * inverse[None, :]
    turned = (lane < ROT)[None, :]
    sign = np.where(lane < ROT // 2, -1.0, 1.0)[None, :]
    cosine = np.where(turned, np.cos(phase), 1.0).astype(np.float32)
    sine = np.where(turned, np.sin(phase) * sign, 0.0).astype(np.float32)
    return (cosine, sine)


def turn(values, cosine, sine):
    lane = lax.broadcasted_iota(jnp.int32, values.shape, 1) % HEAD_DIM
    width = values.shape[1]
    half = ROT // 2
    partner = jnp.where(
        lane < half, pltpu.roll(values, width - half, 1), pltpu.roll(values, half, 1)
    )
    return values * cosine + partner * sine


def norm_up_kernel(
    tokens_ref, gain_ref, shift_ref, bias_ref, weight_ref, normed_ref, stats_ref, low_ref, slope_ref
):
    parts = [tokens_ref[0, j].astype(jnp.float32) for j in range(tokens_ref.shape[1])]
    rows, width = parts[0].shape
    total = sum(jnp.sum(part, axis=1, keepdims=True) for part in parts)
    squares = sum(jnp.sum(part * part, axis=1, keepdims=True) for part in parts)
    mean = total / D
    inverse_std = lax.rsqrt(squares / D - mean * mean + EPSILON)
    up_input = bias_ref[...]
    for j, part in enumerate(parts):
        cols = slice(j * width, (j + 1) * width)
        standard = (part - mean) * inverse_std
        normed = (standard * gain_ref[:, cols] + shift_ref[:, cols]).astype(jnp.bfloat16)
        normed_ref[:, cols] = normed
        up_input = up_input + matmul(normed, weight_rows_of(weight_ref, j * width, width))
    stats_ref[...] = jnp.concatenate(
        [jnp.broadcast_to(mean, (rows, 64)), jnp.broadcast_to(inverse_std, (rows, 64))], axis=1
    )
    root = math.sqrt(2.0 / math.pi)
    square = up_input * up_input
    bend = jnp.tanh(root * (up_input + 0.044715 * square * up_input))
    half = 0.5 * (1.0 + bend)
    low_ref[...] = (up_input * half).astype(jnp.bfloat16)
    slope_ref[...] = half + 0.5 * up_input * (1.0 - bend * bend) * (
        root * (1.0 + 3 * 0.044715 * square)
    )


class Weight:
    def __init__(self, array, rows, start, width):
        self.array, self.rows, self.width = array, rows, width
        self.spec = pl.BlockSpec(
            array.shape[:-2] + (rows, width),
            lambda *_: (0,) * (len(array.shape) - 1) + (start // width,),
        )


def weight_rows_of(weight_ref, start, count):
    _, rows, width = weight_ref.shape
    return weight_ref[pl.ds(start // rows, count // rows)].reshape(count, width)


def norm_up(blocks, gain, shift, bias, weight, rows=256, after=()):
    row_blocks, col_blocks, row_count, width = blocks.shape
    total, hidden = row_blocks * row_count, bias.shape[1]
    per = row_count // rows
    spec = pl.BlockSpec((1, col_blocks, rows, width), lambda i: (i // per, 0, i % per, 0))
    return call(
        norm_up_kernel,
        "norm_up",
        (total // rows,),
        [spec]
        + [whole(1, D), whole(1, D), whole(1, hidden), weight.spec],
        [band(rows, D), band(rows, 128), band(rows, hidden), band(rows, hidden)],
        [
            struct((total, D), jnp.bfloat16),
            struct((total, 128), jnp.float32),
            struct((total, hidden), jnp.bfloat16),
            struct((total, hidden), jnp.float32),
        ],
        flops=6 * total * D * hidden,
        after=after,
    )(blocks, gain, shift, bias, weight.array)


def heads_kernel(normed_ref, bias_ref, cosine_ref, sine_ref, weight_ref, heads_ref):
    pre = matmul(normed_ref[...], weight_rows_of(weight_ref, 0, D)) + bias_ref[...]
    lanes = 2 * HEAD_DIM
    cosine, sine = cosine_ref[...], sine_ref[...]
    factor = 1.0 / math.sqrt(HEAD_DIM)
    heads_ref[:, :lanes] = (turn(pre[:, :lanes], cosine, sine) * factor).astype(jnp.bfloat16)
    heads_ref[:, lanes : 2 * lanes] = turn(pre[:, lanes : 2 * lanes], cosine, sine).astype(
        jnp.bfloat16
    )
    heads_ref[:, 2 * lanes :] = pre[:, 2 * lanes :].astype(jnp.bfloat16)


def project_heads(normed, bias, weight, rows=512, after=()):
    total, width = normed.shape[0], bias.shape[1]
    cosine, sine = rotary_tables(total)
    lanes = 2 * HEAD_DIM
    return call(
        heads_kernel,
        "project_heads",
        (total // rows,),
        [band(rows, D), whole(1, width), band(rows, lanes), band(rows, lanes)]
        + [weight.spec],
        band(rows, width),
        struct((total, width), jnp.bfloat16),
        flops=4 * total * D * width,
        after=after,
    )(normed, bias, jnp.asarray(cosine), jnp.asarray(sine), weight.array)


def cot_spec(cot, rows):
    row_count, width = cot.shape[-2:]
    per = row_count // rows
    return pl.BlockSpec(
        (1, 4, 1, rows, width), lambda i: (i // per % 2, 0, i // per // 2, i % per, 0)
    )


def cot_product(cot_ref, weight_ref):
    width = cot_ref.shape[4]
    total = 0.0
    for j in range(4):
        part = cot_ref[0, j, 0]
        total = total + matmul(part, weight_rows_of(weight_ref, j * width, width))
    return total


def out_grad_kernel(cot_ref, weight_ref, out_ref):
    out_ref[...] = cot_product(cot_ref, weight_ref).astype(jnp.bfloat16)


def attended_gradient(cot, weight, width, rows=512, after=()):
    total = 4 * cot.shape[3]
    return call(
        out_grad_kernel,
        "attended_gradient",
        (total // rows,),
        [cot_spec(cot, rows), weight.spec],
        band(rows, width),
        struct((total, width), jnp.bfloat16),
        flops=8 * total * D * width,
        after=after,
    )(cot, weight.array)


def up_grad_kernel(cot_ref, slope_ref, weight_ref, up_ref, sums_ref):
    @pl.when(pl.program_id(0) == 0)
    def _():
        sums_ref[...] = jnp.zeros_like(sums_ref)

    up = (cot_product(cot_ref, weight_ref) * slope_ref[...]).astype(jnp.bfloat16)
    up_ref[...] = up
    sums_ref[...] += jnp.sum(up.astype(jnp.float32), axis=0, keepdims=True)


def up_gradient(cot, slope, weight, rows=512, after=()):
    total, hidden = slope.shape
    return call(
        up_grad_kernel,
        "up_gradient",
        (total // rows,),
        [cot_spec(cot, rows), band(rows, hidden), weight.spec],
        [band(rows, hidden), whole(1, hidden)],
        [struct((total, hidden), jnp.bfloat16), struct((1, hidden), jnp.float32)],
        flops=4 * total * D * hidden,
        after=after,
    )(cot, slope, weight.array)


def rows_of(index, size):
    return pl.ds(pl.multiple_of(index * size, size), size)


HEADS_HERE = [slice(n * HEAD_DIM, (n + 1) * HEAD_DIM) for n in range(2)]


def turned_into(ref, source_ref, cols):
    chunk = 256

    def one(b, carry):
        rows = rows_of(b, chunk)
        ref[:, rows] = source_ref[rows, cols].T
        return carry

    lax.fori_loop(0, source_ref.shape[0] // chunk, one, 0)


def causal_block(block):
    return lax.broadcasted_iota(jnp.int32, (block, block), 0) <= lax.broadcasted_iota(
        jnp.int32, (block, block), 1
    )


def fold_rows(values, combine):
    rows, cols = values.shape
    return combine(values.reshape(rows // 8, 8, cols), axis=0)


def attention_kernel(block, qkv_ref, attended_ref, log_sums_ref, qt_ref, vt_ref, score_ref):
    i = pl.program_id(0)
    width = 2 * HEAD_DIM

    @pl.when(i == 0)
    def _():
        turned_into(qt_ref, qkv_ref, slice(0, width))
        turned_into(vt_ref, qkv_ref, slice(2 * width, 3 * width))
        log_sums_ref[...] = jnp.zeros_like(log_sums_ref)

    own = rows_of(i, block)
    causal = causal_block(block)

    def score(j, best, diagonal):
        rows = rows_of(j, block)
        new = []
        for n, head in enumerate(HEADS_HERE):
            start = width + n * HEAD_DIM
            part = matmul(qkv_ref[rows, start : start + HEAD_DIM], qt_ref[head, own])
            if diagonal:
                part = jnp.where(causal, part, -1e30)
            score_ref[n, j] = part
            new.append(jnp.maximum(best[n], fold_rows(part, jnp.max)))
        return tuple(new)

    low = jnp.full((8, block), -1e30, jnp.float32)
    best = lax.fori_loop(0, i, lambda j, b: score(j, b, False), (low, low))
    best = score(i, best, True)
    top = [jnp.max(value, axis=0, keepdims=True) for value in best]

    def weigh(j, carry):
        new = []
        for n in range(2):
            weights = jnp.exp(score_ref[n, j] - top[n])
            score_ref[n, j] = weights
            new.append(carry[n] + fold_rows(weights, jnp.sum))
        return tuple(new)

    zero = jnp.zeros((8, block), jnp.float32)
    totals = lax.fori_loop(0, i + 1, weigh, (zero, zero))
    totals = [jnp.sum(total, axis=0, keepdims=True) for total in totals]
    scales = [1.0 / total for total in totals]
    for n in range(2):
        log_sums_ref[n : n + 1, own] = top[n] + jnp.log(totals[n])

    def push(j, carry):
        rows = rows_of(j, block)
        new = []
        for n, head in enumerate(HEADS_HERE):
            probs = (score_ref[n, j] * scales[n]).astype(jnp.bfloat16)
            new.append(carry[n] + matmul(vt_ref[head, rows], probs))
        return tuple(new)

    zero = jnp.zeros((HEAD_DIM, block), jnp.float32)
    out = lax.fori_loop(0, i + 1, push, (zero, zero))
    attended_ref[own, :] = jnp.concatenate(out, axis=0).T.astype(jnp.bfloat16)


def attention(qkv, block=512, after=()):
    rows, width = qkv.shape[0], 2 * HEAD_DIM
    blocks = rows // block
    return call(
        partial(attention_kernel, block),
        "attention",
        (blocks,),
        [whole(rows, 3 * width)],
        [whole(rows, width), whole(8, rows)],
        [struct((rows, width), jnp.bfloat16), struct((8, rows), jnp.float32)],
        [pltpu.VMEM((width, rows), jnp.bfloat16)] * 2
        + [pltpu.VMEM((2, blocks, block, block), jnp.float32)],
        flops=10 * 10**9,
        after=after,
    )(qkv)


def attention_back_kernel(
    blocks,
    block,
    qkv_ref,
    grad_ref,
    log_sums_ref,
    cosine_ref,
    sine_ref,
    pre_grad_ref,
    sums_ref,
    qt_ref,
    kt_ref,
    gt_ref,
    prob_ref,
    slope_ref,
    k_total,
    v_total,
):
    i = pl.program_id(0)
    width = 2 * HEAD_DIM
    factor = 1.0 / math.sqrt(HEAD_DIM)
    chunk = 256

    @pl.when(i == 0)
    def _():
        turned_into(qt_ref, qkv_ref, slice(0, width))
        turned_into(kt_ref, qkv_ref, slice(width, 2 * width))
        turned_into(gt_ref, grad_ref, slice(0, width))
        k_total[...] = jnp.zeros_like(k_total)
        v_total[...] = jnp.zeros_like(v_total)
        sums_ref[...] = jnp.zeros_like(sums_ref)

    own = rows_of(i, block)
    causal = causal_block(block)
    log_sums = [log_sums_ref[n : n + 1, own] for n in range(2)]

    def weigh(j, carry, diagonal):
        rows = rows_of(j, block)
        new = []
        for n, head in enumerate(HEADS_HERE):
            start = width + n * HEAD_DIM
            scores = matmul(qkv_ref[rows, start : start + HEAD_DIM], qt_ref[head, own])
            probs = jnp.exp(scores - log_sums[n])
            if diagonal:
                probs = jnp.where(causal, probs, 0.0)
            start += width
            slope = matmul(qkv_ref[rows, start : start + HEAD_DIM], gt_ref[head, own])
            prob_ref[n, j] = probs
            slope_ref[n, j] = slope
            new.append(carry[n] + fold_rows(probs * slope, jnp.sum))
        return tuple(new)

    zero = jnp.zeros((8, block), jnp.float32)
    dots = lax.fori_loop(0, i, lambda j, c: weigh(j, c, False), (zero, zero))
    dots = weigh(i, dots, True)
    dots = [jnp.sum(dot, axis=0, keepdims=True) for dot in dots]

    def push(j, carry):
        rows = rows_of(j, block)
        new = []
        for n, head in enumerate(HEADS_HERE):
            probs = prob_ref[n, j]
            score_grad = (probs * (slope_ref[n, j] - dots[n])).astype(jnp.bfloat16)
            k_total[rows, head] += matmul(score_grad, qkv_ref[own, head])
            v_total[rows, head] += matmul(probs.astype(jnp.bfloat16), grad_ref[own, head])
            new.append(carry[n] + matmul(kt_ref[head, rows], score_grad))
        return tuple(new)

    zero = jnp.zeros((HEAD_DIM, block), jnp.float32)
    q_grad = lax.fori_loop(0, i + 1, push, (zero, zero))
    q_grad = jnp.concatenate(q_grad, axis=0).T * factor
    q_pre = turn(q_grad, cosine_ref[own, :], -sine_ref[own, :]).astype(jnp.bfloat16)
    pre_grad_ref[own, :width] = q_pre
    sums_ref[:, :width] += jnp.sum(q_pre.astype(jnp.float32), axis=0, keepdims=True)

    @pl.when(i == blocks - 1)
    def _():
        def finish(b, carry):
            rows = rows_of(b, chunk)
            k_pre = turn(k_total[rows, :], cosine_ref[rows, :], -sine_ref[rows, :])
            k_pre = k_pre.astype(jnp.bfloat16)
            v_pre = v_total[rows, :].astype(jnp.bfloat16)
            pre_grad_ref[rows, width : 2 * width] = k_pre
            pre_grad_ref[rows, 2 * width :] = v_pre
            both = jnp.concatenate([k_pre, v_pre], axis=1).astype(jnp.float32)
            return carry + jnp.sum(both, axis=0, keepdims=True)

        sums_ref[:, width:] = lax.fori_loop(
            0, qkv_ref.shape[0] // chunk, finish, jnp.zeros((1, 2 * width), jnp.float32)
        )


def attention_back(qkv, out_grad, log_sums, block=512, after=()):
    rows, width = qkv.shape[0], 2 * HEAD_DIM
    blocks = rows // block
    cosine, sine = rotary_tables(rows)
    return call(
        partial(attention_back_kernel, blocks, block),
        "attention_back",
        (blocks,),
        [whole(rows, 3 * width), whole(rows, width), whole(8, rows)]
        + [whole(rows, width), whole(rows, width)],
        [whole(rows, 3 * width), whole(1, 3 * width)],
        [struct((rows, 3 * width), jnp.bfloat16), struct((1, 3 * width), jnp.float32)],
        [pltpu.VMEM((width, rows), jnp.bfloat16)] * 3
        + [pltpu.VMEM((2, blocks, block, block), jnp.float32)] * 2
        + [pltpu.VMEM((rows, width), jnp.float32)] * 2,
        flops=20 * 10**9,
        after=after,
    )(qkv, out_grad, log_sums, jnp.asarray(cosine), jnp.asarray(sine))


def weight_grad_kernel(riders, *refs):
    out_ref, refs = refs[-1], refs[:-1]
    if riders:
        height = out_ref.shape[1] - refs[0].shape[1]
        out_ref[:, height:, :] = refs[0][...]
        refs = refs[1:]
    cols = out_ref.shape[2]
    start = 0
    for left_ref, right_ref in zip(refs[::2], refs[1::2]):
        if len(right_ref.shape) == 5:
            size = right_ref.shape[3]
            part = 0.0
            for b in range(4):
                rows = slice(b * size, (b + 1) * size)
                part = part + contract_rows(left_ref[rows, :], right_ref[b % 2, 0, b // 2])
        else:
            part = contract_rows(left_ref[...], right_ref[...])
        part = part.astype(jnp.bfloat16)
        stop = start + part.shape[0]
        for n in range(out_ref.shape[0]):
            out_ref[n, start:stop, :] = part[:, n * cols : (n + 1) * cols]
        start = stop


def weight_grad(pairs, parts, rider=None, after=()):
    cols = D // parts
    per = parts // 4
    rows = pairs[0][0].shape[0]
    height = sum(left.shape[1] for left, _ in pairs)
    in_specs, operands = [], []
    if rider is not None:
        in_specs.append(pl.BlockSpec((per,) + rider.shape[1:], lambda i: (i, 0, 0)))
        operands.append(rider)
        height += rider.shape[1]
    for left, right in pairs:
        in_specs.append(whole(*left.shape))
        if right.ndim == 5:
            in_specs.append(
                pl.BlockSpec((2, 1, 2, right.shape[3], D // 4), lambda i: (0, i, 0, 0, 0))
            )
        else:
            in_specs.append(pl.BlockSpec((rows, D // 4), lambda i: (0, i)))
        operands += [left, right]
    return call(
        partial(weight_grad_kernel, rider is not None),
        "weight_grad",
        (4,),
        in_specs,
        pl.BlockSpec((per, height, cols), lambda i: (i, 0, 0)),
        struct((parts, height, cols), jnp.bfloat16),
        flops=4 * rows * height * D,
        after=after,
    )(*operands)


def partial_sum_kernel(sides, axes, index_ref, *refs):
    lefts, refs = refs[: 2 * sides], refs[2 * sides :]
    weights, others, outs = refs[:sides], refs[sides : 2 * sides], refs[2 * sides :]
    rows, width = outs[0].shape[-2:]
    own_m, own_h, core = index_ref[0], index_ref[1], index_ref[2]
    here = lax.rem(pl.program_id(0), 2) == own_h
    for n_m, m in enumerate((own_m, 1 - own_m)):
        out = 0.0
        for n in range(sides):
            weight = weight_rows_of(weights[n], (2 * m + core) * width, width)
            out = out + contract_cols(lefts[n][...], weight)
            other = others[n][m].reshape(width, weight.shape[1])
            out = out + contract_cols(lefts[sides + n][...], other)
        out = out.astype(jnp.bfloat16)
        for half, axis in enumerate(axes):
            part = out[half * rows : (half + 1) * rows]
            if axis == "m":
                outs[2 * half + n_m][0] = part
                continue
            for n_h, mine in enumerate((here, jnp.logical_not(here))):

                @pl.when(mine)
                def _(out_ref=outs[2 * half + n_h], m=m, part=part):
                    out_ref[0, m] = part


def partial_sum(sides, row_count, width, name, axes, after=()):
    total = sides[0][0].shape[0]
    rows = row_count // len(axes)
    blocks = total // row_count
    lefts = [side[0] for side in sides] + [side[1] for side in sides]
    weights = [side[2] for side in sides]
    others = [side[3] for side in sides]
    depth = sum(left.shape[1] for left in lefts)
    specs, shapes = [], []
    for axis in axes:
        if axis == "m":
            specs += [pl.BlockSpec((1, rows, width), lambda i: (i, 0, 0))] * 2
            shapes += [struct((blocks, rows, width), jnp.bfloat16)] * 2
        else:
            specs += [pl.BlockSpec((1, 2, rows, width), lambda i: (i // 2, 0, 0, 0))] * 2
            shapes += [struct((blocks // 2, 2, rows, width), jnp.bfloat16)] * 2
    index = jnp.stack([lax.axis_index(axis) for axis in "mhc"]).astype(jnp.int32)
    return call(
        partial(partial_sum_kernel, len(sides), axes),
        name,
        (blocks,),
        [SCALARS]
        + [band(row_count, left.shape[1]) for left in lefts]
        + [weight.spec for weight in weights]
        + [other.spec for other in others],
        specs,
        shapes,
        flops=2 * total * depth * D,
        after=after,
    )(index, *lefts, *[weight.array for weight in weights], *[other.array for other in others])


def switch_specs(count, block):
    zeros = (0,) * (len(block) - 1)
    return [
        pl.BlockSpec(block, lambda k, j, p: (j + k * (count - 1 - j),) + zeros),
        pl.BlockSpec(block, lambda k, j, p: (j * k,) + zeros),
    ]


def prefetch_call(kernel, name, index, grid, in_specs, out_specs, out_shape, after=()):
    skipped = len(after)

    def ordered(index_ref, *refs):
        kernel(index_ref, *refs[skipped:])

    run = pl.pallas_call(
        ordered,
        grid_spec=pltpu.PrefetchScalarGridSpec(
            num_scalar_prefetch=1,
            grid=grid,
            in_specs=[ANY] * skipped + list(in_specs),
            out_specs=out_specs,
        ),
        out_shape=out_shape,
        compiler_params=pltpu.CompilerParams(vmem_limit_bytes=VMEM_LIMIT),
        cost_estimate=pl.CostEstimate(flops=0, bytes_accessed=0, transcendentals=0),
        name=name,
    )
    return lambda *operands: run(index.astype(jnp.int32).reshape(1), *after, *operands)


def column_specs(shards, turned, block):
    specs, width = [], 0
    for flip, shard in zip(turned, shards):
        height, cols = shard.shape
        if flip:
            specs.append(pl.BlockSpec((height // 4, cols), lambda *at: (block(*at), 0)))
            rows, width = cols, width + height // 4
        else:
            specs.append(pl.BlockSpec((height, cols // 4), lambda *at: (0, block(*at))))
            rows, width = height, width + cols // 4
    return specs, rows, width


def write_columns(turned, refs, store):
    start = 0
    for flip, ref in zip(turned, refs):
        part = ref[...].T if flip else ref[...]
        store(slice(start, start + part.shape[1]), part)
        start += part.shape[1]


def pack_kernel(turned, rows, riders, *refs):
    out_ref, refs = refs[-1], refs[:-1]
    if riders:
        rider, refs = refs[0][...], refs[1:]

    def store(cols, part):
        for n in range(out_ref.shape[0]):
            out_ref[n, 0, :rows, cols] = part

    write_columns(turned, refs, store)
    if riders:
        for n in range(out_ref.shape[0]):
            out_ref[n, 0, rows:, :] = rider


def packed(shards, turned, rider=None):
    wide = lax.axis_size(WIDE)
    specs, rows, width = column_specs(shards, turned, lambda i: i)
    height = rows
    if rider is not None:
        specs = [whole(*rider.shape)] + specs
        shards = [rider] + shards
        height += rider.shape[0]
    blocks = call(
        partial(pack_kernel, turned, rows, rider is not None),
        "pack",
        (4,),
        specs,
        pl.BlockSpec((wide // 4, 1, height, width), lambda i: (0, i, 0, 0)),
        struct((wide // 4, 4, height, width), jnp.bfloat16),
    )(*shards)
    return blocks.reshape(wide, height, width)


def exchanged(blocks, after=()):
    blocks = lax.optimization_barrier((blocks, *after))[0]
    return lax.all_to_all(blocks, WIDE, 0, 0)


def sides_kernel(turned, index_ref, *refs):
    for out_ref, blocks in zip(refs[-2:], (refs[:-2][::2], refs[:-2][1::2])):

        def store(cols, part, out_ref=out_ref):
            out_ref[0, :, cols] = part

        write_columns(turned, blocks, store)


def packed_sides(shards, turned):
    specs, operands, width = [], [], 0
    for flip, shard in zip(turned, shards):
        height, cols = shard.shape
        if flip:
            rows, width = cols, width + height // 4
            shape, at = (height // 4, cols), lambda block: (block, 0)
        else:
            rows, width = height, width + cols // 4
            shape, at = (height, cols // 4), lambda block: (0, block)
        specs.append(pl.BlockSpec(shape, lambda j, p, at=at: at(2 * j + p[0])))
        specs.append(pl.BlockSpec(shape, lambda j, p, at=at: at(2 * j + 1 - p[0])))
        operands += [shard, shard]
    return prefetch_call(
        partial(sides_kernel, turned),
        "pack",
        lax.axis_index("h"),
        (2,),
        specs,
        [pl.BlockSpec((1, rows, width), lambda j, p: (j, 0, 0))] * 2,
        [struct((2, rows, width), jnp.bfloat16)] * 2,
    )(*operands)


def spread_kernel(index_ref, mine_ref, other_ref, out_ref):
    for n in range(out_ref.shape[0]):
        out_ref[n, 0, index_ref[0]] = mine_ref[0]
        out_ref[n, 0, 1 - index_ref[0]] = other_ref[0]


def spread_sides(sides, after=()):
    mine, send = sides
    sequences = lax.axis_size("s")
    _, rows, width = mine.shape
    spec = pl.BlockSpec((1, rows, width), lambda j, p: (j, 0, 0))
    blocks = prefetch_call(
        spread_kernel,
        "spread",
        lax.axis_index("h"),
        (2,),
        [spec, spec],
        pl.BlockSpec((sequences, 1, 2, rows, width), lambda j, p: (0, j, 0, 0, 0)),
        struct((sequences, 2, 2, rows, width), jnp.bfloat16),
        after=after,
    )(mine, shifted(send, "h", 1))
    return blocks.reshape(2 * sequences, 2 * rows, width)


def exchanged_along_line(blocks):
    count, rows, width = blocks.shape
    return lax.all_to_all(blocks, LINE, 0, 0).reshape(2 * count, rows // 2, width)


def unpack_kernel(turned, arrived_ref, *outs):
    total = arrived_ref[0, 0].astype(jnp.float32)
    for n in range(1, arrived_ref.shape[0]):
        total = total + arrived_ref[n, 0].astype(jnp.float32)
    start = 0
    for flip, out_ref in zip(turned, outs):
        height = out_ref.shape[0] if flip else out_ref.shape[1]
        part = total[start : start + height]
        out_ref[...] = part if flip else part.T
        start += height


def scatter_columns(grad, heights, turned, after=()):
    sequences = lax.axis_size("s")
    _, height, rows = grad.shape
    arrived = lax.all_to_all(grad, WIDE, 0, 0)
    riders = arrived[:, sum(heights) :]
    arrived = arrived.reshape(sequences, 4, height, rows)
    height = sum(heights)
    specs, shapes = [], []
    for flip, part in zip(turned, heights):
        if flip:
            specs.append(pl.BlockSpec((part, rows), lambda i: (i, 0)))
            shapes.append(struct((4 * part, rows), jnp.float32))
        else:
            specs.append(pl.BlockSpec((rows, part), lambda i: (0, i)))
            shapes.append(struct((rows, 4 * part), jnp.float32))
    shards = call(
        partial(unpack_kernel, turned),
        "unpack",
        (4,),
        [pl.BlockSpec((sequences, 1, height, rows), lambda i: (0, i, 0, 0))],
        specs,
        shapes,
        after=after,
    )(arrived)
    return shards, riders


def side_sums_kernel(index_ref, arrived_ref, keep_ref, send_ref):
    for out_ref, side in ((keep_ref, index_ref[0]), (send_ref, 1 - index_ref[0])):
        total = arrived_ref[0, 0, side].astype(jnp.float32)
        for n in range(1, arrived_ref.shape[0]):
            total = total + arrived_ref[n, 0, side].astype(jnp.float32)
        out_ref[0] = total.astype(out_ref.dtype)


def unpack_sides_kernel(turned, index_ref, keep_ref, other_ref, *outs):
    def write(total):
        start = 0
        for flip, out_ref in zip(turned, outs):
            height = out_ref.shape[0] if flip else out_ref.shape[1]
            part = total[start : start + height]
            out_ref[...] = part if flip else part.T
            start += height

    @pl.when(pl.program_id(1) == 0)
    def _():
        write(keep_ref[0])

    @pl.when(pl.program_id(1) == 1)
    def _():
        write(other_ref[0].astype(jnp.float32))


def scatter_along_line(grad, heights, turned, after=(), late_after=()):
    sequences, side = lax.axis_size("s"), lax.axis_index("h")
    wide, height, rows = grad.shape
    arrived = lax.all_to_all(grad.reshape(wide // 2, 2 * height, rows), LINE, 0, 0)
    band_of = pl.BlockSpec((1, height, rows), lambda j, p: (j, 0, 0))
    keep, send = prefetch_call(
        side_sums_kernel,
        "side_sums",
        side,
        (2,),
        [pl.BlockSpec((sequences, 1, 2, height, rows), lambda j, p: (0, j, 0, 0, 0))],
        [band_of, band_of],
        [struct((2, height, rows), jnp.float32), struct((2, height, rows), jnp.bfloat16)],
        after=after,
    )(arrived.reshape(sequences, 2, 2, height, rows))
    other = shifted(send, "h", 1)
    riders = keep[:, sum(heights) :] + other[:, sum(heights) :].astype(jnp.float32)
    specs, shapes = [], []
    block = lambda j, n, p: 2 * j + p[0] + n - 2 * n * p[0]
    for flip, part in zip(turned, heights):
        if flip:
            specs.append(pl.BlockSpec((part, rows), lambda j, n, p: (block(j, n, p), 0)))
            shapes.append(struct((4 * part, rows), jnp.float32))
        else:
            specs.append(pl.BlockSpec((rows, part), lambda j, n, p: (0, block(j, n, p))))
            shapes.append(struct((rows, 4 * part), jnp.float32))
    part_of = pl.BlockSpec((1, sum(heights), rows), lambda j, n, p: (j, 0, 0))
    shards = prefetch_call(
        partial(unpack_sides_kernel, turned),
        "unpack",
        side,
        (2, 2),
        [part_of, part_of],
        specs,
        shapes,
        after=late_after,
    )(keep, other)
    return shards, riders


def fold_kernel(index_ref, mine_keep, mine_send, arrived_keep, arrived_send, keep_ref, send_ref):
    keep_ref[...] = mine_keep[...] + arrived_keep[...]
    send_ref[...] = mine_send[...] + arrived_send[...]


def folded(mine, arrived, axes, axis, after=()):
    position = axes.index(axis)
    high, low = 2**position, 2 ** (len(axes) - 1 - position)
    rows, cols = mine.shape[-2:]
    shape = (high, 2, low * rows, cols)
    steps = 2 if low > 1 else 1
    block = low * rows // steps
    halves = [
        pl.BlockSpec((high, None, block, cols), lambda j, p: (0, p[0], j, 0)),
        pl.BlockSpec((high, None, block, cols), lambda j, p: (0, 1 - p[0], j, 0)),
    ]
    out = pl.BlockSpec((high, block, cols), lambda j, p: (0, j, 0))
    mine, arrived = mine.reshape(shape), arrived.reshape(shape)
    keep, send = prefetch_call(
        fold_kernel,
        "fold",
        lax.axis_index(axis),
        (steps,),
        halves * 2,
        [out, out],
        [struct((high, low * rows, cols), jnp.bfloat16)] * 2,
        after=after,
    )(mine, mine, arrived, arrived)
    return [part.reshape(high * low, rows, cols) for part in (keep, send)]


def join_kernel(index_ref, mine_ref, other_ref, out_ref):
    out_ref[index_ref[0]] = mine_ref[...]
    out_ref[1 - index_ref[0]] = other_ref[...]


def joined(mine, other, axis, after=()):
    rows, cols = mine.size // mine.shape[-1] // 2, mine.shape[-1]
    spec = pl.BlockSpec((rows, cols), lambda j, p: (j, 0))
    out = prefetch_call(
        join_kernel,
        "join",
        lax.axis_index(axis),
        (2,),
        [spec, spec],
        pl.BlockSpec((2, rows, cols), lambda j, p: (0, j, 0)),
        struct((2, 2 * rows, cols), mine.dtype),
        after=after,
    )(mine.reshape(2 * rows, cols), other.reshape(2 * rows, cols))
    return out.reshape((2,) + mine.shape)


def finish_kernel(tokens_ref, *refs):
    bias_ref, out_ref = refs[-2:]
    parts = len(refs) // 2 - 1
    rows = refs[0].shape[0]
    for n, (keep_ref, arrived_ref) in enumerate(zip(refs[:parts], refs[parts : 2 * parts])):
        at = slice(n * rows, (n + 1) * rows)
        total = tokens_ref[at, :].astype(jnp.float32) + keep_ref[...].astype(jnp.float32)
        total = total + arrived_ref[...].astype(jnp.float32) + bias_ref[...]
        out_ref[at, :] = total.astype(jnp.bfloat16)


def finished(tokens, keep, arrived, bias, after=()):
    operands = [tokens, *keep, *arrived, bias]
    return call(
        finish_kernel,
        "finish",
        (1,),
        [whole(*operand.shape) for operand in operands],
        whole(*tokens.shape),
        struct(tokens.shape, tokens.dtype),
        after=after,
    )(*operands)


def gather_narrow(value):
    for axis in ("c", "m"):
        other = shifted(value, axis, 1)
        value = jnp.stack(in_order(value, other, lax.axis_index(axis)))
    return value.reshape((4,) + value.shape[2:])


def summed(value, axis):
    total = value
    for step in range(1, lax.axis_size(axis)):
        total = total + shifted(value, axis, step)
    return total


def body(
    tokens,
    cotangent,
    ln_gain,
    ln_shift,
    w_query,
    b_query,
    w_key,
    b_key,
    w_value,
    b_value,
    w_dense,
    b_dense,
    w_fc1,
    b_fc1,
    w_fc2,
    b_fc2,
):
    row_count, feature_count = tokens.shape
    own_g, own_h = lax.axis_index("g"), lax.axis_index("h")
    own_n = lax.axis_index(NARROW)
    quarter = 2 * own_g + own_h
    wide = lax.axis_size(WIDE)
    weight_rows = w_fc1.shape[0]
    lanes = w_query.shape[1] // 4

    vectors = (ln_gain, ln_shift, b_query, b_key, b_value, b_dense, b_fc2, b_fc1)
    lengths = [vector.shape[0] for vector in vectors]
    hidden = w_fc1.shape[1] // 4
    rider = jnp.concatenate(vectors)
    rider = jnp.pad(rider, (0, 16 * hidden - rider.shape[0])).reshape(16, hidden)

    tokens_full = lax.all_gather(tokens, CUBE, axis=0, tiled=False)
    tokens_full = tokens_full.reshape(4, 4, row_count, feature_count)
    up_blocks = packed([w_fc1], [False], rider)
    head_sides = packed_sides(
        [w_query, w_key, w_value, w_dense], [False, False, False, True]
    )
    down_sides = packed_sides([w_fc2], [True])
    other = shifted(cotangent, "g", 1)
    arrived = exchanged(up_blocks, after=[other])
    cot = joined(cotangent, other, "g", after=[up_blocks, head_sides[0], down_sides[0]])
    cot = lax.all_gather(cot, ("h", "m", "c"), axis=0, tiled=False)
    cot = cot.reshape(2, 4, 2, row_count, feature_count)
    head_blocks = spread_sides(head_sides, after=[arrived])
    head_arrived = exchanged_along_line(head_blocks)
    up_weight = Weight(arrived, weight_rows, 0, hidden)
    qkv_weight = Weight(head_arrived, weight_rows, 0, 3 * lanes)
    dense_weight = Weight(head_arrived, weight_rows, 3 * lanes, lanes)

    def from_other_core(array):
        split = array[:, :weight_rows].reshape(2, 2, wide // 4, weight_rows, -1)
        return shifted(pick(split, 1 - lax.axis_index("c"), 1), "c", 1)

    up_other = Weight(from_other_core(arrived), weight_rows, 0, hidden)
    head_other = from_other_core(head_arrived)
    qkv_other = Weight(head_other, weight_rows, 0, 3 * lanes)
    dense_other = Weight(head_other, weight_rows, 3 * lanes, lanes)

    here = arrived[:, weight_rows:].reshape(wide, 16 * hidden)
    local, start = [], 0
    for length in lengths:
        local.append(here[:, start : start + length].astype(jnp.float32).reshape(-1))
        start += length
    shared = gather_narrow(here[:, : 2 * lengths[0]].astype(jnp.float32))
    gain = shared[:, :, : lengths[0]].reshape(1, D)
    shift = shared[:, :, lengths[0] :].reshape(1, D)

    def quarter_of(vector):
        return pick(vector.reshape(4, -1), quarter)

    qkv_bias = jnp.concatenate([quarter_of(vector) for vector in local[2:5]]).reshape(1, -1)
    up_bias = quarter_of(local[7]).reshape(1, -1)
    own_gain, out_bias = local[0], local[5] + local[6]

    normed, stats, up_low, up_slope = norm_up(
        tokens_full, gain, shift, up_bias, up_weight, after=[up_other.array]
    )
    down_blocks = spread_sides(down_sides, after=[normed])
    down_arrived = exchanged_along_line(down_blocks)
    down_weight = Weight(down_arrived, weight_rows, 0, hidden)
    qkv = project_heads(normed, qkv_bias, qkv_weight, after=[head_other])
    attended, log_sums = attention(qkv)
    grad_down = weight_grad([(up_low, cot)], wide, after=[attended])
    attended_grad = attended_gradient(cot, dense_weight, lanes, after=[grad_down])
    grad_down = lax.optimization_barrier((grad_down, attended_grad))[0]
    up_grad, up_sums = up_gradient(cot, up_slope, down_weight, after=[attended_grad])
    qkv_grad, qkv_sums = attention_back(qkv, attended_grad, log_sums, after=[up_grad])
    qkv_grad_other = shifted(qkv_grad, "c", 1)

    grad_up = weight_grad([(up_grad, normed)], wide, after=[qkv_grad])
    up_grad_other = shifted(up_grad, "c", 1)
    grad_up = lax.optimization_barrier((grad_up, qkv_grad_other, up_grad_other))[0]
    normed_grad = partial_sum(
        [
            (qkv_grad, qkv_grad_other, qkv_weight, qkv_other),
            (up_grad, up_grad_other, up_weight, up_other),
        ],
        row_count,
        feature_count,
        "normed_gradient",
        "mh",
        after=[grad_up],
    )

    down_other = lax.optimization_barrier((down_arrived, normed_grad[0]))[0]
    down_other = Weight(from_other_core(down_other), weight_rows, 0, hidden)
    branch = partial_sum(
        [
            (attended, shifted(attended, "c", 1), dense_weight, dense_other),
            (up_low, shifted(up_low, "c", 1), down_weight, down_other),
        ],
        row_count,
        feature_count,
        "branch_sum",
        "mm",
        after=normed_grad[:1],
    )
    def spread(vector):
        placed = jnp.zeros((4, vector.shape[0]), jnp.float32)
        placed = lax.dynamic_update_index_in_dim(placed, vector, quarter, 0)
        return placed.reshape(wide, -1)

    terms = [
        spread(qkv_sums[0, :lanes]),
        spread(qkv_sums[0, lanes : 2 * lanes]),
        spread(qkv_sums[0, 2 * lanes :]),
        jnp.sum(cotangent.astype(jnp.float32), axis=0).reshape(wide, -1),
        spread(up_sums[0]),
    ]
    rider = jnp.concatenate(terms, axis=1).astype(jnp.bfloat16)
    early_count = rider.shape[1]
    rider = jnp.pad(rider, ((0, 0), (0, 16 * weight_rows - early_count)))
    grad_heads = weight_grad(
        [(qkv_grad, normed), (attended, cot)],
        wide,
        rider.reshape(wide, 16, weight_rows),
        after=branch[:1],
    )
    first = [normed_grad[:2], normed_grad[2:]]
    second = [branch[:2], branch[2:]]

    def fold(part, arrived, axes, after, axis=None):
        other = shifted(part[1], arrived, 1)
        return folded(part[0], other, axes, axis or axes[-1], after=[after])

    first[0] = fold(first[0], "m", "gh", grad_heads)
    (grad_down,), _ = scatter_columns(grad_down, [hidden], [True], after=first[0][:1])
    first[1] = fold(first[1], "h", "gm", grad_down)
    second[0] = fold(second[0], "m", "gh", first[1][0])
    later = lax.optimization_barrier((branch[3], first[1][0]))[0]
    second[1] = [branch[2], later]
    first[0] = fold(first[0], "h", "g", second[0][0])
    first[1] = fold(first[1], "m", "g", first[0][0])
    (grad_up,), _ = scatter_columns(grad_up, [hidden], [False], after=first[1][:1])

    def last(keep, send):
        arrived = lax.optimization_barrier((shifted(send[0], "g", 1), grad_up))[0]
        return keep[0].astype(jnp.float32) + arrived.astype(jnp.float32)

    local_x = tokens.astype(jnp.float32)
    standard_grad = jnp.concatenate([last(*part) for part in first], axis=0)
    own_stats = pick(stats.reshape(4, row_count, 128), quarter)
    row_mean, inverse_std = own_stats[:, :1], own_stats[:, 64:65]
    standard = (local_x - row_mean) * inverse_std
    scaled_grad = standard_grad * own_gain
    row_sums = jnp.stack([jnp.sum(scaled_grad, axis=1), jnp.sum(scaled_grad * standard, axis=1)])
    for axis in ("c", "m"):
        row_sums = row_sums + shifted(row_sums, axis, 1)
    input_grad = (
        scaled_grad - row_sums[0][:, None] / D - standard * (row_sums[1][:, None] / D)
    ) * inverse_std + cotangent.astype(jnp.float32)

    own_terms = [jnp.sum(standard_grad * standard, axis=0), jnp.sum(standard_grad, axis=0)]
    own_terms = [term.reshape(wide, -1) for term in own_terms]
    late = summed(jnp.concatenate(own_terms, axis=1), "h")
    late = summed(summed(late, "g"), "s")
    second[1] = fold(second[1], "m", "gh", standard_grad, "g")
    second[0] = fold(second[0], "h", "g", second[1][0])
    second[1] = fold(second[1], "g", "h", second[0][0])
    (grad_query, grad_key, grad_value, grad_dense), riders = scatter_along_line(
        grad_heads,
        [lanes] * 4,
        [False, False, False, True],
        after=[standard_grad],
        late_after=second[1][:1],
    )
    early = jnp.sum(riders.astype(jnp.float32), axis=0).reshape(-1)[:early_count]
    output = finished(
        tokens,
        [part[0][0] for part in second],
        [shifted(part[1][0], axis, 1) for part, axis in zip(second, "gh")],
        out_bias.reshape(1, -1),
        after=[grad_dense],
    )
    terms = own_terms + terms
    vector_sums = jnp.concatenate([pick(late, lax.axis_index(WIDE)), early])
    vector_grads, start = [], 0
    for term in terms:
        vector_grads.append(vector_sums[start : start + term.shape[1]])
        start += term.shape[1]
    return (
        output,
        input_grad,
        vector_grads[0],
        vector_grads[1],
        grad_query,
        vector_grads[2],
        grad_key,
        vector_grads[3],
        grad_value,
        vector_grads[4],
        grad_dense,
        vector_grads[5],
        grad_up,
        vector_grads[6],
        grad_down,
        vector_grads[5],
    )


def solution(mesh):
    wide = mesh.shape["wide"]
    inner = Mesh(mesh.devices.reshape(wide // 4, 2, 2, 2, 2), ("s", "g", "h", "m", "c"))
    acts = P(WIDE, NARROW)
    vector = P(NARROW + WIDE)
    by_rows = P(WIDE, NARROW)
    by_cols = P(NARROW, WIDE)
    specs = (
        (acts, acts, vector, vector)
        + (by_rows, vector) * 3
        + (by_cols, vector, by_rows, vector, by_cols, vector)
    )
    return jax.shard_map(body, mesh=inner, in_specs=specs, out_specs=specs, check_vma=False)
```

```python
from functools import partial
import math

import jax
import jax.numpy as jnp
import numpy as np
from jax import lax
from jax.experimental import pallas as pl
from jax.experimental.pallas import tpu as pltpu
from jax.sharding import Mesh, PartitionSpec as P

D = 2048
HEAD_DIM = 64
ROT = 32
EPSILON = 1e-05
VMEM_LIMIT = 56 * 2**20
COST = 1

WIDE = ("s", "g", "h")
LINE = ("s", "g")
LINE = ("s", "g")
NARROW = ("m", "c")
CUBE = ("g", "h", "m", "c")


def matmul(left_side, right_side):
    return jnp.dot(left_side, right_side, preferred_element_type=jnp.float32)


def contract_rows(left_side, right_side):
    return lax.dot_general(
        left_side, right_side, (((0,), (0,)), ((), ())), preferred_element_type=jnp.float32
    )


def contract_cols(left_side, right_side):
    return lax.dot_general(
        left_side, right_side, (((1,), (1,)), ((), ())), preferred_element_type=jnp.float32
    )


def pick(blocks, index, axis=0):
    return lax.dynamic_index_in_dim(blocks, index, axis, keepdims=False)


def shifted(value, axis, step):
    count = lax.axis_size(axis)
    return lax.ppermute(value, axis, [(source, (source + step) % count) for source in range(count)])


def in_order(mine, other, index):
    return (jnp.where(index == 0, mine, other), jnp.where(index == 0, other, mine))


def call(
    kernel, name, grid, in_specs, out_specs, out_shape, scratch=(), flops=0, after=()
):
    skipped = len(after)

    def ordered(*refs):
        kernel(*refs[skipped:])

    run = pl.pallas_call(
        ordered,
        grid=grid,
        in_specs=[ANY] * skipped + list(in_specs),
        out_specs=out_specs,
        out_shape=out_shape,
        scratch_shapes=list(scratch),
        compiler_params=pltpu.CompilerParams(vmem_limit_bytes=VMEM_LIMIT),
        cost_estimate=pl.CostEstimate(flops=COST * flops // 1000, bytes_accessed=0, transcendentals=0),
        name=name,
    )
    return lambda *operands: run(*after, *operands)


def whole(*shape):
    return pl.BlockSpec(shape, lambda i: (0,) * len(shape))


def band(rows, cols):
    return pl.BlockSpec((rows, cols), lambda i: (i, 0))


ANY = pl.BlockSpec(memory_space=pl.ANY)
SCALARS = pl.BlockSpec(memory_space=pltpu.SMEM)


def struct(shape, dtype):
    return jax.ShapeDtypeStruct(shape, dtype)


def rotary_tables(rows):
    lane = np.arange(2 * HEAD_DIM) % HEAD_DIM
    pair = (lane % (ROT // 2)).astype(np.float32)
    inverse = np.exp(pair * np.float32(-2.0 * math.log(10000.0) / ROT)).astype(np.float32)
    phase = np.arange(rows, dtype=np.float32)[:, None] * inverse[None, :]
    turned = (lane < ROT)[None, :]
    sign = np.where(lane < ROT // 2, -1.0, 1.0)[None, :]
    cosine = np.where(turned, np.cos(phase), 1.0).astype(np.float32)
    sine = np.where(turned, np.sin(phase) * sign, 0.0).astype(np.float32)
    return (cosine, sine)


def turn(values, cosine, sine):
    lane = lax.broadcasted_iota(jnp.int32, values.shape, 1) % HEAD_DIM
    width = values.shape[1]
    half = ROT // 2
    partner = jnp.where(
        lane < half, pltpu.roll(values, width - half, 1), pltpu.roll(values, half, 1)
    )
    return values * cosine + partner * sine


def norm_up_kernel(
    tokens_ref, gain_ref, shift_ref, bias_ref, weight_ref, normed_ref, stats_ref, low_ref, slope_ref
):
    parts = [tokens_ref[0, j].astype(jnp.float32) for j in range(tokens_ref.shape[1])]
    rows, width = parts[0].shape
    total = sum(jnp.sum(part, axis=1, keepdims=True) for part in parts)
    squares = sum(jnp.sum(part * part, axis=1, keepdims=True) for part in parts)
    mean = total / D
    inverse_std = lax.rsqrt(squares / D - mean * mean + EPSILON)
    up_input = bias_ref[...]
    for j, part in enumerate(parts):
        cols = slice(j * width, (j + 1) * width)
        standard = (part - mean) * inverse_std
        normed = (standard * gain_ref[:, cols] + shift_ref[:, cols]).astype(jnp.bfloat16)
        normed_ref[:, cols] = normed
        up_input = up_input + matmul(normed, weight_rows_of(weight_ref, j * width, width))
    stats_ref[...] = jnp.concatenate(
        [jnp.broadcast_to(mean, (rows, 64)), jnp.broadcast_to(inverse_std, (rows, 64))], axis=1
    )
    root = math.sqrt(2.0 / math.pi)
    square = up_input * up_input
    bend = jnp.tanh(root * (up_input + 0.044715 * square * up_input))
    half = 0.5 * (1.0 + bend)
    low_ref[...] = (up_input * half).astype(jnp.bfloat16)
    slope_ref[...] = half + 0.5 * up_input * (1.0 - bend * bend) * (
        root * (1.0 + 3 * 0.044715 * square)
    )


class Weight:
    def __init__(self, array, rows, start, width):
        self.array, self.rows, self.width = array, rows, width
        self.spec = pl.BlockSpec(
            array.shape[:-2] + (rows, width),
            lambda *_: (0,) * (len(array.shape) - 1) + (start // width,),
        )


def weight_rows_of(weight_ref, start, count):
    _, rows, width = weight_ref.shape
    return weight_ref[pl.ds(start // rows, count // rows)].reshape(count, width)


def norm_up(blocks, gain, shift, bias, weight, rows=256, after=()):
    row_blocks, col_blocks, row_count, width = blocks.shape
    total, hidden = row_blocks * row_count, bias.shape[1]
    per = row_count // rows
    spec = pl.BlockSpec((1, col_blocks, rows, width), lambda i: (i // per, 0, i % per, 0))
    return call(
        norm_up_kernel,
        "norm_up",
        (total // rows,),
        [spec]
        + [whole(1, D), whole(1, D), whole(1, hidden), weight.spec],
        [band(rows, D), band(rows, 128), band(rows, hidden), band(rows, hidden)],
        [
            struct((total, D), jnp.bfloat16),
            struct((total, 128), jnp.float32),
            struct((total, hidden), jnp.bfloat16),
            struct((total, hidden), jnp.float32),
        ],
        flops=6 * total * D * hidden,
        after=after,
    )(blocks, gain, shift, bias, weight.array)


def heads_kernel(normed_ref, bias_ref, cosine_ref, sine_ref, weight_ref, heads_ref):
    pre = matmul(normed_ref[...], weight_rows_of(weight_ref, 0, D)) + bias_ref[...]
    lanes = 2 * HEAD_DIM
    cosine, sine = cosine_ref[...], sine_ref[...]
    factor = 1.0 / math.sqrt(HEAD_DIM)
    heads_ref[:, :lanes] = (turn(pre[:, :lanes], cosine, sine) * factor).astype(jnp.bfloat16)
    heads_ref[:, lanes : 2 * lanes] = turn(pre[:, lanes : 2 * lanes], cosine, sine).astype(
        jnp.bfloat16
    )
    heads_ref[:, 2 * lanes :] = pre[:, 2 * lanes :].astype(jnp.bfloat16)


def project_heads(normed, bias, weight, rows=512, after=()):
    total, width = normed.shape[0], bias.shape[1]
    cosine, sine = rotary_tables(total)
    lanes = 2 * HEAD_DIM
    return call(
        heads_kernel,
        "project_heads",
        (total // rows,),
        [band(rows, D), whole(1, width), band(rows, lanes), band(rows, lanes)]
        + [weight.spec],
        band(rows, width),
        struct((total, width), jnp.bfloat16),
        flops=4 * total * D * width,
        after=after,
    )(normed, bias, jnp.asarray(cosine), jnp.asarray(sine), weight.array)


def cot_spec(cot, rows):
    row_count, width = cot.shape[-2:]
    per = row_count // rows
    return pl.BlockSpec(
        (1, 4, 1, rows, width), lambda i: (i // per % 2, 0, i // per // 2, i % per, 0)
    )


def cot_product(cot_ref, weight_ref):
    width = cot_ref.shape[4]
    total = 0.0
    for j in range(4):
        part = cot_ref[0, j, 0]
        total = total + matmul(part, weight_rows_of(weight_ref, j * width, width))
    return total


def out_grad_kernel(cot_ref, weight_ref, out_ref):
    out_ref[...] = cot_product(cot_ref, weight_ref).astype(jnp.bfloat16)


def attended_gradient(cot, weight, width, rows=512, after=()):
    total = 4 * cot.shape[3]
    return call(
        out_grad_kernel,
        "attended_gradient",
        (total // rows,),
        [cot_spec(cot, rows), weight.spec],
        band(rows, width),
        struct((total, width), jnp.bfloat16),
        flops=8 * total * D * width,
        after=after,
    )(cot, weight.array)


def up_grad_kernel(cot_ref, slope_ref, weight_ref, up_ref, sums_ref):
    @pl.when(pl.program_id(0) == 0)
    def _():
        sums_ref[...] = jnp.zeros_like(sums_ref)

    up = (cot_product(cot_ref, weight_ref) * slope_ref[...]).astype(jnp.bfloat16)
    up_ref[...] = up
    sums_ref[...] += jnp.sum(up.astype(jnp.float32), axis=0, keepdims=True)


def up_gradient(cot, slope, weight, rows=512, after=()):
    total, hidden = slope.shape
    return call(
        up_grad_kernel,
        "up_gradient",
        (total // rows,),
        [cot_spec(cot, rows), band(rows, hidden), weight.spec],
        [band(rows, hidden), whole(1, hidden)],
        [struct((total, hidden), jnp.bfloat16), struct((1, hidden), jnp.float32)],
        flops=4 * total * D * hidden,
        after=after,
    )(cot, slope, weight.array)


def rows_of(index, size):
    return pl.ds(pl.multiple_of(index * size, size), size)


HEADS_HERE = [slice(n * HEAD_DIM, (n + 1) * HEAD_DIM) for n in range(2)]


def turned_into(ref, source_ref, cols):
    chunk = 256

    def one(b, carry):
        rows = rows_of(b, chunk)
        ref[:, rows] = source_ref[rows, cols].T
        return carry

    lax.fori_loop(0, source_ref.shape[0] // chunk, one, 0)


def causal_block(block):
    return lax.broadcasted_iota(jnp.int32, (block, block), 0) <= lax.broadcasted_iota(
        jnp.int32, (block, block), 1
    )


def fold_rows(values, combine):
    rows, cols = values.shape
    return combine(values.reshape(rows // 8, 8, cols), axis=0)


def attention_kernel(block, qkv_ref, attended_ref, log_sums_ref, qt_ref, vt_ref, score_ref):
    i = pl.program_id(0)
    width = 2 * HEAD_DIM

    @pl.when(i == 0)
    def _():
        turned_into(qt_ref, qkv_ref, slice(0, width))
        turned_into(vt_ref, qkv_ref, slice(2 * width, 3 * width))
        log_sums_ref[...] = jnp.zeros_like(log_sums_ref)

    own = rows_of(i, block)
    causal = causal_block(block)

    def score(j, best, diagonal):
        rows = rows_of(j, block)
        new = []
        for n, head in enumerate(HEADS_HERE):
            start = width + n * HEAD_DIM
            part = matmul(qkv_ref[rows, start : start + HEAD_DIM], qt_ref[head, own])
            if diagonal:
                part = jnp.where(causal, part, -1e30)
            score_ref[n, j] = part
            new.append(jnp.maximum(best[n], fold_rows(part, jnp.max)))
        return tuple(new)

    low = jnp.full((8, block), -1e30, jnp.float32)
    best = lax.fori_loop(0, i, lambda j, b: score(j, b, False), (low, low))
    best = score(i, best, True)
    top = [jnp.max(value, axis=0, keepdims=True) for value in best]

    def weigh(j, carry):
        new = []
        for n in range(2):
            weights = jnp.exp(score_ref[n, j] - top[n])
            score_ref[n, j] = weights
            new.append(carry[n] + fold_rows(weights, jnp.sum))
        return tuple(new)

    zero = jnp.zeros((8, block), jnp.float32)
    totals = lax.fori_loop(0, i + 1, weigh, (zero, zero))
    totals = [jnp.sum(total, axis=0, keepdims=True) for total in totals]
    scales = [1.0 / total for total in totals]
    for n in range(2):
        log_sums_ref[n : n + 1, own] = top[n] + jnp.log(totals[n])

    def push(j, carry):
        rows = rows_of(j, block)
        new = []
        for n, head in enumerate(HEADS_HERE):
            probs = (score_ref[n, j] * scales[n]).astype(jnp.bfloat16)
            new.append(carry[n] + matmul(vt_ref[head, rows], probs))
        return tuple(new)

    zero = jnp.zeros((HEAD_DIM, block), jnp.float32)
    out = lax.fori_loop(0, i + 1, push, (zero, zero))
    attended_ref[own, :] = jnp.concatenate(out, axis=0).T.astype(jnp.bfloat16)


def attention(qkv, block=512, after=()):
    rows, width = qkv.shape[0], 2 * HEAD_DIM
    blocks = rows // block
    return call(
        partial(attention_kernel, block),
        "attention",
        (blocks,),
        [whole(rows, 3 * width)],
        [whole(rows, width), whole(8, rows)],
        [struct((rows, width), jnp.bfloat16), struct((8, rows), jnp.float32)],
        [pltpu.VMEM((width, rows), jnp.bfloat16)] * 2
        + [pltpu.VMEM((2, blocks, block, block), jnp.float32)],
        flops=10 * 10**9,
        after=after,
    )(qkv)


def attention_back_kernel(
    blocks,
    block,
    qkv_ref,
    grad_ref,
    log_sums_ref,
    cosine_ref,
    sine_ref,
    pre_grad_ref,
    sums_ref,
    qt_ref,
    kt_ref,
    gt_ref,
    prob_ref,
    slope_ref,
    k_ref,
    v_ref,
    k_total,
    v_total,
):
    i = pl.program_id(0)
    width = 2 * HEAD_DIM
    factor = 1.0 / math.sqrt(HEAD_DIM)
    chunk = 256

    @pl.when(i == 0)
    def _():
        turned_into(qt_ref, qkv_ref, slice(0, width))
        turned_into(kt_ref, qkv_ref, slice(width, 2 * width))
        turned_into(gt_ref, grad_ref, slice(0, width))
        for n in range(2):
            for ref, begin in ((k_ref, width), (v_ref, 2 * width)):
                begin += n * HEAD_DIM
                ref[n] = qkv_ref[:, begin : begin + HEAD_DIM]
        k_total[...] = jnp.zeros_like(k_total)
        v_total[...] = jnp.zeros_like(v_total)
        sums_ref[...] = jnp.zeros_like(sums_ref)

    own = rows_of(i, block)
    causal = causal_block(block)
    log_sums = [log_sums_ref[n : n + 1, own] for n in range(2)]

    def weigh(j, carry, diagonal):
        rows = rows_of(j, block)
        new = []
        for n, head in enumerate(HEADS_HERE):
            scores = matmul(k_ref[n, rows, :], qt_ref[head, own])
            probs = jnp.exp(scores - log_sums[n])
            if diagonal:
                probs = jnp.where(causal, probs, 0.0)
            slope = matmul(v_ref[n, rows, :], gt_ref[head, own])
            prob_ref[n, j] = probs
            slope_ref[n, j] = slope
            new.append(carry[n] + fold_rows(probs * slope, jnp.sum))
        return tuple(new)

    zero = jnp.zeros((8, block), jnp.float32)
    dots = lax.fori_loop(0, i, lambda j, c: weigh(j, c, False), (zero, zero))
    dots = weigh(i, dots, True)
    dots = [jnp.sum(dot, axis=0, keepdims=True) for dot in dots]

    def push(j, carry):
        rows = rows_of(j, block)
        new = []
        for n, head in enumerate(HEADS_HERE):
            probs = prob_ref[n, j]
            score_grad = (probs * (slope_ref[n, j] - dots[n])).astype(jnp.bfloat16)
            k_total[n, rows, :] += matmul(score_grad, qkv_ref[own, head])
            v_total[n, rows, :] += matmul(probs.astype(jnp.bfloat16), grad_ref[own, head])
            new.append(carry[n] + matmul(kt_ref[head, rows], score_grad))
        return tuple(new)

    zero = jnp.zeros((HEAD_DIM, block), jnp.float32)
    q_grad = lax.fori_loop(0, i + 1, push, (zero, zero))
    q_grad = jnp.concatenate(q_grad, axis=0).T * factor
    q_pre = turn(q_grad, cosine_ref[own, :], -sine_ref[own, :]).astype(jnp.bfloat16)
    pre_grad_ref[own, :width] = q_pre
    sums_ref[:, :width] += jnp.sum(q_pre.astype(jnp.float32), axis=0, keepdims=True)

    @pl.when(i == blocks - 1)
    def _():
        def finish(b, carry):
            rows = rows_of(b, chunk)
            k_sum = jnp.concatenate([k_total[0, rows, :], k_total[1, rows, :]], axis=1)
            v_sum = jnp.concatenate([v_total[0, rows, :], v_total[1, rows, :]], axis=1)
            k_pre = turn(k_sum, cosine_ref[rows, :], -sine_ref[rows, :])
            k_pre = k_pre.astype(jnp.bfloat16)
            v_pre = v_sum.astype(jnp.bfloat16)
            pre_grad_ref[rows, width : 2 * width] = k_pre
            pre_grad_ref[rows, 2 * width :] = v_pre
            both = jnp.concatenate([k_pre, v_pre], axis=1).astype(jnp.float32)
            return carry + jnp.sum(both, axis=0, keepdims=True)

        sums_ref[:, width:] = lax.fori_loop(
            0, qkv_ref.shape[0] // chunk, finish, jnp.zeros((1, 2 * width), jnp.float32)
        )


def attention_back(qkv, out_grad, log_sums, block=512, after=()):
    rows, width = qkv.shape[0], 2 * HEAD_DIM
    blocks = rows // block
    cosine, sine = rotary_tables(rows)
    return call(
        partial(attention_back_kernel, blocks, block),
        "attention_back",
        (blocks,),
        [whole(rows, 3 * width), whole(rows, width), whole(8, rows)]
        + [whole(rows, width), whole(rows, width)],
        [whole(rows, 3 * width), whole(1, 3 * width)],
        [struct((rows, 3 * width), jnp.bfloat16), struct((1, 3 * width), jnp.float32)],
        [pltpu.VMEM((width, rows), jnp.bfloat16)] * 3
        + [pltpu.VMEM((2, blocks, block, block), jnp.float32)] * 2
        + [pltpu.VMEM((2, rows, HEAD_DIM), jnp.bfloat16)] * 2
        + [pltpu.VMEM((2, rows, HEAD_DIM), jnp.float32)] * 2,
        flops=20 * 10**9,
        after=after,
    )(qkv, out_grad, log_sums, jnp.asarray(cosine), jnp.asarray(sine))


def weight_grad_kernel(riders, *refs):
    out_ref, refs = refs[-1], refs[:-1]
    if riders:
        height = out_ref.shape[1] - refs[0].shape[1]
        out_ref[:, height:, :] = refs[0][...]
        refs = refs[1:]
    cols = out_ref.shape[2]
    start = 0
    for left_ref, right_ref in zip(refs[::2], refs[1::2]):
        if len(right_ref.shape) == 5:
            size = right_ref.shape[3]
            part = 0.0
            for b in range(4):
                rows = slice(b * size, (b + 1) * size)
                part = part + contract_rows(left_ref[rows, :], right_ref[b % 2, 0, b // 2])
        else:
            part = contract_rows(left_ref[...], right_ref[...])
        part = part.astype(jnp.bfloat16)
        stop = start + part.shape[0]
        for n in range(out_ref.shape[0]):
            out_ref[n, start:stop, :] = part[:, n * cols : (n + 1) * cols]
        start = stop


def weight_grad(pairs, parts, rider=None, after=()):
    cols = D // parts
    per = parts // 4
    rows = pairs[0][0].shape[0]
    height = sum(left.shape[1] for left, _ in pairs)
    in_specs, operands = [], []
    if rider is not None:
        in_specs.append(pl.BlockSpec((per,) + rider.shape[1:], lambda i: (i, 0, 0)))
        operands.append(rider)
        height += rider.shape[1]
    for left, right in pairs:
        in_specs.append(whole(*left.shape))
        if right.ndim == 5:
            in_specs.append(
                pl.BlockSpec((2, 1, 2, right.shape[3], D // 4), lambda i: (0, i, 0, 0, 0))
            )
        else:
            in_specs.append(pl.BlockSpec((rows, D // 4), lambda i: (0, i)))
        operands += [left, right]
    return call(
        partial(weight_grad_kernel, rider is not None),
        "weight_grad",
        (4,),
        in_specs,
        pl.BlockSpec((per, height, cols), lambda i: (i, 0, 0)),
        struct((parts, height, cols), jnp.bfloat16),
        flops=4 * rows * height * D,
        after=after,
    )(*operands)


def partial_sum_kernel(sides, axes, index_ref, *refs):
    lefts, refs = refs[: 2 * sides], refs[2 * sides :]
    weights, others, outs = refs[:sides], refs[sides : 2 * sides], refs[2 * sides :]
    rows, width = outs[0].shape[-2:]
    own_m, own_h, core = index_ref[0], index_ref[1], index_ref[2]
    here = lax.rem(pl.program_id(0), 2) == own_h
    for n_m, m in enumerate((own_m, 1 - own_m)):
        out = 0.0
        for n in range(sides):
            weight = weight_rows_of(weights[n], (2 * m + core) * width, width)
            out = out + contract_cols(lefts[n][...], weight)
            other = others[n][m].reshape(width, weight.shape[1])
            out = out + contract_cols(lefts[sides + n][...], other)
        out = out.astype(jnp.bfloat16)
        for half, axis in enumerate(axes):
            part = out[half * rows : (half + 1) * rows]
            if axis == "m":
                outs[2 * half + n_m][0] = part
                continue
            for n_h, mine in enumerate((here, jnp.logical_not(here))):

                @pl.when(mine)
                def _(out_ref=outs[2 * half + n_h], m=m, part=part):
                    out_ref[0, m] = part


def partial_sum(sides, row_count, width, name, axes, after=()):
    total = sides[0][0].shape[0]
    rows = row_count // len(axes)
    blocks = total // row_count
    lefts = [side[0] for side in sides] + [side[1] for side in sides]
    weights = [side[2] for side in sides]
    others = [side[3] for side in sides]
    depth = sum(left.shape[1] for left in lefts)
    specs, shapes = [], []
    for axis in axes:
        if axis == "m":
            specs += [pl.BlockSpec((1, rows, width), lambda i: (i, 0, 0))] * 2
            shapes += [struct((blocks, rows, width), jnp.bfloat16)] * 2
        else:
            specs += [pl.BlockSpec((1, 2, rows, width), lambda i: (i // 2, 0, 0, 0))] * 2
            shapes += [struct((blocks // 2, 2, rows, width), jnp.bfloat16)] * 2
    index = jnp.stack([lax.axis_index(axis) for axis in "mhc"]).astype(jnp.int32)
    return call(
        partial(partial_sum_kernel, len(sides), axes),
        name,
        (blocks,),
        [SCALARS]
        + [band(row_count, left.shape[1]) for left in lefts]
        + [weight.spec for weight in weights]
        + [other.spec for other in others],
        specs,
        shapes,
        flops=2 * total * depth * D,
        after=after,
    )(index, *lefts, *[weight.array for weight in weights], *[other.array for other in others])


def switch_specs(count, block):
    zeros = (0,) * (len(block) - 1)
    return [
        pl.BlockSpec(block, lambda k, j, p: (j + k * (count - 1 - j),) + zeros),
        pl.BlockSpec(block, lambda k, j, p: (j * k,) + zeros),
    ]


def prefetch_call(kernel, name, index, grid, in_specs, out_specs, out_shape, after=()):
    skipped = len(after)

    def ordered(index_ref, *refs):
        kernel(index_ref, *refs[skipped:])

    run = pl.pallas_call(
        ordered,
        grid_spec=pltpu.PrefetchScalarGridSpec(
            num_scalar_prefetch=1,
            grid=grid,
            in_specs=[ANY] * skipped + list(in_specs),
            out_specs=out_specs,
        ),
        out_shape=out_shape,
        compiler_params=pltpu.CompilerParams(vmem_limit_bytes=VMEM_LIMIT),
        cost_estimate=pl.CostEstimate(flops=0, bytes_accessed=0, transcendentals=0),
        name=name,
    )
    return lambda *operands: run(index.astype(jnp.int32).reshape(1), *after, *operands)


def column_specs(shards, turned, block):
    specs, width = [], 0
    for flip, shard in zip(turned, shards):
        height, cols = shard.shape
        if flip:
            specs.append(pl.BlockSpec((height // 4, cols), lambda *at: (block(*at), 0)))
            rows, width = cols, width + height // 4
        else:
            specs.append(pl.BlockSpec((height, cols // 4), lambda *at: (0, block(*at))))
            rows, width = height, width + cols // 4
    return specs, rows, width


def write_columns(turned, refs, store):
    start = 0
    for flip, ref in zip(turned, refs):
        part = ref[...].T if flip else ref[...]
        store(slice(start, start + part.shape[1]), part)
        start += part.shape[1]


def pack_kernel(turned, rows, riders, *refs):
    out_ref, refs = refs[-1], refs[:-1]
    if riders:
        rider, refs = refs[0][...], refs[1:]

    def store(cols, part):
        for n in range(out_ref.shape[0]):
            out_ref[n, 0, :rows, cols] = part

    write_columns(turned, refs, store)
    if riders:
        for n in range(out_ref.shape[0]):
            out_ref[n, 0, rows:, :] = rider


def packed(shards, turned, rider=None):
    wide = lax.axis_size(WIDE)
    specs, rows, width = column_specs(shards, turned, lambda i: i)
    height = rows
    if rider is not None:
        specs = [whole(*rider.shape)] + specs
        shards = [rider] + shards
        height += rider.shape[0]
    blocks = call(
        partial(pack_kernel, turned, rows, rider is not None),
        "pack",
        (4,),
        specs,
        pl.BlockSpec((wide // 4, 1, height, width), lambda i: (0, i, 0, 0)),
        struct((wide // 4, 4, height, width), jnp.bfloat16),
    )(*shards)
    return blocks.reshape(wide, height, width)


def exchanged(blocks, after=()):
    blocks = lax.optimization_barrier((blocks, *after))[0]
    return lax.all_to_all(blocks, WIDE, 0, 0)


def sides_kernel(turned, index_ref, *refs):
    for out_ref, blocks in zip(refs[-2:], (refs[:-2][::2], refs[:-2][1::2])):

        def store(cols, part, out_ref=out_ref):
            out_ref[0, :, cols] = part

        write_columns(turned, blocks, store)


def packed_sides(shards, turned):
    specs, operands, width = [], [], 0
    for flip, shard in zip(turned, shards):
        height, cols = shard.shape
        if flip:
            rows, width = cols, width + height // 4
            shape, at = (height // 4, cols), lambda block: (block, 0)
        else:
            rows, width = height, width + cols // 4
            shape, at = (height, cols // 4), lambda block: (0, block)
        specs.append(pl.BlockSpec(shape, lambda j, p, at=at: at(2 * j + p[0])))
        specs.append(pl.BlockSpec(shape, lambda j, p, at=at: at(2 * j + 1 - p[0])))
        operands += [shard, shard]
    return prefetch_call(
        partial(sides_kernel, turned),
        "pack",
        lax.axis_index("h"),
        (2,),
        specs,
        [pl.BlockSpec((1, rows, width), lambda j, p: (j, 0, 0))] * 2,
        [struct((2, rows, width), jnp.bfloat16)] * 2,
    )(*operands)


def spread_kernel(index_ref, mine_ref, other_ref, out_ref):
    for n in range(out_ref.shape[0]):
        out_ref[n, 0, index_ref[0]] = mine_ref[0]
        out_ref[n, 0, 1 - index_ref[0]] = other_ref[0]


def spread_sides(sides, after=()):
    mine, send = sides
    sequences = lax.axis_size("s")
    _, rows, width = mine.shape
    spec = pl.BlockSpec((1, rows, width), lambda j, p: (j, 0, 0))
    blocks = prefetch_call(
        spread_kernel,
        "spread",
        lax.axis_index("h"),
        (2,),
        [spec, spec],
        pl.BlockSpec((sequences, 1, 2, rows, width), lambda j, p: (0, j, 0, 0, 0)),
        struct((sequences, 2, 2, rows, width), jnp.bfloat16),
        after=after,
    )(mine, shifted(send, "h", 1))
    return blocks.reshape(2 * sequences, 2 * rows, width)


def exchanged_along_line(blocks):
    count, rows, width = blocks.shape
    return lax.all_to_all(blocks, LINE, 0, 0).reshape(2 * count, rows // 2, width)


def unpack_kernel(turned, arrived_ref, *outs):
    total = arrived_ref[0, 0].astype(jnp.float32)
    for n in range(1, arrived_ref.shape[0]):
        total = total + arrived_ref[n, 0].astype(jnp.float32)
    start = 0
    for flip, out_ref in zip(turned, outs):
        height = out_ref.shape[0] if flip else out_ref.shape[1]
        part = total[start : start + height]
        out_ref[...] = part if flip else part.T
        start += height


def scatter_columns(grad, heights, turned, after=()):
    sequences = lax.axis_size("s")
    _, height, rows = grad.shape
    arrived = lax.all_to_all(grad, WIDE, 0, 0)
    riders = arrived[:, sum(heights) :]
    arrived = arrived.reshape(sequences, 4, height, rows)
    height = sum(heights)
    specs, shapes = [], []
    for flip, part in zip(turned, heights):
        if flip:
            specs.append(pl.BlockSpec((part, rows), lambda i: (i, 0)))
            shapes.append(struct((4 * part, rows), jnp.float32))
        else:
            specs.append(pl.BlockSpec((rows, part), lambda i: (0, i)))
            shapes.append(struct((rows, 4 * part), jnp.float32))
    shards = call(
        partial(unpack_kernel, turned),
        "unpack",
        (4,),
        [pl.BlockSpec((sequences, 1, height, rows), lambda i: (0, i, 0, 0))],
        specs,
        shapes,
        after=after,
    )(arrived)
    return shards, riders


def side_sums_kernel(index_ref, arrived_ref, keep_ref, send_ref):
    for out_ref, side in ((keep_ref, index_ref[0]), (send_ref, 1 - index_ref[0])):
        total = arrived_ref[0, 0, side].astype(jnp.float32)
        for n in range(1, arrived_ref.shape[0]):
            total = total + arrived_ref[n, 0, side].astype(jnp.float32)
        out_ref[0] = total.astype(out_ref.dtype)


def unpack_sides_kernel(turned, index_ref, keep_ref, other_ref, *outs):
    def write(total):
        start = 0
        for flip, out_ref in zip(turned, outs):
            height = out_ref.shape[0] if flip else out_ref.shape[1]
            part = total[start : start + height]
            out_ref[...] = part if flip else part.T
            start += height

    @pl.when(pl.program_id(1) == 0)
    def _():
        write(keep_ref[0])

    @pl.when(pl.program_id(1) == 1)
    def _():
        write(other_ref[0].astype(jnp.float32))


def scatter_along_line(grad, heights, turned, after=(), late_after=()):
    sequences, side = lax.axis_size("s"), lax.axis_index("h")
    wide, height, rows = grad.shape
    arrived = lax.all_to_all(grad.reshape(wide // 2, 2 * height, rows), LINE, 0, 0)
    band_of = pl.BlockSpec((1, height, rows), lambda j, p: (j, 0, 0))
    keep, send = prefetch_call(
        side_sums_kernel,
        "side_sums",
        side,
        (2,),
        [pl.BlockSpec((sequences, 1, 2, height, rows), lambda j, p: (0, j, 0, 0, 0))],
        [band_of, band_of],
        [struct((2, height, rows), jnp.float32), struct((2, height, rows), jnp.bfloat16)],
        after=after,
    )(arrived.reshape(sequences, 2, 2, height, rows))
    other = shifted(send, "h", 1)
    riders = keep[:, sum(heights) :] + other[:, sum(heights) :].astype(jnp.float32)
    specs, shapes = [], []
    block = lambda j, n, p: 2 * j + p[0] + n - 2 * n * p[0]
    for flip, part in zip(turned, heights):
        if flip:
            specs.append(pl.BlockSpec((part, rows), lambda j, n, p: (block(j, n, p), 0)))
            shapes.append(struct((4 * part, rows), jnp.float32))
        else:
            specs.append(pl.BlockSpec((rows, part), lambda j, n, p: (0, block(j, n, p))))
            shapes.append(struct((rows, 4 * part), jnp.float32))
    part_of = pl.BlockSpec((1, sum(heights), rows), lambda j, n, p: (j, 0, 0))
    shards = prefetch_call(
        partial(unpack_sides_kernel, turned),
        "unpack",
        side,
        (2, 2),
        [part_of, part_of],
        specs,
        shapes,
        after=late_after,
    )(keep, other)
    return shards, riders


def fold_kernel(index_ref, mine_keep, mine_send, arrived_keep, arrived_send, keep_ref, send_ref):
    keep_ref[...] = mine_keep[...] + arrived_keep[...]
    send_ref[...] = mine_send[...] + arrived_send[...]


def folded(mine, arrived, axes, axis, after=()):
    position = axes.index(axis)
    high, low = 2**position, 2 ** (len(axes) - 1 - position)
    rows, cols = mine.shape[-2:]
    shape = (high, 2, low * rows, cols)
    steps = 2 if low > 1 else 1
    block = low * rows // steps
    halves = [
        pl.BlockSpec((high, None, block, cols), lambda j, p: (0, p[0], j, 0)),
        pl.BlockSpec((high, None, block, cols), lambda j, p: (0, 1 - p[0], j, 0)),
    ]
    out = pl.BlockSpec((high, block, cols), lambda j, p: (0, j, 0))
    mine, arrived = mine.reshape(shape), arrived.reshape(shape)
    keep, send = prefetch_call(
        fold_kernel,
        "fold",
        lax.axis_index(axis),
        (steps,),
        halves * 2,
        [out, out],
        [struct((high, low * rows, cols), jnp.bfloat16)] * 2,
        after=after,
    )(mine, mine, arrived, arrived)
    return [part.reshape(high * low, rows, cols) for part in (keep, send)]


def join_kernel(index_ref, mine_ref, other_ref, out_ref):
    out_ref[index_ref[0]] = mine_ref[...]
    out_ref[1 - index_ref[0]] = other_ref[...]


def joined(mine, other, axis, after=()):
    rows, cols = mine.size // mine.shape[-1] // 2, mine.shape[-1]
    spec = pl.BlockSpec((rows, cols), lambda j, p: (j, 0))
    out = prefetch_call(
        join_kernel,
        "join",
        lax.axis_index(axis),
        (2,),
        [spec, spec],
        pl.BlockSpec((2, rows, cols), lambda j, p: (0, j, 0)),
        struct((2, 2 * rows, cols), mine.dtype),
        after=after,
    )(mine.reshape(2 * rows, cols), other.reshape(2 * rows, cols))
    return out.reshape((2,) + mine.shape)


def finish_kernel(tokens_ref, *refs):
    bias_ref, out_ref = refs[-2:]
    parts = len(refs) // 2 - 1
    rows = refs[0].shape[0]
    for n, (keep_ref, arrived_ref) in enumerate(zip(refs[:parts], refs[parts : 2 * parts])):
        at = slice(n * rows, (n + 1) * rows)
        total = tokens_ref[at, :].astype(jnp.float32) + keep_ref[...].astype(jnp.float32)
        total = total + arrived_ref[...].astype(jnp.float32) + bias_ref[...]
        out_ref[at, :] = total.astype(jnp.bfloat16)


def finished(tokens, keep, arrived, bias, after=()):
    operands = [tokens, *keep, *arrived, bias]
    return call(
        finish_kernel,
        "finish",
        (1,),
        [whole(*operand.shape) for operand in operands],
        whole(*tokens.shape),
        struct(tokens.shape, tokens.dtype),
        after=after,
    )(*operands)


def gather_narrow(value):
    for axis in ("c", "m"):
        other = shifted(value, axis, 1)
        value = jnp.stack(in_order(value, other, lax.axis_index(axis)))
    return value.reshape((4,) + value.shape[2:])


def summed(value, axis):
    total = value
    for step in range(1, lax.axis_size(axis)):
        total = total + shifted(value, axis, step)
    return total


def body(
    tokens,
    cotangent,
    ln_gain,
    ln_shift,
    w_query,
    b_query,
    w_key,
    b_key,
    w_value,
    b_value,
    w_dense,
    b_dense,
    w_fc1,
    b_fc1,
    w_fc2,
    b_fc2,
):
    row_count, feature_count = tokens.shape
    own_g, own_h = lax.axis_index("g"), lax.axis_index("h")
    own_n = lax.axis_index(NARROW)
    quarter = 2 * own_g + own_h
    wide = lax.axis_size(WIDE)
    weight_rows = w_fc1.shape[0]
    lanes = w_query.shape[1] // 4

    vectors = (ln_gain, ln_shift, b_query, b_key, b_value, b_dense, b_fc2, b_fc1)
    lengths = [vector.shape[0] for vector in vectors]
    hidden = w_fc1.shape[1] // 4
    rider = jnp.concatenate(vectors)
    rider = jnp.pad(rider, (0, 16 * hidden - rider.shape[0])).reshape(16, hidden)

    tokens_full = lax.all_gather(tokens, CUBE, axis=0, tiled=False)
    tokens_full = tokens_full.reshape(4, 4, row_count, feature_count)
    up_blocks = packed([w_fc1], [False], rider)
    head_sides = packed_sides(
        [w_query, w_key, w_value, w_dense], [False, False, False, True]
    )
    down_sides = packed_sides([w_fc2], [True])
    other = shifted(cotangent, "g", 1)
    arrived = exchanged(up_blocks, after=[other])
    cot = joined(cotangent, other, "g", after=[up_blocks, head_sides[0], down_sides[0]])
    cot = lax.all_gather(cot, ("h", "m", "c"), axis=0, tiled=False)
    cot = cot.reshape(2, 4, 2, row_count, feature_count)
    head_blocks = spread_sides(head_sides, after=[arrived])
    head_arrived = exchanged_along_line(head_blocks)
    up_weight = Weight(arrived, weight_rows, 0, hidden)
    qkv_weight = Weight(head_arrived, weight_rows, 0, 3 * lanes)
    dense_weight = Weight(head_arrived, weight_rows, 3 * lanes, lanes)

    def from_other_core(array):
        split = array[:, :weight_rows].reshape(2, 2, wide // 4, weight_rows, -1)
        return shifted(pick(split, 1 - lax.axis_index("c"), 1), "c", 1)

    up_other = Weight(from_other_core(arrived), weight_rows, 0, hidden)
    head_other = from_other_core(head_arrived)
    qkv_other = Weight(head_other, weight_rows, 0, 3 * lanes)
    dense_other = Weight(head_other, weight_rows, 3 * lanes, lanes)

    here = arrived[:, weight_rows:].reshape(wide, 16 * hidden)
    local, start = [], 0
    for length in lengths:
        local.append(here[:, start : start + length].astype(jnp.float32).reshape(-1))
        start += length
    shared = gather_narrow(here[:, : 2 * lengths[0]].astype(jnp.float32))
    gain = shared[:, :, : lengths[0]].reshape(1, D)
    shift = shared[:, :, lengths[0] :].reshape(1, D)

    def quarter_of(vector):
        return pick(vector.reshape(4, -1), quarter)

    qkv_bias = jnp.concatenate([quarter_of(vector) for vector in local[2:5]]).reshape(1, -1)
    up_bias = quarter_of(local[7]).reshape(1, -1)
    own_gain, out_bias = local[0], local[5] + local[6]

    normed, stats, up_low, up_slope = norm_up(
        tokens_full, gain, shift, up_bias, up_weight, after=[up_other.array]
    )
    down_blocks = spread_sides(down_sides, after=[normed])
    down_arrived = exchanged_along_line(down_blocks)
    down_weight = Weight(down_arrived, weight_rows, 0, hidden)
    qkv = project_heads(normed, qkv_bias, qkv_weight, after=[head_other])
    attended, log_sums = attention(qkv)
    grad_down = weight_grad([(up_low, cot)], wide, after=[attended])
    attended_grad = attended_gradient(cot, dense_weight, lanes, after=[grad_down])
    grad_down = lax.optimization_barrier((grad_down, attended_grad))[0]
    up_grad, up_sums = up_gradient(cot, up_slope, down_weight, after=[attended_grad])
    qkv_grad, qkv_sums = attention_back(qkv, attended_grad, log_sums, after=[up_grad])
    qkv_grad_other = shifted(qkv_grad, "c", 1)

    grad_up = weight_grad([(up_grad, normed)], wide, after=[qkv_grad])
    up_grad_other = shifted(up_grad, "c", 1)
    grad_up = lax.optimization_barrier((grad_up, qkv_grad_other, up_grad_other))[0]
    normed_grad = partial_sum(
        [
            (qkv_grad, qkv_grad_other, qkv_weight, qkv_other),
            (up_grad, up_grad_other, up_weight, up_other),
        ],
        row_count,
        feature_count,
        "normed_gradient",
        "mh",
        after=[grad_up],
    )

    down_other = lax.optimization_barrier((down_arrived, normed_grad[0]))[0]
    down_other = Weight(from_other_core(down_other), weight_rows, 0, hidden)
    branch = partial_sum(
        [
            (attended, shifted(attended, "c", 1), dense_weight, dense_other),
            (up_low, shifted(up_low, "c", 1), down_weight, down_other),
        ],
        row_count,
        feature_count,
        "branch_sum",
        "mm",
        after=normed_grad[:1],
    )
    def spread(vector):
        placed = jnp.zeros((4, vector.shape[0]), jnp.float32)
        placed = lax.dynamic_update_index_in_dim(placed, vector, quarter, 0)
        return placed.reshape(wide, -1)

    terms = [
        spread(qkv_sums[0, :lanes]),
        spread(qkv_sums[0, lanes : 2 * lanes]),
        spread(qkv_sums[0, 2 * lanes :]),
        jnp.sum(cotangent.astype(jnp.float32), axis=0).reshape(wide, -1),
        spread(up_sums[0]),
    ]
    rider = jnp.concatenate(terms, axis=1).astype(jnp.bfloat16)
    early_count = rider.shape[1]
    rider = jnp.pad(rider, ((0, 0), (0, 16 * weight_rows - early_count)))
    grad_heads = weight_grad(
        [(qkv_grad, normed), (attended, cot)],
        wide,
        rider.reshape(wide, 16, weight_rows),
        after=branch[:1],
    )
    first = [normed_grad[:2], normed_grad[2:]]
    second = [branch[:2], branch[2:]]

    def fold(part, arrived, axes, after, axis=None):
        other = shifted(part[1], arrived, 1)
        return folded(part[0], other, axes, axis or axes[-1], after=[after])

    first[0] = fold(first[0], "m", "gh", grad_heads)
    (grad_down,), _ = scatter_columns(grad_down, [hidden], [True], after=first[0][:1])
    first[1] = fold(first[1], "h", "gm", grad_down)
    second[0] = fold(second[0], "m", "gh", first[1][0])
    later = lax.optimization_barrier((branch[3], first[1][0]))[0]
    second[1] = [branch[2], later]
    first[0] = fold(first[0], "h", "g", second[0][0])
    first[1] = fold(first[1], "m", "g", first[0][0])
    (grad_up,), _ = scatter_columns(grad_up, [hidden], [False], after=first[1][:1])

    def last(keep, send):
        arrived = lax.optimization_barrier((shifted(send[0], "g", 1), grad_up))[0]
        return keep[0].astype(jnp.float32) + arrived.astype(jnp.float32)

    local_x = tokens.astype(jnp.float32)
    standard_grad = jnp.concatenate([last(*part) for part in first], axis=0)
    own_stats = pick(stats.reshape(4, row_count, 128), quarter)
    row_mean, inverse_std = own_stats[:, :1], own_stats[:, 64:65]
    standard = (local_x - row_mean) * inverse_std
    scaled_grad = standard_grad * own_gain
    row_sums = jnp.stack([jnp.sum(scaled_grad, axis=1), jnp.sum(scaled_grad * standard, axis=1)])
    for axis in ("c", "m"):
        row_sums = row_sums + shifted(row_sums, axis, 1)
    input_grad = (
        scaled_grad - row_sums[0][:, None] / D - standard * (row_sums[1][:, None] / D)
    ) * inverse_std + cotangent.astype(jnp.float32)

    own_terms = [jnp.sum(standard_grad * standard, axis=0), jnp.sum(standard_grad, axis=0)]
    own_terms = [term.reshape(wide, -1) for term in own_terms]
    late = summed(jnp.concatenate(own_terms, axis=1), "h")
    late = summed(summed(late, "g"), "s")
    second[1] = fold(second[1], "m", "gh", standard_grad, "g")
    second[0] = fold(second[0], "h", "g", second[1][0])
    second[1] = fold(second[1], "g", "h", second[0][0])
    (grad_query, grad_key, grad_value, grad_dense), riders = scatter_along_line(
        grad_heads,
        [lanes] * 4,
        [False, False, False, True],
        after=[standard_grad],
        late_after=second[1][:1],
    )
    early = jnp.sum(riders.astype(jnp.float32), axis=0).reshape(-1)[:early_count]
    output = finished(
        tokens,
        [part[0][0] for part in second],
        [shifted(part[1][0], axis, 1) for part, axis in zip(second, "gh")],
        out_bias.reshape(1, -1),
        after=[grad_dense],
    )
    terms = own_terms + terms
    vector_sums = jnp.concatenate([pick(late, lax.axis_index(WIDE)), early])
    vector_grads, start = [], 0
    for term in terms:
        vector_grads.append(vector_sums[start : start + term.shape[1]])
        start += term.shape[1]
    return (
        output,
        input_grad,
        vector_grads[0],
        vector_grads[1],
        grad_query,
        vector_grads[2],
        grad_key,
        vector_grads[3],
        grad_value,
        vector_grads[4],
        grad_dense,
        vector_grads[5],
        grad_up,
        vector_grads[6],
        grad_down,
        vector_grads[5],
    )


def solution(mesh):
    wide = mesh.shape["wide"]
    inner = Mesh(mesh.devices.reshape(wide // 4, 2, 2, 2, 2), ("s", "g", "h", "m", "c"))
    acts = P(WIDE, NARROW)
    vector = P(NARROW + WIDE)
    by_rows = P(WIDE, NARROW)
    by_cols = P(NARROW, WIDE)
    specs = (
        (acts, acts, vector, vector)
        + (by_rows, vector) * 3
        + (by_cols, vector, by_rows, vector, by_cols, vector)
    )
    return jax.shard_map(body, mesh=inner, in_specs=specs, out_specs=specs, check_vma=False)
```
